32 devices in a mesh: section: 4 (over z), fsdp: 8 (over y, x, core).
Axes of the slice: x: 2, y: 2, z: 4, core: 2. Of those that a mesh axis runs over, the one named last changes fastest.
Arguments:
- feats: bfloat16 [4, 8, 256, 1536], P(None, 'fsdp'), may hold values from -6 to 6
- w_in: bfloat16 [2, 4, 1536, 3072], P(None, 'section', 'fsdp'), may hold values from -0.15625 to 0.15625
- dw_kernel: bfloat16 [2, 4, 31, 1536], P(None, 'section', None, 'fsdp'), may hold values from -1 to 1
- mask_embed: bfloat16 [1536], replicated, may hold values from -6 to 6
- w_ctx: bfloat16 [1536, 768], replicated, may hold values from -0.15625 to 0.15625
- w_tgt: bfloat16 [1536, 768], replicated, may hold values from -0.15625 to 0.15625
- mask_starts: int32 [4, 8, 12], P(None, 'fsdp'), may hold values from 0 to 246
- distractors: int32 [4, 8, 256, 100], P(None, 'fsdp', 'section'), may hold values from 0 to 255
Outputs:
- frame_loss: float32 [4, 8, 256], P(None, 'fsdp', 'section')
The draws below stay inside these ranges and needn't reach their ends.
All inputs are finite; a program needn't handle non-finite values.
Results may differ from the reference program's by a relative error of at most 0.0054.
Values may be sent and summed in bfloat16 or wider, within the bound.
No kernel may reach another device: no remote copies, remote signals or barrier semaphores. Data moves between devices by JAX's collectives and lax.ppermute only.
A program may use at most 128 MiB of HBM per device.

```python
import jax
import jax.numpy as jnp
from jax import lax

D = 1536
E = 768
KERNEL = 31
NEG = 100
MASK_LEN = 10
SPANS = 12
MICRO = 4
REPEATS = 2
FRAMES = 256
SECTIONS = 4
UTTS = 8
N_SECTION = 4


def plant(array, stream_key, least, largest):
    index_at = [jax.random.randint(jax.random.fold_in(stream_key, axis), (), 0, length) for axis, length in enumerate(array.shape)]
    widest = array.shape.index(max(array.shape))
    next_to = index_at[:widest] + [(index_at[widest] + 1) % array.shape[widest]] + index_at[widest + 1:]
    return array.at[tuple(index_at)].set(least).at[tuple(next_to)].set(largest)


def block_levels(rng, shape, split, smallest, largest):
    level, own = 1.0, jax.random.fold_in(rng, 6)
    for dim, parts in split:
        steps = jnp.exp(jax.random.uniform(jax.random.fold_in(own, dim), (parts,), jnp.float32, smallest / len(split), largest / len(split)))
        level = level * jnp.repeat(steps, shape[dim] // parts).reshape([-1 if axis == dim else 1 for axis in range(len(shape))])
    return level


def centred(key, extent, deviation, bound, split=(), kind=jnp.bfloat16):
    drawn = jax.random.normal(key, extent, jnp.float32) * deviation
    if len(split) > 0:
        drawn = block_levels(key, extent, split, -0.22, 0.18) * drawn
    return jnp.clip(drawn, min=-bound, max=bound).astype(kind)


def setup_inputs(seed: int = 0) -> dict:
    key_of = jax.random.split(jax.random.key(seed), 9)
    feats = centred(key_of[0], (MICRO, UTTS, FRAMES, D), 1.0, 6.0, ((1, 8),))
    w_in = centred(key_of[1], (REPEATS, SECTIONS, D, 2 * D), D ** -0.5, 0.15625, ((1, 4), (2, 8)))
    dw_kernel = centred(key_of[2], (REPEATS, SECTIONS, KERNEL, D), KERNEL ** -0.5, 1.0, ((1, 4), (3, 8)))
    mask_embed = centred(key_of[3], (D,), 1.0, 6.0)
    w_ctx = centred(key_of[4], (D, E), D ** -0.5, 0.15625)
    w_tgt = centred(key_of[5], (D, E), D ** -0.5, 0.15625)
    mask_starts = plant(jax.random.randint(key_of[6], (MICRO, UTTS, SPANS), 0, FRAMES - MASK_LEN + 1), jax.random.fold_in(key_of[6], 1), 0, FRAMES - MASK_LEN).astype(jnp.int32)
    distractors = plant(jax.random.randint(key_of[7], (MICRO, UTTS, FRAMES, NEG), 0, FRAMES), jax.random.fold_in(key_of[7], 1), 0, FRAMES - 1).astype(jnp.int32)
    return dict(feats=feats, w_in=w_in, dw_kernel=dw_kernel, mask_embed=mask_embed, w_ctx=w_ctx, w_tgt=w_tgt, mask_starts=mask_starts, distractors=distractors)


def conv_layer(batch, weight, kernel):
    width = batch.shape[2]
    frames = batch.shape[1]
    values = batch.astype(jnp.float32)
    center = lax.optimization_barrier(jnp.mean(values, axis=2, keepdims=True))
    spread = lax.optimization_barrier(jnp.mean((values - center) ** 2, axis=2, keepdims=True))
    normed = ((values - center) * lax.rsqrt(spread + 1e-05)).astype(jnp.bfloat16)
    proj = jnp.dot(normed.reshape(-1, width), weight, preferred_element_type=jnp.float32)
    proj = proj.reshape(batch.shape[0], frames, 2 * width)
    glu = (proj[:, :, :width] * jax.nn.sigmoid(proj[:, :, width:])).astype(jnp.bfloat16)
    taps = kernel.shape[0]
    half = taps // 2
    padded = jnp.pad(glu, ((0, 0), (half, half), (0, 0)))
    mixed = jnp.zeros(values.shape, jnp.float32)
    for tap in range(taps):
        mixed = mixed + padded[:, tap:tap + frames, :].astype(jnp.float32) * kernel[tap].astype(jnp.float32)
    return (values + jax.nn.silu(mixed)).astype(jnp.bfloat16)

def unit_rows(values):
    return (values * lax.rsqrt(lax.optimization_barrier(jnp.sum(values * values, axis=-1, keepdims=True)) + 1e-06)).astype(jnp.bfloat16)

def reference(feats, w_in, dw_kernel, mask_embed, w_ctx, w_tgt, mask_starts, distractors):
    spots = jnp.arange(FRAMES, dtype=jnp.int32)
    starts = mask_starts[..., None]
    covered = jnp.any((spots >= starts) & (spots < starts + MASK_LEN), axis=2)
    masked = jnp.where(covered[..., None], mask_embed, feats)
    batch = masked.reshape(MICRO * UTTS, FRAMES, D)
    weights = w_in.reshape(REPEATS * N_SECTION, D, 2 * D)
    kernels = dw_kernel.reshape(REPEATS * N_SECTION, KERNEL, D)

    def layer_step(carry, pair):
        return (conv_layer(carry, pair[0], pair[1]), None)
    batch, unused = lax.scan(layer_step, batch, (weights, kernels))
    ctx = jnp.dot(batch.reshape(-1, D), w_ctx, preferred_element_type=jnp.float32)
    ctx = unit_rows(ctx).reshape(MICRO, UTTS, FRAMES, E)
    tgt = jnp.dot(feats.reshape(-1, D), w_tgt, preferred_element_type=jnp.float32)
    tgt = unit_rows(tgt).reshape(MICRO, UTTS, FRAMES, E)
    sims = jnp.einsum('mufe,muje->mufj', ctx.astype(jnp.float32), tgt.astype(jnp.float32))
    positive = jnp.diagonal(sims, axis1=2, axis2=3) * 10.0
    negative = jnp.take_along_axis(sims, distractors, axis=3) * 10.0
    total = jnp.exp(positive) + lax.optimization_barrier(jnp.sum(jnp.exp(negative), axis=3))
    return jnp.log(total) - positive
```

```python
import functools

import jax
import jax.numpy as jnp
from jax import lax
from jax.experimental import pallas as pl
from jax.experimental.pallas import tpu as pltpu
from jax.sharding import PartitionSpec as P

MASK_LEN = 10
LANES = 128
PAD = 16
VMEM_LIMIT = 48 * 1024 * 1024


def sigmoid(v):
    return 0.5 + 0.5 * jnp.tanh(0.5 * v)


def layer_body(chunks, taps, x_ref, wv_ref, wg_ref, k_ref, out_ref, normed, glu):
    step = pl.program_id(0)
    frames, width = x_ref.shape
    part = wv_ref.shape[1]
    subs = part // LANES
    rows = min(64, frames)

    def project(slot):
        values = jnp.dot(normed[...], wv_ref[...], preferred_element_type=jnp.float32)
        gates = jnp.dot(normed[...], wg_ref[...], preferred_element_type=jnp.float32)
        gated = (values * sigmoid(gates)).astype(jnp.bfloat16).astype(jnp.float32)
        for sub in range(subs):
            glu[slot, sub, PAD : PAD + frames, :] = gated[:, sub * LANES : (sub + 1) * LANES]

    def mix(slot):
        first = pl.multiple_of((step - 1) * part, part)
        for sub in range(subs):
            cols = slice(sub * LANES, (sub + 1) * LANES)
            for row in range(0, frames, rows):
                acc = jnp.zeros((rows, LANES), jnp.float32)
                for tap in range(taps):
                    start = PAD - taps // 2 + row + tap
                    acc = acc + glu[slot, sub, start : start + rows, :] * k_ref[tap : tap + 1, cols]
                base = x_ref[row : row + rows, pl.ds(first + sub * LANES, LANES)]
                out_ref[row : row + rows, cols] = (
                    base.astype(jnp.float32) + acc * sigmoid(acc)
                ).astype(jnp.bfloat16)

    @pl.when(step == 0)
    def _():
        zeros = jnp.zeros((2, subs, PAD, LANES), jnp.float32)
        glu[:, :, 0:PAD, :] = zeros
        glu[:, :, PAD + frames :, :] = zeros
        for row in range(0, frames, rows):
            values = x_ref[row : row + rows, :].astype(jnp.float32)
            center = jnp.mean(values, axis=1, keepdims=True)
            moved = values - center
            spread = jnp.mean(moved * moved, axis=1, keepdims=True)
            normed[row : row + rows, :] = (moved * lax.rsqrt(spread + 1e-05)).astype(jnp.bfloat16)
        project(0)

    @pl.when((step > 0) & (step < chunks) & (step % 2 == 1))
    def _():
        project(1)
        mix(0)

    @pl.when((step > 0) & (step < chunks) & (step % 2 == 0))
    def _():
        project(0)
        mix(1)

    @pl.when(step == chunks)
    def _():
        mix((chunks - 1) % 2)


def layer(x, weight, kernel):
    frames, width = x.shape
    part = 256
    chunks = width // part
    taps = 31
    return pl.pallas_call(
        functools.partial(layer_body, chunks, taps),
        grid=(chunks + 1,),
        in_specs=[
            pl.BlockSpec((frames, width), lambda j: (0, 0)),
            pl.BlockSpec((width, part), lambda j: (0, jnp.minimum(j, chunks - 1))),
            pl.BlockSpec((width, part), lambda j: (0, chunks + jnp.minimum(j, chunks - 1))),
            pl.BlockSpec((kernel.shape[0], part), lambda j: (0, jnp.maximum(j - 1, 0))),
        ],
        out_specs=pl.BlockSpec((frames, part), lambda j: (0, jnp.maximum(j - 1, 0))),
        out_shape=jax.ShapeDtypeStruct((frames, width), jnp.bfloat16),
        scratch_shapes=[
            pltpu.VMEM((frames, width), jnp.bfloat16),
            pltpu.VMEM((2, part // LANES, frames + 2 * PAD, LANES), jnp.float32),
        ],
        compiler_params=pltpu.CompilerParams(vmem_limit_bytes=VMEM_LIMIT),
        cost_estimate=pl.CostEstimate(
            flops=4 * frames * width * width, bytes_accessed=4 * width * width, transcendentals=0
        ),
        name="layer",
    )(x, weight, weight, kernel)


def unit_rows(values):
    return (values * lax.rsqrt(jnp.sum(values * values, axis=-1, keepdims=True) + 1e-06)).astype(
        jnp.bfloat16
    )


def loss_body(count, x_ref, w_ref, tgt_ref, pick_ref, out_ref):
    frames = x_ref.shape[0]
    ctx = unit_rows(jnp.dot(x_ref[...], w_ref[...], preferred_element_type=jnp.float32))
    sims = lax.dot_general(
        ctx, tgt_ref[...], (((1,), (1,)), ((), ())), preferred_element_type=jnp.float32
    )
    row = lax.broadcasted_iota(jnp.int32, sims.shape, 0)
    col = lax.broadcasted_iota(jnp.int32, sims.shape, 1)
    positive = jnp.sum(jnp.where(row == col, sims, 0.0), axis=1, keepdims=True) * 10.0
    picks = pick_ref[...]
    lane = picks % LANES
    block = picks // LANES
    negative = jnp.zeros(picks.shape, jnp.float32)
    for part in range(frames // LANES):
        found = jnp.take_along_axis(sims[:, part * LANES : (part + 1) * LANES], lane, axis=1)
        negative = jnp.where(block == part, found, negative)
    place = lax.broadcasted_iota(jnp.int32, picks.shape, 1)
    terms = jnp.where(place < count, jnp.exp(negative * 10.0), 0.0)
    total = jnp.exp(positive) + jnp.sum(terms, axis=1, keepdims=True)
    out_ref[...] = jnp.broadcast_to(jnp.log(total) - positive, out_ref.shape)


def loss_rows(x, w_ctx, tgt, picks, count):
    frames = x.shape[0]
    out = pl.pallas_call(
        functools.partial(loss_body, count),
        out_shape=jax.ShapeDtypeStruct((frames, LANES), jnp.float32),
        compiler_params=pltpu.CompilerParams(vmem_limit_bytes=VMEM_LIMIT),
        name="loss",
    )(x, w_ctx, tgt, picks)
    return out[:, 0]


def on_device(feats, w_in, dw_kernel, mask_embed, w_ctx, w_tgt, mask_starts, distractors):
    sections = lax.axis_size("section")
    section = lax.axis_index("section")
    micro = feats.shape[0]
    frames = feats.shape[2]
    repeats = w_in.shape[0]
    last = sections - 1
    feats_local = feats[:, 0]

    weights = []
    for turn in range(repeats):
        rows = w_in[turn, 0]
        if turn > 0:
            rows, weights[-1] = lax.optimization_barrier((rows, weights[-1]))
        weights.append(lax.all_gather(rows, "fsdp", axis=0, tiled=True))
    full_k = lax.all_gather(dw_kernel[:, 0], "fsdp", axis=2, tiled=True)
    taps = full_k.shape[1]
    full_k = jnp.pad(full_k, ((0, 0), (0, -taps % 8), (0, 0))).astype(jnp.float32)

    spots = jnp.arange(frames, dtype=jnp.int32)
    starts = mask_starts[:, 0][:, :, None]
    covered = jnp.any(
        (spots[None, None, :] >= starts) & (spots[None, None, :] < starts + MASK_LEN), axis=1
    )
    masked_in = jnp.where(covered[:, :, None], mask_embed[None, None, :], feats_local)
    tgt = unit_rows(
        jnp.einsum("mjd,de->mje", feats_local, w_tgt, preferred_element_type=jnp.float32)
    )

    picks = distractors[:, 0]
    count = picks.shape[2]
    pieces = [
        picks if s == last else lax.ppermute(picks, "section", [(s, last)]) for s in range(sections)
    ]
    picks = jnp.concatenate(pieces, axis=1)
    picks = jnp.pad(picks, ((0, 0), (0, 0), (0, -count % LANES)))

    def work(step, s):
        offset = step - s
        if offset < 0:
            return None
        turn, slot = offset // sections, offset % sections
        return (turn, slot) if slot < micro and turn < repeats else None

    state = jnp.zeros((frames, feats.shape[3]), jnp.bfloat16)
    losses = []
    for step in range(repeats * sections + micro - 1):
        plan = [work(step, s) for s in range(sections)]
        turns = sorted({item[0] for item in plan if item is not None})
        if plan[0] is not None and plan[0][0] == 0:
            state = jnp.where(section == 0, masked_in[plan[0][1]], state)
        choice = jnp.array(
            [0 if item is None else 1 + turns.index(item[0]) for item in plan], jnp.int32
        )[section]
        branches = [lambda x: x]
        for turn in turns:
            branches.append(lambda x, turn=turn: layer(x, weights[turn], full_k[turn]))
        result = lax.switch(choice, branches, state)
        ends = plan[last]
        if ends is not None and ends[0] == repeats - 1:
            slot = ends[1]
            losses.append(
                lax.cond(
                    section == last,
                    lambda x, slot=slot: loss_rows(x, w_ctx, tgt[slot], picks[slot], count),
                    lambda x: jnp.zeros((frames,), jnp.float32),
                    result,
                )
            )
        route = []
        for s, item in enumerate(plan):
            if item is not None and not (s == last and item[0] == repeats - 1):
                route.append((s, (s + 1) % sections))
        if route:
            state = lax.ppermute(result, "section", route)

    loss = jnp.stack(losses)
    share = frames // sections
    mine = jnp.zeros((micro, share), jnp.float32)
    for s in range(sections):
        cut = loss[:, s * share : (s + 1) * share]
        if s == last:
            mine = mine + jnp.where(section == last, cut, 0.0)
        else:
            mine = mine + lax.ppermute(cut, "section", [(last, s)])
    return mine[:, None, :]


def solution(mesh):
    placed = (
        P(None, "fsdp", None, None),
        P(None, "section", "fsdp", None),
        P(None, "section", None, "fsdp"),
        P(),
        P(),
        P(),
        P(None, "fsdp", None),
        P(None, "fsdp", "section", None),
    )
    return jax.shard_map(
        on_device, mesh=mesh, in_specs=placed, out_specs=P(None, "fsdp", "section"), check_vma=False
    )
```

```python
import functools

import jax
import jax.numpy as jnp
from jax import lax
from jax.experimental import pallas as pl
from jax.experimental.pallas import tpu as pltpu
from jax.sharding import PartitionSpec as P

MASK_LEN = 10
LANES = 128
PAD = 16
VMEM_LIMIT = 48 * 1024 * 1024


def sigmoid(v):
    return 0.5 + 0.5 * jnp.tanh(0.5 * v)


def layer_body(
    entry, taps, turns, fresh_slot, has_recv, flags, *refs
):
    refs = list(refs)
    fresh = refs.pop(0) if fresh_slot is not None else None
    recv = refs.pop(0) if has_recv else None
    sources = [refs.pop(0) for _ in turns]
    k_ref, out_ref, x_ref, normed, wbuf, glu, x_sem, w_sem = refs
    chunks, _, width, part = wbuf.shape
    frames = x_ref.shape[0]
    subs = part // LANES
    rows = min(64, frames)
    valid = flags[entry, 0]
    turn = flags[entry, 1]
    take_fresh = flags[entry, 2]

    def weight_copy(source, j, side):
        cols = pl.ds(side * width + j * part, part)
        return pltpu.make_async_copy(source.at[:, cols], wbuf.at[j, side], w_sem.at[j, side])

    def project(j, slot):
        values = jnp.dot(normed[...], wbuf[j, 0], preferred_element_type=jnp.float32)
        gates = jnp.dot(normed[...], wbuf[j, 1], preferred_element_type=jnp.float32)
        gated = (values * sigmoid(gates)).astype(jnp.bfloat16).astype(jnp.float32)
        for sub in range(subs):
            glu[slot, sub, PAD : PAD + frames, :] = gated[:, sub * LANES : (sub + 1) * LANES]

    def mix(j, slot):
        for sub in range(subs):
            first = pl.multiple_of(j * part + sub * LANES, LANES)
            cols = pl.ds(first, LANES)
            for row in range(0, frames, rows):
                acc = jnp.zeros((rows, LANES), jnp.float32)
                for tap in range(taps):
                    start = PAD - taps // 2 + row + tap
                    acc = acc + glu[slot, sub, start : start + rows, :] * k_ref[turn, tap : tap + 1, cols]
                base = x_ref[row : row + rows, cols]
                out_ref[row : row + rows, cols] = (
                    base.astype(jnp.float32) + acc * sigmoid(acc)
                ).astype(jnp.bfloat16)

    def wait_weights(j):
        for side in range(2):
            pltpu.make_async_copy(
                sources[0].at[:, pl.ds(0, part)], wbuf.at[j, side], w_sem.at[j, side]
            ).wait()

    @pl.when(valid == 1)
    def _():
        if fresh is None:
            copy = pltpu.make_async_copy(recv, x_ref, x_sem)
            copy.start()
        elif recv is None:
            copy = pltpu.make_async_copy(fresh.at[fresh_slot], x_ref, x_sem)
            copy.start()
        else:
            copy = pltpu.make_async_copy(recv, x_ref, x_sem)

            @pl.when(take_fresh == 1)
            def _():
                pltpu.make_async_copy(fresh.at[fresh_slot], x_ref, x_sem).start()

            @pl.when(take_fresh == 0)
            def _():
                copy.start()

        for source, which in zip(sources, turns):

            def start_all(source=source):
                for j in range(chunks):
                    for side in range(2):
                        weight_copy(source, j, side).start()

            if len(turns) == 1:
                start_all()
            else:
                pl.when(turn == which)(start_all)

        zeros = jnp.zeros((2, subs, PAD, LANES), jnp.float32)
        glu[:, :, 0:PAD, :] = zeros
        glu[:, :, PAD + frames :, :] = zeros
        copy.wait()
        for row in range(0, frames, rows):
            values = x_ref[row : row + rows, :].astype(jnp.float32)
            center = jnp.mean(values, axis=1, keepdims=True)
            moved = values - center
            spread = jnp.mean(moved * moved, axis=1, keepdims=True)
            normed[row : row + rows, :] = (moved * lax.rsqrt(spread + 1e-05)).astype(jnp.bfloat16)
        wait_weights(0)
        project(0, 0)

        @pl.loop(0, chunks - 1)
        def _(j):
            wait_weights(j + 1)
            project(j + 1, (j + 1) % 2)
            mix(j, j % 2)

        mix(chunks - 1, (chunks - 1) % 2)


def layer(entry, flags, fresh, fresh_slot, recv, weights, turns, kernels, taps):
    frames, width = (recv.shape if recv is not None else fresh.shape[1:])
    part = 256
    chunks = width // part
    anywhere = pl.BlockSpec(memory_space=pl.ANY)
    operands = [flags]
    specs = [pl.BlockSpec(memory_space=pltpu.SMEM)]
    if fresh_slot is not None:
        operands.append(fresh)
        specs.append(anywhere)
    if recv is not None:
        operands.append(recv)
        specs.append(anywhere)
    for turn in turns:
        operands.append(weights[turn])
        specs.append(anywhere)
    operands.append(kernels)
    specs.append(pl.BlockSpec(memory_space=pltpu.VMEM))
    return pl.pallas_call(
        functools.partial(layer_body, entry, taps, turns, fresh_slot, recv is not None),
        in_specs=specs,
        out_specs=pl.BlockSpec(memory_space=pltpu.VMEM),
        out_shape=jax.ShapeDtypeStruct((frames, width), jnp.bfloat16),
        scratch_shapes=[
            pltpu.VMEM((frames, width), jnp.bfloat16),
            pltpu.VMEM((frames, width), jnp.bfloat16),
            pltpu.VMEM((chunks, 2, width, part), jnp.bfloat16),
            pltpu.VMEM((2, part // LANES, frames + 2 * PAD, LANES), jnp.float32),
            pltpu.SemaphoreType.DMA,
            pltpu.SemaphoreType.DMA((chunks, 2)),
        ],
        compiler_params=pltpu.CompilerParams(vmem_limit_bytes=VMEM_LIMIT),
        cost_estimate=pl.CostEstimate(
            flops=4 * frames * width * width, bytes_accessed=4 * width * width, transcendentals=0
        ),
        name="layer",
    )(*operands)


def unit_rows(values):
    return (values * lax.rsqrt(jnp.sum(values * values, axis=-1, keepdims=True) + 1e-06)).astype(
        jnp.bfloat16
    )


def target_body(wanted, flags, feats, w_tgt, *refs):
    out, feats_ref, w_ref, out_ref, sems = refs[-5:]

    @pl.when(flags[0, 3] == wanted)
    def _():
        copies = [
            pltpu.make_async_copy(w_tgt, w_ref, sems.at[0]),
            pltpu.make_async_copy(feats, feats_ref, sems.at[1]),
        ]
        for copy in copies:
            copy.start()
        for copy in copies:
            copy.wait()

        @pl.loop(0, feats_ref.shape[0])
        def _(slot):
            out_ref[slot] = unit_rows(
                jnp.dot(feats_ref[slot], w_ref[...], preferred_element_type=jnp.float32)
            )

        back = pltpu.make_async_copy(out_ref, out, sems.at[2])
        back.start()
        back.wait()


def targets(flags, feats, w_tgt, wanted, earlier=None):
    operands = [flags, feats, w_tgt] + ([] if earlier is None else [earlier])
    anywhere = pl.BlockSpec(memory_space=pl.ANY)
    shape = feats.shape[:2] + w_tgt.shape[1:]
    return pl.pallas_call(
        functools.partial(target_body, wanted),
        in_specs=[pl.BlockSpec(memory_space=pltpu.SMEM)] + [anywhere] * (len(operands) - 1),
        out_specs=anywhere,
        out_shape=jax.ShapeDtypeStruct(shape, jnp.bfloat16),
        scratch_shapes=[
            pltpu.VMEM(feats.shape, jnp.bfloat16),
            pltpu.VMEM(w_tgt.shape, jnp.bfloat16),
            pltpu.VMEM(shape, jnp.bfloat16),
            pltpu.SemaphoreType.DMA((3,)),
        ],
        input_output_aliases={} if earlier is None else {3: 0},
        compiler_params=pltpu.CompilerParams(vmem_limit_bytes=VMEM_LIMIT),
        cost_estimate=pl.CostEstimate(
            flops=2 * feats.size * w_tgt.shape[1],
            bytes_accessed=2 * (feats.size + w_tgt.size),
            transcendentals=0,
        ),
        name="targets",
    )(*operands)


def loss_body(slot, count, flags, x_ref, w_ref, tgt_ref, pick_ref, out_ref):
    frames = x_ref.shape[0]

    @pl.when(flags[0, 4] == 1)
    def _():
        ctx = unit_rows(jnp.dot(x_ref[...], w_ref[...], preferred_element_type=jnp.float32))
        sims = lax.dot_general(
            ctx, tgt_ref[slot], (((1,), (1,)), ((), ())), preferred_element_type=jnp.float32
        )
        row = lax.broadcasted_iota(jnp.int32, sims.shape, 0)
        col = lax.broadcasted_iota(jnp.int32, sims.shape, 1)
        positive = jnp.sum(jnp.where(row == col, sims, 0.0), axis=1, keepdims=True) * 10.0
        picks = pick_ref[slot]
        lane = picks % LANES
        block = picks // LANES
        negative = jnp.zeros(picks.shape, jnp.float32)
        for part in range(frames // LANES):
            found = jnp.take_along_axis(sims[:, part * LANES : (part + 1) * LANES], lane, axis=1)
            negative = jnp.where(block == part, found, negative)
        place = lax.broadcasted_iota(jnp.int32, picks.shape, 1)
        terms = jnp.where(place < count, jnp.exp(negative * 10.0), 0.0)
        total = jnp.exp(positive) + jnp.sum(terms, axis=1, keepdims=True)
        wide = jnp.broadcast_to(jnp.log(total) - positive, (frames, LANES))
        out_ref[...] = wide.T[0:1, :]


def loss_rows(slot, flags, x, w_ctx, tgt, picks, count):
    frames = x.shape[0]
    whole = pl.BlockSpec(memory_space=pltpu.VMEM)
    return pl.pallas_call(
        functools.partial(loss_body, slot, count),
        in_specs=[pl.BlockSpec(memory_space=pltpu.SMEM)] + [whole] * 4,
        out_specs=whole,
        out_shape=jax.ShapeDtypeStruct((1, frames), jnp.float32),
        compiler_params=pltpu.CompilerParams(vmem_limit_bytes=VMEM_LIMIT),
        name="loss",
    )(flags, x, w_ctx, tgt, picks)


def swap(block, axis, mask):
    return lax.ppermute(block, axis, [(i, i ^ mask) for i in range(lax.axis_size(axis))])


def place_body(count, starts, *refs):
    pieces, out, sems = refs[:count], refs[-2], refs[-1]
    copies = []
    for i, piece in enumerate(pieces):
        rows = pl.ds(pl.multiple_of(starts[i], 16), piece.shape[0])
        copies.append(pltpu.make_async_copy(piece, out.at[rows], sems.at[i]))
    for copy in copies:
        copy.start()
    for copy in copies:
        copy.wait()


def placed(pieces, starts, total, earlier=None):
    anywhere = pl.BlockSpec(memory_space=pl.ANY)
    count = len(pieces)
    operands = [jnp.stack(starts).astype(jnp.int32)] + pieces
    aliases = {}
    if earlier is not None:
        aliases = {len(operands): 0}
        operands.append(earlier)
    return pl.pallas_call(
        functools.partial(place_body, count),
        in_specs=[pl.BlockSpec(memory_space=pltpu.SMEM)] + [anywhere] * (len(operands) - 1),
        out_specs=anywhere,
        out_shape=jax.ShapeDtypeStruct((total,) + pieces[0].shape[1:], pieces[0].dtype),
        scratch_shapes=[pltpu.SemaphoreType.DMA((count,))],
        input_output_aliases=aliases,
        name="placed",
    )(*operands)


def doubled_rows(block, axis):
    me = lax.axis_index(axis)
    size = lax.axis_size(axis)
    if size & (size - 1):
        return lax.all_gather(block, axis, axis=0, tiled=True)
    rows = block.shape[0]
    mask = 1
    held = block
    while mask < size:
        held = jnp.concatenate([held, swap(held, axis, mask)], axis=0)
        mask *= 2
    whole = jnp.zeros_like(held)
    for mask in range(size):
        piece = held[mask * rows : (mask + 1) * rows]
        whole = lax.dynamic_update_slice_in_dim(whole, piece, (me ^ mask) * rows, 0)
    return whole


def crossed(block, axis, beside):
    me = lax.axis_index(axis)
    size = block.shape[0]
    half = size // 2
    pieces = {0: block, 2: swap(block, axis, 2), 4: swap(block, axis, 4)}
    upper = swap(pieces[4][:half], axis, 2)
    lower = swap(pieces[2][half:], axis, 4)
    for held in (0, 2, 4):
        pieces[held ^ 1] = swap(pieces[held], axis, 1)
    whole = placed(list(pieces.values()), [(me ^ mask) * size for mask in pieces], size * 8)
    whole, *beside = lax.optimization_barrier((whole, *beside))
    final = [upper, lower, swap(upper, axis, 1), swap(lower, axis, 1)]
    starts = [(me ^ 6) * size, (me ^ 6) * size + half, (me ^ 7) * size, (me ^ 7) * size + half]
    return placed(final, starts, size * 8, whole), beside


def gathered_rows(block, axis, beside):
    if lax.axis_size(axis) == 8:
        return crossed(block, axis, beside)
    return lax.all_gather(block, axis, axis=0, tiled=True), beside


def on_device(feats, w_in, dw_kernel, mask_embed, w_ctx, w_tgt, mask_starts, distractors):
    sections = lax.axis_size("section")
    section = lax.axis_index("section")
    micro = feats.shape[0]
    frames = feats.shape[2]
    repeats = w_in.shape[0]
    last = sections - 1
    feats_local = feats[:, 0]

    taps = dw_kernel.shape[2]
    own = jnp.swapaxes(jnp.pad(dw_kernel[:, 0], ((0, 0), (0, -taps % 8), (0, 0))), 1, 2)
    own = jnp.swapaxes(own, 0, 1).reshape(own.shape[1], -1)
    full_k = doubled_rows(own, "fsdp").reshape(feats.shape[3], repeats, -1)
    full_k = jnp.transpose(full_k, (1, 2, 0)).astype(jnp.float32)

    spots = jnp.arange(frames, dtype=jnp.int32)
    starts = mask_starts[:, 0][:, :, None]
    covered = jnp.any(
        (spots[None, None, :] >= starts) & (spots[None, None, :] < starts + MASK_LEN), axis=1
    )
    masked_in = jnp.where(covered[:, :, None], mask_embed[None, None, :], feats_local)
    def work(step, s):
        offset = step - s
        if offset < 0:
            return None
        turn, slot = offset // sections, offset % sections
        return (turn, slot) if slot < micro and turn < repeats else None

    plans = []
    for step in range(repeats * sections + micro - 1):
        plans.append([work(step, s) for s in range(sections)])
    table = [
        [
            [
                int(plan[s] is not None),
                0 if plan[s] is None else plan[s][0],
                int(s == 0 and plan[s] is not None and plan[s][0] == 0),
                0,
                int(s == last),
            ]
            for plan in plans
        ]
        for s in range(sections)
    ]
    flags = lax.dynamic_index_in_dim(jnp.array(table, jnp.int32), section, 0, keepdims=False)
    odd = lax.axis_index("fsdp") % 2
    flags = flags + jnp.array([0, 0, 0, 1, 0], jnp.int32) * odd

    first, beside = gathered_rows(w_in[0, 0], "fsdp", (full_k, masked_in, flags))
    full_k, masked_in, flags = beside
    weights = [first]
    for turn in range(1, repeats):
        rows, weights[-1] = lax.optimization_barrier((w_in[turn, 0], weights[-1]))
        weights.append(lax.all_gather(rows, "fsdp", axis=0, tiled=True))

    picks = distractors[:, 0]
    count = picks.shape[2]
    pieces = [
        picks if s == last else lax.ppermute(picks, "section", [(s, last)]) for s in range(sections)
    ]
    picks = jnp.concatenate(pieces, axis=1)
    picks = jnp.pad(picks, ((0, 0), (0, 0), (0, -count % LANES)))

    flags, weights[0] = lax.optimization_barrier((flags, weights[0]))
    tgt = targets(flags, feats_local, w_tgt, 1)
    flags, tgt = lax.optimization_barrier((flags, tgt))
    state = None
    losses = []
    for step, plan in enumerate(plans):
        turns = sorted({item[0] for item in plan if item is not None})
        slot = plan[0][1] if plan[0] is not None and plan[0][0] == 0 else None
        result = layer(step, flags, masked_in, slot, state, weights, turns, full_k, taps)
        if step == micro:
            result, tgt = lax.optimization_barrier((result, tgt))
            tgt = targets(flags, feats_local, w_tgt, 0, tgt)
        ends = plan[last]
        if ends is not None and ends[0] == repeats - 1:
            losses.append(loss_rows(ends[1], flags, result, w_ctx, tgt, picks, count))
        route = []
        for s, item in enumerate(plan):
            if item is not None and not (s == last and item[0] == repeats - 1):
                route.append((s, (s + 1) % sections))
        if route:
            state = lax.ppermute(result, "section", route)

    loss = jnp.concatenate(losses, axis=0)
    share = frames // sections
    mine = jnp.zeros((micro, share), jnp.float32)
    for s in range(sections):
        cut = loss[:, s * share : (s + 1) * share]
        if s == last:
            mine = mine + jnp.where(section == last, cut, 0.0)
        else:
            mine = mine + lax.ppermute(cut, "section", [(last, s)])
    return mine[:, None, :]


def solution(mesh):
    placed = (
        P(None, "fsdp", None, None),
        P(None, "section", "fsdp", None),
        P(None, "section", None, "fsdp"),
        P(),
        P(),
        P(),
        P(None, "fsdp", None),
        P(None, "fsdp", "section", None),
    )
    return jax.shard_map(
        on_device, mesh=mesh, in_specs=placed, out_specs=P(None, "fsdp", "section"), check_vma=False
    )
```

```python
import functools

import jax
import jax.numpy as jnp
from jax import lax
from jax.experimental import pallas as pl
from jax.experimental.pallas import tpu as pltpu
from jax.sharding import PartitionSpec as P

MASK_LEN = 10
LANES = 128
PAD = 16
VMEM_LIMIT = 48 * 1024 * 1024


def sigmoid(v):
    return 0.5 + 0.5 * jnp.tanh(0.5 * v)


def layer_body(entry, taps, kinds, fresh_slot, has_recv, emit, merge, flags, *refs):
    refs = list(refs)
    fresh = refs.pop(0) if fresh_slot is not None else None
    recv = refs.pop(0) if has_recv else None
    sources = [[refs.pop(0) for _ in range(count)] for _, _, count in kinds]
    starts = refs.pop(0) if emit else None
    k_ref = refs.pop(0)
    if merge:
        del refs[:2]
    out = refs.pop(0)
    whole = refs.pop(0) if emit else None
    normed, wbuf, glu, w_sem = (refs.pop(0) for _ in range(4))
    x_ref, x_sem = (refs.pop(0), refs.pop(0)) if fresh is not None else (recv, None)
    out_ref, out_sem = (refs.pop(0), refs.pop(0)) if merge else (out, None)
    keep_sem = refs.pop(0) if emit else None
    chunks, _, width, part = wbuf.shape
    frames = x_ref.shape[0]
    subs = part // LANES
    rows = min(128, frames)
    half = taps // 2
    valid = flags[entry, 0]
    turn = flags[entry, 1]
    take_fresh = flags[entry, 2]

    def weight_copies(kind, source, j, side):
        target, sem = wbuf.at[j, side], w_sem.at[j, side]
        cols = pl.ds(side * width + j * part, part)
        if kind == "rows":
            return [pltpu.make_async_copy(source[0].at[:, cols], target, sem)]
        if kind == "chunked":
            return [pltpu.make_async_copy(source[0].at[j, side], target, sem)]
        copies = []
        for i, piece in enumerate(source):
            size = piece.shape[0]
            place = pl.ds(pl.multiple_of(starts[i], size), size)
            copies.append(pltpu.make_async_copy(piece.at[:, cols], target.at[place], sem))
        return copies

    def start_weights(kind, source):
        for j in range(chunks):
            for side in range(2):
                for copy in weight_copies(kind, source, j, side):
                    copy.start()

    def wait_weights(j):
        for side in range(2):
            target = wbuf.at[j, side]
            pltpu.make_async_copy(target, target, w_sem.at[j, side]).wait()

    def project(j, slot):
        values = jnp.dot(normed[...], wbuf[j, 0], preferred_element_type=jnp.float32)
        gates = jnp.dot(normed[...], wbuf[j, 1], preferred_element_type=jnp.float32)
        gated = (values * sigmoid(gates)).astype(jnp.bfloat16).astype(jnp.float32)
        for sub in range(subs):
            glu[slot, sub, PAD : PAD + frames, :] = gated[:, sub * LANES : (sub + 1) * LANES]

    def mix(j, slot):
        for sub in range(subs):
            first = pl.multiple_of(j * part + sub * LANES, LANES)
            cols = pl.ds(first, LANES)
            scale = k_ref[turn, :, cols]
            for row in range(0, frames, rows):
                acc = jnp.zeros((rows, LANES), jnp.float32)
                for low in range(8):
                    highs = range(low, taps, 8)
                    begin = row + PAD - half + low
                    span = glu[slot, sub, begin : begin + rows + highs[-1] - low, :]
                    for tap in highs:
                        acc = acc + span[tap - low : tap - low + rows] * scale[tap : tap + 1]
                base = x_ref[row : row + rows, cols].astype(jnp.float32)
                out_ref[row : row + rows, cols] = (base + acc * sigmoid(acc)).astype(jnp.bfloat16)

    def compute():
        zeros = jnp.zeros((2, subs, PAD, LANES), jnp.float32)
        glu[:, :, 0:PAD, :] = zeros
        glu[:, :, PAD + frames :, :] = zeros
        if x_sem is not None:
            pltpu.make_async_copy(x_ref, x_ref, x_sem).wait()
        for row in range(0, frames, 64):
            values = x_ref[row : row + 64, :].astype(jnp.float32)
            center = jnp.mean(values, axis=1, keepdims=True)
            moved = values - center
            spread = jnp.mean(moved * moved, axis=1, keepdims=True)
            normed[row : row + 64, :] = (moved * lax.rsqrt(spread + 1e-05)).astype(jnp.bfloat16)
        wait_weights(0)
        project(0, 0)

        @pl.loop(0, chunks - 1)
        def _(j):
            wait_weights(j + 1)
            project(j + 1, (j + 1) % 2)
            mix(j, j % 2)

        mix(chunks - 1, (chunks - 1) % 2)

    def start_input():
        if fresh is None:
            return
        if recv is None:
            pltpu.make_async_copy(fresh.at[fresh_slot], x_ref, x_sem).start()
            return

        @pl.when(take_fresh == 1)
        def _():
            pltpu.make_async_copy(fresh.at[fresh_slot], x_ref, x_sem).start()

        @pl.when(take_fresh == 0)
        def _():
            pltpu.make_async_copy(recv, x_ref, x_sem).start()

    def keep(j, side):
        return pltpu.make_async_copy(wbuf.at[j, side], whole.at[j, side], keep_sem.at[j, side])

    if emit:
        start_weights(kinds[0][0], sources[0])

        @pl.when(valid == 1)
        def _():
            start_input()
            compute()

        @pl.when(valid == 0)
        def _():
            for j in range(chunks):
                wait_weights(j)

        for j in range(chunks):
            for side in range(2):
                keep(j, side).start()
        for j in range(chunks):
            for side in range(2):
                keep(j, side).wait()
    else:

        @pl.when(valid == 1)
        def _():
            start_input()
            for (which, kind, _), source in zip(kinds, sources):
                if len(kinds) == 1:
                    start_weights(kind, source)
                else:
                    pl.when(turn == which)(functools.partial(start_weights, kind, source))
            compute()
            if merge:
                copy = pltpu.make_async_copy(out_ref, out, out_sem)
                copy.start()
                copy.wait()


def layer(entry, flags, fresh, fresh_slot, recv, weights, kernels, taps, starts=None, merge=None):
    frames, width = recv.shape if recv is not None else fresh.shape[1:]
    part = 256
    chunks = width // part
    emit = starts is not None
    anywhere = pl.BlockSpec(memory_space=pl.ANY)
    local = pl.BlockSpec(memory_space=pltpu.VMEM)
    smem = pl.BlockSpec(memory_space=pltpu.SMEM)
    operands, specs = [flags], [smem]
    if fresh_slot is not None:
        operands.append(fresh)
        specs.append(anywhere)
    if recv is not None:
        operands.append(recv)
        specs.append(anywhere if fresh_slot is not None else local)
    for _, _, arrays in weights:
        operands += arrays
        specs += [anywhere] * len(arrays)
    if emit:
        operands.append(starts)
        specs.append(smem)
    operands.append(kernels)
    specs.append(local)
    aliases = {}
    if merge is not None:
        aliases = {len(operands): 0}
        operands += merge
        specs += [anywhere] * 2
    out_shape = [jax.ShapeDtypeStruct((frames, width), jnp.bfloat16)]
    out_specs = [local if merge is None else anywhere]
    scratch = [
        pltpu.VMEM((frames, width), jnp.bfloat16),
        pltpu.VMEM((chunks, 2, width, part), jnp.bfloat16),
        pltpu.VMEM((2, part // LANES, frames + 2 * PAD, LANES), jnp.float32),
        pltpu.SemaphoreType.DMA((chunks, 2)),
    ]
    if fresh_slot is not None:
        scratch += [pltpu.VMEM((frames, width), jnp.bfloat16), pltpu.SemaphoreType.DMA]
    if merge is not None:
        scratch += [pltpu.VMEM((frames, width), jnp.bfloat16), pltpu.SemaphoreType.DMA]
    if emit:
        out_shape.append(jax.ShapeDtypeStruct((chunks, 2, width, part), jnp.bfloat16))
        out_specs.append(anywhere)
        scratch.append(pltpu.SemaphoreType.DMA((chunks, 2)))
    kinds = [(turn, kind, len(arrays)) for turn, kind, arrays in weights]
    return pl.pallas_call(
        functools.partial(
            layer_body,
            entry,
            taps,
            kinds,
            fresh_slot,
            recv is not None,
            emit,
            merge is not None,
        ),
        in_specs=specs,
        out_specs=out_specs,
        out_shape=out_shape,
        scratch_shapes=scratch,
        input_output_aliases=aliases,
        compiler_params=pltpu.CompilerParams(vmem_limit_bytes=VMEM_LIMIT),
        cost_estimate=pl.CostEstimate(
            flops=4 * frames * width * width, bytes_accessed=4 * width * width, transcendentals=0
        ),
        name="layer",
    )(*operands)


def unit_rows(values):
    return (values * lax.rsqrt(jnp.sum(values * values, axis=-1, keepdims=True) + 1e-06)).astype(
        jnp.bfloat16
    )


def target_body(feats_ref, w_ref, out_ref):
    out_ref[0] = unit_rows(jnp.dot(feats_ref[0], w_ref[...], preferred_element_type=jnp.float32))


def targets(feats, w_tgt):
    micro, frames, width = feats.shape
    wide = w_tgt.shape[1]
    return pl.pallas_call(
        target_body,
        grid=(micro,),
        in_specs=[
            pl.BlockSpec((1, frames, width), lambda i: (i, 0, 0)),
            pl.BlockSpec((width, wide), lambda i: (0, 0)),
        ],
        out_specs=pl.BlockSpec((1, frames, wide), lambda i: (i, 0, 0)),
        out_shape=jax.ShapeDtypeStruct((micro, frames, wide), jnp.bfloat16),
        compiler_params=pltpu.CompilerParams(vmem_limit_bytes=VMEM_LIMIT),
        cost_estimate=pl.CostEstimate(
            flops=2 * feats.size * wide,
            bytes_accessed=2 * (feats.size + w_tgt.size),
            transcendentals=0,
        ),
        name="targets",
    )(feats, w_tgt)


def loss_body(slot, count, flags, x_ref, w_ref, tgt_ref, pick_ref, out_ref):
    frames = x_ref.shape[0]

    @pl.when(flags[0, 3] == 1)
    def _():
        ctx = unit_rows(jnp.dot(x_ref[...], w_ref[...], preferred_element_type=jnp.float32))
        sims = lax.dot_general(
            ctx, tgt_ref[slot], (((1,), (1,)), ((), ())), preferred_element_type=jnp.float32
        )
        row = lax.broadcasted_iota(jnp.int32, sims.shape, 0)
        col = lax.broadcasted_iota(jnp.int32, sims.shape, 1)
        positive = jnp.sum(jnp.where(row == col, sims, 0.0), axis=1, keepdims=True) * 10.0
        picks = pick_ref[slot]
        lane = picks % LANES
        block = picks // LANES
        negative = jnp.zeros(picks.shape, jnp.float32)
        for part in range(frames // LANES):
            found = jnp.take_along_axis(sims[:, part * LANES : (part + 1) * LANES], lane, axis=1)
            negative = jnp.where(block == part, found, negative)
        place = lax.broadcasted_iota(jnp.int32, picks.shape, 1)
        terms = jnp.where(place < count, jnp.exp(negative * 10.0), 0.0)
        total = jnp.exp(positive) + jnp.sum(terms, axis=1, keepdims=True)
        wide = jnp.broadcast_to(jnp.log(total) - positive, (frames, LANES))
        out_ref[...] = wide.T[0:1, :]


def loss_rows(slot, flags, x, w_ctx, tgt, picks, count):
    frames = x.shape[0]
    whole = pl.BlockSpec(memory_space=pltpu.VMEM)
    return pl.pallas_call(
        functools.partial(loss_body, slot, count),
        in_specs=[pl.BlockSpec(memory_space=pltpu.SMEM)] + [whole] * 4,
        out_specs=whole,
        out_shape=jax.ShapeDtypeStruct((1, frames), jnp.float32),
        compiler_params=pltpu.CompilerParams(vmem_limit_bytes=VMEM_LIMIT),
        name="loss",
    )(flags, x, w_ctx, tgt, picks)


def swap(block, axis, mask):
    return lax.ppermute(block, axis, [(i, i ^ mask) for i in range(lax.axis_size(axis))])


def doubled_rows(block, axis):
    me = lax.axis_index(axis)
    size = lax.axis_size(axis)
    if size & (size - 1):
        return lax.all_gather(block, axis, axis=0, tiled=True)
    rows = block.shape[0]
    mask = 1
    held = block
    while mask < size:
        held = jnp.concatenate([held, swap(held, axis, mask)], axis=0)
        mask *= 2
    whole = jnp.zeros_like(held)
    for mask in range(size):
        piece = held[mask * rows : (mask + 1) * rows]
        whole = lax.dynamic_update_slice_in_dim(whole, piece, (me ^ mask) * rows, 0)
    return whole


def crossed(block, axis):
    me = lax.axis_index(axis)
    half = block.shape[0] // 2
    pieces = {(0, 0): block[:half], (0, 1): block[half:]}
    pieces[2, 1] = swap(pieces[0, 1], axis, 2)
    pieces[4, 0] = swap(pieces[0, 0], axis, 4)
    pieces[2, 0] = swap(pieces[0, 0], axis, 2)
    pieces[4, 1] = swap(pieces[0, 1], axis, 4)
    pieces[6, 0] = swap(pieces[4, 0], axis, 2)
    pieces[6, 1] = swap(pieces[2, 1], axis, 4)
    for held in list(pieces):
        pieces[held[0] ^ 1, held[1]] = swap(pieces[held], axis, 1)
    starts = [(me ^ mask) * block.shape[0] + side * half for mask, side in pieces]
    return list(pieces.values()), jnp.stack(starts).astype(jnp.int32)


def on_device(feats, w_in, dw_kernel, mask_embed, w_ctx, w_tgt, mask_starts, distractors):
    sections = lax.axis_size("section")
    section = lax.axis_index("section")
    micro = feats.shape[0]
    frames = feats.shape[2]
    repeats = w_in.shape[0]
    last = sections - 1
    feats_local = feats[:, 0]

    taps = dw_kernel.shape[2]
    own = jnp.swapaxes(jnp.pad(dw_kernel[:, 0], ((0, 0), (0, -taps % 8), (0, 0))), 1, 2)
    own = jnp.swapaxes(own, 0, 1).reshape(own.shape[1], -1)
    full_k = doubled_rows(own, "fsdp").reshape(feats.shape[3], repeats, -1)
    full_k = jnp.transpose(full_k, (1, 2, 0)).astype(jnp.float32)

    spots = jnp.arange(frames, dtype=jnp.int32)
    starts = mask_starts[:, 0][:, :, None]
    covered = jnp.any(
        (spots[None, None, :] >= starts) & (spots[None, None, :] < starts + MASK_LEN), axis=1
    )
    masked_in = jnp.where(covered[:, :, None], mask_embed[None, None, :], feats_local)

    def work(step, s):
        offset = step - s
        if offset < 0:
            return None
        turn, slot = offset // sections, offset % sections
        return (turn, slot) if slot < micro and turn < repeats else None

    steps = repeats * sections + micro - 1
    plans = [[work(step, s) for s in range(sections)] for step in range(steps)]
    table = [
        [
            [
                int(plan[s] is not None),
                0 if plan[s] is None else plan[s][0],
                int(s == 0 and plan[s] is not None and plan[s][0] == 0),
                int(s == last),
            ]
            for plan in plans + plans[:1]
        ]
        for s in range(sections)
    ]
    odd = lax.axis_index("fsdp") % 2
    lanes = lax.broadcasted_iota(jnp.int32, (steps + 1, 4), 1)
    entries = lax.broadcasted_iota(jnp.int32, (steps + 1, 4), 0)
    off = (lanes == 0) & (((entries == 0) & (odd == 1)) | ((entries == steps) & (odd == 0)))
    flags = lax.dynamic_index_in_dim(jnp.array(table, jnp.int32), section, 0, keepdims=False)
    flags = jnp.where(off, 0, flags)

    picks = distractors[:, 0]
    count = picks.shape[2]
    pieces = [
        picks if s == last else lax.ppermute(picks, "section", [(s, last)]) for s in range(sections)
    ]
    picks = jnp.concatenate(pieces, axis=1)
    picks = jnp.pad(picks, ((0, 0), (0, 0), (0, -count % LANES)))
    tgt = targets(feats_local, w_tgt)

    beside = (full_k, masked_in, flags, picks, tgt)
    if lax.axis_size("fsdp") == 8:
        pieces, starts = crossed(w_in[0, 0], "fsdp")
        kind = "pieces"
        (pieces, starts), beside = lax.optimization_barrier(((pieces, starts), beside))
    else:
        pieces, starts = [lax.all_gather(w_in[0, 0], "fsdp", axis=0, tiled=True)], None
        kind = "rows"
        pieces, beside = lax.optimization_barrier((pieces, beside))
    full_k, masked_in, flags, picks, tgt = beside

    result = layer(0, flags, masked_in, 0, None, [(0, kind, pieces)], full_k, taps, starts)
    kept = pieces if starts is None else [result[1]]
    w_late, kept = lax.optimization_barrier((w_in, kept))
    weights = [(0, kind if starts is None else "chunked", kept)]
    result = result[0]
    for turn in range(1, repeats):
        rows = w_late[turn, 0]
        weights.append((turn, "rows", [lax.all_gather(rows, "fsdp", axis=0, tiled=True)]))

    size = lax.axis_size("fsdp")
    token = lax.ppermute(result[:16, :LANES], "fsdp", [(i, i + 1) for i in range(0, size, 2)])
    result = layer(
        steps, flags, masked_in, 0, None, weights[:1], full_k, taps, None, (result, token)
    )[0]
    losses = []
    for step, plan in enumerate(plans):
        if step > 0:
            turns = sorted({item[0] for item in plan if item is not None})
            slot = plan[0][1] if plan[0] is not None and plan[0][0] == 0 else None
            used = [weights[turn] for turn in turns]
            result = layer(step, flags, masked_in, slot, state, used, full_k, taps)[0]
        ends = plan[last]
        if ends is not None and ends[0] == repeats - 1:
            losses.append(loss_rows(ends[1], flags, result, w_ctx, tgt, picks, count))
        route = []
        for s, item in enumerate(plan):
            if item is not None and not (s == last and item[0] == repeats - 1):
                route.append((s, (s + 1) % sections))
        if route:
            state = lax.ppermute(result, "section", route)

    loss = jnp.concatenate(losses, axis=0)
    share = frames // sections
    mine = jnp.zeros((micro, share), jnp.float32)
    for s in range(sections):
        cut = loss[:, s * share : (s + 1) * share]
        if s == last:
            mine = mine + jnp.where(section == last, cut, 0.0)
        else:
            mine = mine + lax.ppermute(cut, "section", [(last, s)])
    return mine[:, None, :]


def solution(mesh):
    placed = (
        P(None, "fsdp", None, None),
        P(None, "section", "fsdp", None),
        P(None, "section", None, "fsdp"),
        P(),
        P(),
        P(),
        P(None, "fsdp", None),
        P(None, "fsdp", "section", None),
    )
    return jax.shard_map(
        on_device, mesh=mesh, in_specs=placed, out_specs=P(None, "fsdp", "section"), check_vma=False
    )
```

```python
import functools

import jax
import jax.numpy as jnp
from jax import lax
from jax.experimental import pallas as pl
from jax.experimental.pallas import tpu as pltpu
from jax.sharding import PartitionSpec as P

MASK_LEN = 10
LANES = 128
PAD = 16
VMEM_LIMIT = 48 * 1024 * 1024


def sigmoid(v):
    return 0.5 + 0.5 * jnp.tanh(0.5 * v)


def layer_body(entry, taps, kinds, fresh_slot, recvs, spare, flags, *refs):
    refs = list(refs)
    fresh = refs.pop(0) if fresh_slot is not None else None
    recv = [refs.pop(0) for _ in range(recvs)]
    sources = [[refs.pop(0) for _ in range(count)] for _, _, count in kinds]
    starts, k_ref = refs.pop(0), refs.pop(0)
    del refs[:spare]
    out_ref, mark_ref, normed, wbuf, glu, w_sem = (refs.pop(0) for _ in range(6))
    x_ref, x_sem = refs if refs else (recv[0], None)
    chunks, _, width, part = wbuf.shape
    frames = x_ref.shape[0]
    subs = part // LANES
    rows = min(128, frames)
    half = taps // 2
    valid = flags[entry, 0]
    turn = flags[entry, 1]

    def weight_copies(kind, source, j, side):
        target, sem = wbuf.at[j, side], w_sem.at[j, side]
        cols = pl.ds(pl.multiple_of(side * width + j * part, part), part)
        if kind == "rows":
            return [pltpu.make_async_copy(source[0].at[:, cols], target, sem)]
        copies = []
        for i, piece in enumerate(source):
            size = piece.shape[0]
            place = pl.ds(pl.multiple_of(starts[i], size), size)
            copies.append(pltpu.make_async_copy(piece.at[:, cols], target.at[place], sem))
        return copies

    def start_weights(j):
        def issue(kind, source):
            for side in range(2):
                for copy in weight_copies(kind, source, j, side):
                    copy.start()

        for (which, kind, _), source in zip(kinds, sources):
            if len(kinds) == 1:
                issue(kind, source)
            else:
                pl.when(turn == which)(functools.partial(issue, kind, source))

    def wait_weights(j):
        for side in range(2):
            target = wbuf.at[j, side]
            pltpu.make_async_copy(target, target, w_sem.at[j, side]).wait()

    def project(j, slot):
        values = jnp.dot(normed[...], wbuf[j, 0], preferred_element_type=jnp.float32)
        gates = jnp.dot(normed[...], wbuf[j, 1], preferred_element_type=jnp.float32)
        gated = (values * sigmoid(gates)).astype(jnp.bfloat16).astype(jnp.float32)
        for sub in range(subs):
            glu[slot, sub, PAD : PAD + frames, :] = gated[:, sub * LANES : (sub + 1) * LANES]

    def mix(j, slot):
        for sub in range(subs):
            first = pl.multiple_of(j * part + sub * LANES, LANES)
            cols = pl.ds(first, LANES)
            scale = k_ref[turn, :, cols]
            for row in range(0, frames, rows):
                acc = jnp.zeros((rows, LANES), jnp.float32)
                for low in range(8):
                    highs = range(low, taps, 8)
                    begin = row + PAD - half + low
                    span = glu[slot, sub, begin : begin + rows + highs[-1] - low, :]
                    for tap in highs:
                        acc = acc + span[tap - low : tap - low + rows] * scale[tap : tap + 1]
                base = x_ref[row : row + rows, cols].astype(jnp.float32)
                out_ref[row : row + rows, cols] = (base + acc * sigmoid(acc)).astype(jnp.bfloat16)

    @pl.when(valid == 1)
    def _():
        ahead = min(3, chunks)
        if x_sem is not None:
            options = ([] if fresh is None else [fresh.at[fresh_slot]]) + recv
            first = 0 if fresh is not None else 1
            for i, option in enumerate(options):

                @pl.when(flags[entry, 2] == first + i)
                def _(option=option):
                    pltpu.make_async_copy(option, x_ref, x_sem).start()

        for j in range(ahead):
            start_weights(j)
        zeros = jnp.zeros((2, subs, PAD, LANES), jnp.float32)
        glu[:, :, 0:PAD, :] = zeros
        glu[:, :, PAD + frames :, :] = zeros
        if x_sem is not None:
            pltpu.make_async_copy(x_ref, x_ref, x_sem).wait()
        for row in range(0, frames, 64):
            values = x_ref[row : row + 64, :].astype(jnp.float32)
            center = jnp.mean(values, axis=1, keepdims=True)
            moved = values - center
            spread = jnp.mean(moved * moved, axis=1, keepdims=True)
            normed[row : row + 64, :] = (moved * lax.rsqrt(spread + 1e-05)).astype(jnp.bfloat16)
        wait_weights(0)
        project(0, 0)

        @pl.loop(0, chunks - 1)
        def _(j):
            wait_weights(j + 1)

            @pl.when(j + ahead < chunks)
            def _():
                start_weights(j + ahead)

            mix(j, j % 2)
            project(j + 1, (j + 1) % 2)

        mix(chunks - 1, (chunks - 1) % 2)

    mark_ref[...] = jnp.zeros(mark_ref.shape, mark_ref.dtype)


def layer(entry, flags, fresh, fresh_slot, recvs, weights, starts, kernels, taps, spare=()):
    frames, width = recvs[0].shape if recvs else fresh.shape[1:]
    part = 256
    chunks = width // part
    anywhere = pl.BlockSpec(memory_space=pl.ANY)
    local = pl.BlockSpec(memory_space=pltpu.VMEM)
    smem = pl.BlockSpec(memory_space=pltpu.SMEM)
    select = fresh_slot is not None or len(recvs) > 1
    operands, specs = [flags], [smem]
    if fresh_slot is not None:
        operands.append(fresh)
        specs.append(anywhere)
    operands += recvs
    specs += [anywhere if select else local] * len(recvs)
    for _, _, arrays in weights:
        operands += arrays
        specs += [anywhere] * len(arrays)
    operands += [starts, kernels, *spare]
    specs += [smem, local] + [anywhere] * len(spare)
    scratch = [
        pltpu.VMEM((frames, width), jnp.bfloat16),
        pltpu.VMEM((chunks, 2, width, part), jnp.bfloat16),
        pltpu.VMEM((2, part // LANES, frames + 2 * PAD, LANES), jnp.float32),
        pltpu.SemaphoreType.DMA((chunks, 2)),
    ]
    if select:
        scratch += [pltpu.VMEM((frames, width), jnp.bfloat16), pltpu.SemaphoreType.DMA]
    kinds = [(turn, kind, len(arrays)) for turn, kind, arrays in weights]
    return pl.pallas_call(
        functools.partial(
            layer_body, entry, taps, kinds, fresh_slot, len(recvs), len(spare)
        ),
        in_specs=specs,
        out_specs=[local, local],
        out_shape=[
            jax.ShapeDtypeStruct((frames, width), jnp.bfloat16),
            jax.ShapeDtypeStruct((8, LANES), jnp.float32),
        ],
        scratch_shapes=scratch,
        compiler_params=pltpu.CompilerParams(vmem_limit_bytes=VMEM_LIMIT),
        cost_estimate=pl.CostEstimate(
            flops=4 * frames * width * width, bytes_accessed=4 * width * width, transcendentals=0
        ),
        name="layer",
    )(*operands)


def unit_rows(values):
    return (values * lax.rsqrt(jnp.sum(values * values, axis=-1, keepdims=True) + 1e-06)).astype(
        jnp.bfloat16
    )


def target_body(feats_ref, w_ref, out_ref):
    out_ref[0] = unit_rows(jnp.dot(feats_ref[0], w_ref[...], preferred_element_type=jnp.float32))


def targets(feats, w_tgt):
    micro, frames, width = feats.shape
    wide = w_tgt.shape[1]
    return pl.pallas_call(
        target_body,
        grid=(micro,),
        in_specs=[
            pl.BlockSpec((1, frames, width), lambda i: (i, 0, 0)),
            pl.BlockSpec((width, wide), lambda i: (0, 0)),
        ],
        out_specs=pl.BlockSpec((1, frames, wide), lambda i: (i, 0, 0)),
        out_shape=jax.ShapeDtypeStruct((micro, frames, wide), jnp.bfloat16),
        compiler_params=pltpu.CompilerParams(vmem_limit_bytes=VMEM_LIMIT),
        cost_estimate=pl.CostEstimate(
            flops=2 * feats.size * wide,
            bytes_accessed=2 * (feats.size + w_tgt.size),
            transcendentals=0,
        ),
        name="targets",
    )(feats, w_tgt)


def loss_body(slot, count, flags, x_ref, w_ref, tgt_ref, pick_ref, out_ref):
    frames = x_ref.shape[0]

    @pl.when(flags[0, 3] == 1)
    def _():
        ctx = unit_rows(jnp.dot(x_ref[...], w_ref[...], preferred_element_type=jnp.float32))
        sims = lax.dot_general(
            ctx, tgt_ref[slot], (((1,), (1,)), ((), ())), preferred_element_type=jnp.float32
        )
        row = lax.broadcasted_iota(jnp.int32, sims.shape, 0)
        col = lax.broadcasted_iota(jnp.int32, sims.shape, 1)
        positive = jnp.sum(jnp.where(row == col, sims, 0.0), axis=1, keepdims=True) * 10.0
        picks = pick_ref[slot]
        lane = picks % LANES
        block = picks // LANES
        negative = jnp.zeros(picks.shape, jnp.float32)
        for part in range(frames // LANES):
            found = jnp.take_along_axis(sims[:, part * LANES : (part + 1) * LANES], lane, axis=1)
            negative = jnp.where(block == part, found, negative)
        place = lax.broadcasted_iota(jnp.int32, picks.shape, 1)
        terms = jnp.where(place < count, jnp.exp(negative * 10.0), 0.0)
        total = jnp.exp(positive) + jnp.sum(terms, axis=1, keepdims=True)
        wide = jnp.broadcast_to(jnp.log(total) - positive, (frames, LANES))
        out_ref[...] = wide.T[0:1, :]


def loss_rows(slot, flags, x, w_ctx, tgt, picks, count):
    frames = x.shape[0]
    whole = pl.BlockSpec(memory_space=pltpu.VMEM)
    return pl.pallas_call(
        functools.partial(loss_body, slot, count),
        in_specs=[pl.BlockSpec(memory_space=pltpu.SMEM)] + [whole] * 4,
        out_specs=whole,
        out_shape=jax.ShapeDtypeStruct((1, frames), jnp.float32),
        compiler_params=pltpu.CompilerParams(vmem_limit_bytes=VMEM_LIMIT),
        name="loss",
    )(flags, x, w_ctx, tgt, picks)


def swap(block, axis, mask):
    return lax.ppermute(block, axis, [(i, i ^ mask) for i in range(lax.axis_size(axis))])


def doubled_rows(block, axis):
    me = lax.axis_index(axis)
    size = lax.axis_size(axis)
    if size & (size - 1):
        return lax.all_gather(block, axis, axis=0, tiled=True)
    rows = block.shape[0]
    mask = 1
    held = block
    while mask < size:
        held = jnp.concatenate([held, swap(held, axis, mask)], axis=0)
        mask *= 2
    whole = jnp.zeros_like(held)
    for mask in range(size):
        piece = held[mask * rows : (mask + 1) * rows]
        whole = lax.dynamic_update_slice_in_dim(whole, piece, (me ^ mask) * rows, 0)
    return whole


def crossed(block, axis):
    size = lax.axis_size(axis)
    me = lax.axis_index(axis)
    odd = me % 2
    ahead = [(i, i ^ (2 if i % 2 else 4)) for i in range(size)]
    other = [(i, i ^ (4 if i % 2 else 2)) for i in range(size)]
    near = lax.ppermute(block, axis, ahead)
    block, near = lax.optimization_barrier((block, near))
    far = lax.ppermute(near, axis, other)
    side = lax.ppermute(block, axis, other)
    first, second = 4 - 2 * odd, 2 + 2 * odd
    pieces = [block, near, side, far]
    masks = [0, first, second, 6]
    pieces += [swap(piece, axis, 1) for piece in pieces]
    masks += [1, second ^ 1, first ^ 1, 7]
    starts = jnp.stack([(me ^ mask) * block.shape[0] for mask in masks]).astype(jnp.int32)
    return pieces, starts, near


def on_device(feats, w_in, dw_kernel, mask_embed, w_ctx, w_tgt, mask_starts, distractors):
    sections = lax.axis_size("section")
    section = lax.axis_index("section")
    micro = feats.shape[0]
    frames = feats.shape[2]
    repeats = w_in.shape[0]
    last = sections - 1
    feats_local = feats[:, 0]

    spots = jnp.arange(frames, dtype=jnp.int32)
    starts = mask_starts[:, 0][:, :, None]
    covered = jnp.any(
        (spots[None, None, :] >= starts) & (spots[None, None, :] < starts + MASK_LEN), axis=1
    )
    masked_in = jnp.where(covered[:, :, None], mask_embed[None, None, :], feats_local)

    def work(step, s):
        offset = step - s
        if offset < 0:
            return None
        turn, slot = offset // sections, offset % sections
        return (turn, slot) if slot < micro and turn < repeats else None

    steps = repeats * sections + micro - 1
    plans = [[work(step, s) for s in range(sections)] for step in range(steps)]
    table = [
        [
            [
                int(plan[s] is not None),
                0 if plan[s] is None else plan[s][0],
                int(not (s == 0 and plan[s] is not None and plan[s][0] == 0)),
                int(s == last),
            ]
            for plan in plans + plans[:1]
        ]
        for s in range(sections)
    ]
    odd = lax.axis_index("fsdp") % 2
    lanes = lax.broadcasted_iota(jnp.int32, (steps + 1, 4), 1)
    entries = lax.broadcasted_iota(jnp.int32, (steps + 1, 4), 0)
    off = (lanes == 0) & (((entries == 0) & (odd == 1)) | ((entries == steps) & (odd == 0)))
    flags = lax.dynamic_index_in_dim(jnp.array(table, jnp.int32), section, 0, keepdims=False)
    flags = jnp.where(off, 0, flags)
    flags = jnp.where((entries == 1) & (lanes == 2) & (flags == 1), 1 + odd, flags)

    size = lax.axis_size("fsdp")
    if size == 8:
        pieces, starts, near = crossed(w_in[0, 0], "fsdp")
        kind = "pieces"
        dw, picks, near = lax.optimization_barrier((dw_kernel, distractors[:, 0], near))
        pieces[1] = near
    else:
        pieces = [lax.all_gather(w_in[0, 0], "fsdp", axis=0, tiled=True)]
        starts = jnp.zeros((1,), jnp.int32)
        kind = "rows"
        dw, picks = dw_kernel, distractors[:, 0]
    taps = dw.shape[2]
    own = jnp.swapaxes(jnp.pad(dw[:, 0], ((0, 0), (0, -taps % 8), (0, 0))), 1, 2)
    own = jnp.swapaxes(own, 0, 1).reshape(own.shape[1], -1)
    full_k = doubled_rows(own, "fsdp").reshape(feats.shape[3], repeats, -1)
    full_k = jnp.transpose(full_k, (1, 2, 0)).astype(jnp.float32)

    count = picks.shape[2]
    parts = [
        picks if s == last else lax.ppermute(picks, "section", [(s, last)]) for s in range(sections)
    ]
    picks = jnp.concatenate(parts, axis=1)
    picks = jnp.pad(picks, ((0, 0), (0, 0), (0, -count % LANES)))
    tgt = targets(feats_local, w_tgt)

    beside = (full_k, masked_in, flags, picks, tgt, starts)
    pieces, beside = lax.optimization_barrier((pieces, beside))
    full_k, masked_in, flags, picks, tgt, starts = beside
    weights = [(0, kind, pieces)]

    def first_hop(block, parity):
        route = [(f, size + f) for f in range(parity, size, 2)]
        return lax.ppermute(block, ("section", "fsdp"), route)

    early, mark = layer(0, flags, masked_in, 0, [], weights, starts, full_k, taps)
    token = lax.ppermute(mark, "fsdp", [(i, i + 1) for i in range(0, size, 2)])
    early = first_hop(early, 0)
    result, mark = layer(steps, flags, masked_in, 0, [], weights, starts, full_k, taps, (token,))
    state = [early, first_hop(result, 1)]
    w_late, mark = lax.optimization_barrier((w_in, mark))
    for turn in range(1, repeats):
        rows = w_late[turn, 0]
        weights.append((turn, "rows", [lax.all_gather(rows, "fsdp", axis=0, tiled=True)]))

    losses = []
    for step, plan in enumerate(plans):
        if step == 0:
            continue
        turns = sorted({item[0] for item in plan if item is not None})
        slot = plan[0][1] if plan[0] is not None and plan[0][0] == 0 else None
        used = [weights[turn] for turn in turns]
        spare = (mark,) if step == 1 else ()
        result, _ = layer(step, flags, masked_in, slot, state, used, starts, full_k, taps, spare)
        ends = plan[last]
        if ends is not None and ends[0] == repeats - 1:
            losses.append(loss_rows(ends[1], flags, result, w_ctx, tgt, picks, count))
        route = []
        for s, item in enumerate(plan):
            if item is not None and not (s == last and item[0] == repeats - 1):
                route.append((s, (s + 1) % sections))
        if route:
            state = [lax.ppermute(result, "section", route)]

    loss = jnp.concatenate(losses, axis=0)
    share = frames // sections
    mine = jnp.zeros((micro, share), jnp.float32)
    for s in range(sections):
        cut = loss[:, s * share : (s + 1) * share]
        if s == last:
            mine = mine + jnp.where(section == last, cut, 0.0)
        else:
            mine = mine + lax.ppermute(cut, "section", [(last, s)])
    return mine[:, None, :]


def solution(mesh):
    placed = (
        P(None, "fsdp", None, None),
        P(None, "section", "fsdp", None),
        P(None, "section", None, "fsdp"),
        P(),
        P(),
        P(),
        P(None, "fsdp", None),
        P(None, "fsdp", "section", None),
    )
    return jax.shard_map(
        on_device, mesh=mesh, in_specs=placed, out_specs=P(None, "fsdp", "section"), check_vma=False
    )
```

```python
import functools

import jax
import jax.numpy as jnp
from jax import lax
from jax.experimental import pallas as pl
from jax.experimental.pallas import tpu as pltpu
from jax.sharding import PartitionSpec as P

MASK_LEN = 10
LANES = 128
PAD = 16
VMEM_LIMIT = 48 * 1024 * 1024


def sigmoid(v):
    return 0.5 + 0.5 * jnp.tanh(0.5 * v)


def layer_body(entry, taps, kinds, fresh_slot, recvs, spare, flags, *refs):
    refs = list(refs)
    fresh = refs.pop(0) if fresh_slot is not None else None
    recv = [refs.pop(0) for _ in range(recvs)]
    sources = [[refs.pop(0) for _ in range(count)] for _, _, count in kinds]
    starts, k_ref = refs.pop(0), refs.pop(0)
    del refs[:spare]
    out_ref, mark_ref, normed, wbuf, glu, w_sem = (refs.pop(0) for _ in range(6))
    x_ref, x_sem = refs if refs else (recv[0], None)
    chunks, _, width, part = wbuf.shape
    frames = x_ref.shape[0]
    subs = part // LANES
    rows = min(128, frames)
    half = taps // 2
    valid = flags[entry, 0]
    turn = flags[entry, 1]

    def weight_copies(kind, source, j, side):
        target, sem = wbuf.at[j, side], w_sem.at[j, side]
        cols = pl.ds(pl.multiple_of(side * width + j * part, part), part)
        if kind == "rows":
            return [pltpu.make_async_copy(source[0].at[:, cols], target, sem)]
        copies = []
        for i, piece in enumerate(source):
            size = piece.shape[0]
            place = pl.ds(pl.multiple_of(starts[i], size), size)
            copies.append(pltpu.make_async_copy(piece.at[:, cols], target.at[place], sem))
        return copies

    def start_weights(j):
        def issue(kind, source):
            for side in range(2):
                for copy in weight_copies(kind, source, j, side):
                    copy.start()

        for (which, kind, _), source in zip(kinds, sources):
            if len(kinds) == 1:
                issue(kind, source)
            else:
                pl.when(turn == which)(functools.partial(issue, kind, source))

    def wait_weights(j):
        for side in range(2):
            target = wbuf.at[j, side]
            pltpu.make_async_copy(target, target, w_sem.at[j, side]).wait()

    def project(j, slot):
        values = jnp.dot(normed[...], wbuf[j, 0], preferred_element_type=jnp.float32)
        gates = jnp.dot(normed[...], wbuf[j, 1], preferred_element_type=jnp.float32)
        gated = (values * sigmoid(gates)).astype(jnp.bfloat16).astype(jnp.float32)
        for sub in range(subs):
            glu[slot, sub, PAD : PAD + frames, :] = gated[:, sub * LANES : (sub + 1) * LANES]

    def mix(j, slot):
        for sub in range(subs):
            first = pl.multiple_of(j * part + sub * LANES, LANES)
            cols = pl.ds(first, LANES)
            scale = k_ref[turn, :, cols]
            for row in range(0, frames, rows):
                acc = jnp.zeros((rows, LANES), jnp.float32)
                for low in range(8):
                    highs = range(low, taps, 8)
                    begin = row + PAD - half + low
                    span = glu[slot, sub, begin : begin + rows + highs[-1] - low, :]
                    for tap in highs:
                        acc = acc + span[tap - low : tap - low + rows] * scale[tap : tap + 1]
                base = x_ref[row : row + rows, cols].astype(jnp.float32)
                out_ref[row : row + rows, cols] = (base + acc * sigmoid(acc)).astype(jnp.bfloat16)

    @pl.when(valid == 1)
    def _():
        ahead = min(3, chunks)
        if x_sem is not None:
            options = ([] if fresh is None else [fresh.at[fresh_slot]]) + recv
            first = 0 if fresh is not None else 1
            for i, option in enumerate(options):

                @pl.when(flags[entry, 2] == first + i)
                def _(option=option):
                    pltpu.make_async_copy(option, x_ref, x_sem).start()

        for j in range(ahead):
            start_weights(j)
        zeros = jnp.zeros((2, subs, PAD, LANES), jnp.float32)
        glu[:, :, 0:PAD, :] = zeros
        glu[:, :, PAD + frames :, :] = zeros
        if x_sem is not None:
            pltpu.make_async_copy(x_ref, x_ref, x_sem).wait()
        for row in range(0, frames, 64):
            values = x_ref[row : row + 64, :].astype(jnp.float32)
            center = jnp.mean(values, axis=1, keepdims=True)
            moved = values - center
            spread = jnp.mean(moved * moved, axis=1, keepdims=True)
            normed[row : row + 64, :] = (moved * lax.rsqrt(spread + 1e-05)).astype(jnp.bfloat16)
        wait_weights(0)
        project(0, 0)

        @pl.loop(0, chunks - 1)
        def _(j):
            wait_weights(j + 1)

            @pl.when(j + ahead < chunks)
            def _():
                start_weights(j + ahead)

            mix(j, j % 2)
            project(j + 1, (j + 1) % 2)

        mix(chunks - 1, (chunks - 1) % 2)

    mark_ref[...] = jnp.zeros(mark_ref.shape, mark_ref.dtype)


def layer(entry, flags, fresh, fresh_slot, recvs, weights, starts, kernels, taps, spare=()):
    frames, width = recvs[0].shape if recvs else fresh.shape[1:]
    part = 256
    chunks = width // part
    anywhere = pl.BlockSpec(memory_space=pl.ANY)
    local = pl.BlockSpec(memory_space=pltpu.VMEM)
    smem = pl.BlockSpec(memory_space=pltpu.SMEM)
    select = fresh_slot is not None or len(recvs) > 1
    operands, specs = [flags], [smem]
    if fresh_slot is not None:
        operands.append(fresh)
        specs.append(anywhere)
    operands += recvs
    specs += [anywhere if select else local] * len(recvs)
    for _, _, arrays in weights:
        operands += arrays
        specs += [anywhere] * len(arrays)
    operands += [starts, kernels, *spare]
    specs += [smem, local] + [anywhere] * len(spare)
    scratch = [
        pltpu.VMEM((frames, width), jnp.bfloat16),
        pltpu.VMEM((chunks, 2, width, part), jnp.bfloat16),
        pltpu.VMEM((2, part // LANES, frames + 2 * PAD, LANES), jnp.float32),
        pltpu.SemaphoreType.DMA((chunks, 2)),
    ]
    if select:
        scratch += [pltpu.VMEM((frames, width), jnp.bfloat16), pltpu.SemaphoreType.DMA]
    kinds = [(turn, kind, len(arrays)) for turn, kind, arrays in weights]
    return pl.pallas_call(
        functools.partial(
            layer_body, entry, taps, kinds, fresh_slot, len(recvs), len(spare)
        ),
        in_specs=specs,
        out_specs=[local, local],
        out_shape=[
            jax.ShapeDtypeStruct((frames, width), jnp.bfloat16),
            jax.ShapeDtypeStruct((8, LANES), jnp.float32),
        ],
        scratch_shapes=scratch,
        compiler_params=pltpu.CompilerParams(vmem_limit_bytes=VMEM_LIMIT),
        cost_estimate=pl.CostEstimate(
            flops=4 * frames * width * width, bytes_accessed=4 * width * width, transcendentals=0
        ),
        name="layer",
    )(*operands)


def unit_rows(values):
    return (values * lax.rsqrt(jnp.sum(values * values, axis=-1, keepdims=True) + 1e-06)).astype(
        jnp.bfloat16
    )


def target_body(wanted, flags, feats, w_tgt, *refs):
    out, feats_ref, w_ref, out_ref, sems = refs[-5:]

    @pl.when(flags[0, 4] == wanted)
    def _():
        load_w = pltpu.make_async_copy(w_tgt, w_ref, sems.at[0])
        load_x = pltpu.make_async_copy(feats, feats_ref, sems.at[1])
        load_w.start()
        load_x.start()
        load_w.wait()
        load_x.wait()

        @pl.loop(0, feats_ref.shape[0])
        def _(slot):
            out_ref[slot] = unit_rows(
                jnp.dot(feats_ref[slot], w_ref[...], preferred_element_type=jnp.float32)
            )

        back = pltpu.make_async_copy(out_ref, out, sems.at[2])
        back.start()
        back.wait()


def targets(flags, feats, w_tgt, wanted, spare, earlier=None):
    operands = [flags, feats, w_tgt, spare] + ([] if earlier is None else [earlier])
    anywhere = pl.BlockSpec(memory_space=pl.ANY)
    shape = feats.shape[:2] + w_tgt.shape[1:]
    return pl.pallas_call(
        functools.partial(target_body, wanted),
        in_specs=[pl.BlockSpec(memory_space=pltpu.SMEM)] + [anywhere] * (len(operands) - 1),
        out_specs=anywhere,
        out_shape=jax.ShapeDtypeStruct(shape, jnp.bfloat16),
        scratch_shapes=[
            pltpu.VMEM(feats.shape, jnp.bfloat16),
            pltpu.VMEM(w_tgt.shape, jnp.bfloat16),
            pltpu.VMEM(shape, jnp.bfloat16),
            pltpu.SemaphoreType.DMA((3,)),
        ],
        input_output_aliases={} if earlier is None else {4: 0},
        compiler_params=pltpu.CompilerParams(vmem_limit_bytes=VMEM_LIMIT),
        cost_estimate=pl.CostEstimate(
            flops=2 * feats.size * w_tgt.shape[1],
            bytes_accessed=2 * (feats.size + w_tgt.size),
            transcendentals=0,
        ),
        name="targets",
    )(*operands)


def loss_body(slot, count, flags, x_ref, w_ref, tgt_ref, pick_ref, out_ref):
    frames = x_ref.shape[0]

    @pl.when(flags[0, 3] == 1)
    def _():
        ctx = unit_rows(jnp.dot(x_ref[...], w_ref[...], preferred_element_type=jnp.float32))
        sims = lax.dot_general(
            ctx, tgt_ref[slot], (((1,), (1,)), ((), ())), preferred_element_type=jnp.float32
        )
        row = lax.broadcasted_iota(jnp.int32, sims.shape, 0)
        col = lax.broadcasted_iota(jnp.int32, sims.shape, 1)
        positive = jnp.sum(jnp.where(row == col, sims, 0.0), axis=1, keepdims=True) * 10.0
        picks = pick_ref[slot]
        lane = picks % LANES
        block = picks // LANES
        negative = jnp.zeros(picks.shape, jnp.float32)
        for part in range(frames // LANES):
            found = jnp.take_along_axis(sims[:, part * LANES : (part + 1) * LANES], lane, axis=1)
            negative = jnp.where(block == part, found, negative)
        place = lax.broadcasted_iota(jnp.int32, picks.shape, 1)
        terms = jnp.where(place < count, jnp.exp(negative * 10.0), 0.0)
        total = jnp.exp(positive) + jnp.sum(terms, axis=1, keepdims=True)
        wide = jnp.broadcast_to(jnp.log(total) - positive, (frames, LANES))
        out_ref[...] = wide.T[0:1, :]


def loss_rows(slot, flags, x, w_ctx, tgt, picks, count):
    frames = x.shape[0]
    whole = pl.BlockSpec(memory_space=pltpu.VMEM)
    return pl.pallas_call(
        functools.partial(loss_body, slot, count),
        in_specs=[pl.BlockSpec(memory_space=pltpu.SMEM)] + [whole] * 4,
        out_specs=whole,
        out_shape=jax.ShapeDtypeStruct((1, frames), jnp.float32),
        compiler_params=pltpu.CompilerParams(vmem_limit_bytes=VMEM_LIMIT),
        name="loss",
    )(flags, x, w_ctx, tgt, picks)


def swap(block, axis, mask):
    return lax.ppermute(block, axis, [(i, i ^ mask) for i in range(lax.axis_size(axis))])


def doubled_rows(block, axis):
    me = lax.axis_index(axis)
    size = lax.axis_size(axis)
    if size & (size - 1):
        return lax.all_gather(block, axis, axis=0, tiled=True)
    mask = 1
    while mask < size:
        other = swap(block, axis, mask)
        upper = (me & mask) != 0
        block = jnp.concatenate(
            [jnp.where(upper, other, block), jnp.where(upper, block, other)], axis=0
        )
        mask *= 2
    return block


def crossed(block, axis):
    size = lax.axis_size(axis)
    me = lax.axis_index(axis)
    odd = me % 2
    ahead = [(i, i ^ (2 if i % 2 else 4)) for i in range(size)]
    other = [(i, i ^ (4 if i % 2 else 2)) for i in range(size)]
    near = lax.ppermute(block, axis, ahead)
    block, near = lax.optimization_barrier((block, near))
    far = lax.ppermute(near, axis, other)
    side = lax.ppermute(block, axis, other)
    first, second = 4 - 2 * odd, 2 + 2 * odd
    pieces = [block, near, side, far]
    masks = [0, first, second, 6]
    pieces += [swap(piece, axis, 1) for piece in pieces]
    masks += [1, second ^ 1, first ^ 1, 7]
    starts = jnp.stack([(me ^ mask) * block.shape[0] for mask in masks]).astype(jnp.int32)
    return pieces, starts, near


def on_device(feats, w_in, dw_kernel, mask_embed, w_ctx, w_tgt, mask_starts, distractors):
    sections = lax.axis_size("section")
    section = lax.axis_index("section")
    micro = feats.shape[0]
    frames = feats.shape[2]
    repeats = w_in.shape[0]
    last = sections - 1
    feats_local = feats[:, 0]

    spots = jnp.arange(frames, dtype=jnp.int32)
    starts = mask_starts[:, 0][:, :, None]
    covered = jnp.any(
        (spots[None, None, :] >= starts) & (spots[None, None, :] < starts + MASK_LEN), axis=1
    )
    masked_in = jnp.where(covered[:, :, None], mask_embed[None, None, :], feats_local)

    def work(step, s):
        offset = step - s
        if offset < 0:
            return None
        turn, slot = offset // sections, offset % sections
        return (turn, slot) if slot < micro and turn < repeats else None

    steps = repeats * sections + micro - 1
    plans = [[work(step, s) for s in range(sections)] for step in range(steps)]
    table = [
        [
            [
                int(plan[s] is not None),
                0 if plan[s] is None else plan[s][0],
                int(not (s == 0 and plan[s] is not None and plan[s][0] == 0)),
                int(s == last),
                0,
            ]
            for plan in plans + plans[:1]
        ]
        for s in range(sections)
    ]
    odd = lax.axis_index("fsdp") % 2
    lanes = lax.broadcasted_iota(jnp.int32, (steps + 1, 5), 1)
    entries = lax.broadcasted_iota(jnp.int32, (steps + 1, 5), 0)
    off = (lanes == 0) & (((entries == 0) & (odd == 1)) | ((entries == steps) & (odd == 0)))
    flags = lax.dynamic_index_in_dim(jnp.array(table, jnp.int32), section, 0, keepdims=False)
    flags = jnp.where(off, 0, flags)
    flags = jnp.where(lanes == 4, odd, flags)
    flags = jnp.where((entries == 1) & (lanes == 2) & (flags == 1), 1 + odd, flags)

    size = lax.axis_size("fsdp")
    if size == 8:
        pieces, starts, near = crossed(w_in[0, 0], "fsdp")
        kind = "pieces"
        dw, near = lax.optimization_barrier((dw_kernel, near))
        pieces[1] = near
    else:
        pieces = [lax.all_gather(w_in[0, 0], "fsdp", axis=0, tiled=True)]
        starts = jnp.zeros((1,), jnp.int32)
        kind = "rows"
        dw = dw_kernel
    taps = dw.shape[2]
    own = jnp.swapaxes(jnp.pad(dw[:, 0], ((0, 0), (0, -taps % 8), (0, 0))), 1, 2)
    own = jnp.swapaxes(own, 0, 1).reshape(own.shape[1], -1)
    full_k = doubled_rows(own, "fsdp").reshape(feats.shape[3], repeats, -1)
    full_k = jnp.transpose(full_k, (1, 2, 0)).astype(jnp.float32)

    beside = (full_k, masked_in, flags, starts)
    pieces, beside = lax.optimization_barrier((pieces, beside))
    full_k, masked_in, flags, starts = beside
    weights = [(0, kind, pieces)]

    def first_hop(block, parity):
        route = [(f, size + f) for f in range(parity, size, 2)]
        return lax.ppermute(block, ("section", "fsdp"), route)

    early, mark = layer(0, flags, masked_in, 0, [], weights, starts, full_k, taps)
    token = lax.ppermute(mark, "fsdp", [(i, i + 1) for i in range(0, size, 2)])
    early = first_hop(early, 0)
    tgt = targets(flags, feats_local, w_tgt, 1, token)
    result, mark = layer(steps, flags, masked_in, 0, [], weights, starts, full_k, taps, (tgt,))
    state = [early, first_hop(result, 1)]
    w_late, picks, mark = lax.optimization_barrier((w_in, distractors[:, 0], mark))
    for turn in range(1, repeats):
        rows = w_late[turn, 0]
        weights.append((turn, "rows", [lax.all_gather(rows, "fsdp", axis=0, tiled=True)]))
    tgt = targets(flags, feats_local, w_tgt, 0, mark, tgt)
    count = picks.shape[2]
    parts = [
        picks if s == last else lax.ppermute(picks, "section", [(s, last)]) for s in range(sections)
    ]

    losses = []
    for step, plan in enumerate(plans):
        if step == 0:
            continue
        turns = sorted({item[0] for item in plan if item is not None})
        slot = plan[0][1] if plan[0] is not None and plan[0][0] == 0 else None
        used = [weights[turn] for turn in turns]
        spare = (tgt, *parts) if step == 1 else ()
        result, _ = layer(step, flags, masked_in, slot, state, used, starts, full_k, taps, spare)
        if step == 1:
            picks = jnp.pad(jnp.concatenate(parts, axis=1), ((0, 0), (0, 0), (0, -count % LANES)))
        ends = plan[last]
        if ends is not None and ends[0] == repeats - 1:
            losses.append(loss_rows(ends[1], flags, result, w_ctx, tgt, picks, count))
        route = []
        for s, item in enumerate(plan):
            if item is not None and not (s == last and item[0] == repeats - 1):
                route.append((s, (s + 1) % sections))
        if route:
            state = [lax.ppermute(result, "section", route)]

    loss = jnp.concatenate(losses, axis=0)
    share = frames // sections
    mine = jnp.zeros((micro, share), jnp.float32)
    for s in range(sections):
        cut = loss[:, s * share : (s + 1) * share]
        if s == last:
            mine = mine + jnp.where(section == last, cut, 0.0)
        else:
            mine = mine + lax.ppermute(cut, "section", [(last, s)])
    return mine[:, None, :]


def solution(mesh):
    placed = (
        P(None, "fsdp", None, None),
        P(None, "section", "fsdp", None),
        P(None, "section", None, "fsdp"),
        P(),
        P(),
        P(),
        P(None, "fsdp", None),
        P(None, "fsdp", "section", None),
    )
    return jax.shard_map(
        on_device, mesh=mesh, in_specs=placed, out_specs=P(None, "fsdp", "section"), check_vma=False
    )
```

```python
import functools

import jax
import jax.numpy as jnp
from jax import lax
from jax.experimental import pallas as pl
from jax.experimental.pallas import tpu as pltpu
from jax.sharding import PartitionSpec as P

MASK_LEN = 10
LANES = 128
PAD = 16
VMEM_LIMIT = 48 * 1024 * 1024


def sigmoid(v):
    return 0.5 + 0.5 * jnp.tanh(0.5 * v)


def layer_body(entry, taps, kinds, fresh_slot, recvs, spare, base, flags, *refs):
    refs = list(refs)
    fresh = refs.pop(0) if fresh_slot is not None else None
    recv = [refs.pop(0) for _ in range(recvs)]
    sources = [[refs.pop(0) for _ in range(count)] for _, _, count in kinds]
    starts, k_ref = refs.pop(0), refs.pop(0)
    del refs[:spare]
    out_ref, mark_ref, normed, wbuf, glu, w_sem = (refs.pop(0) for _ in range(6))
    x_ref, x_sem = refs if refs else (recv[0], None)
    chunks, width, part = wbuf.shape
    part = part // 2
    frames = x_ref.shape[0]
    subs = part // LANES
    rows = min(128, frames)
    half = taps // 2
    valid = flags[entry, 0]
    turn = flags[entry, 1]

    def weight_copies(kind, source, j, side):
        target, sem = wbuf.at[j, :, pl.ds(side * part, part)], w_sem.at[j]
        cols = pl.ds(pl.multiple_of(side * width + j * part, part), part)
        if kind == "rows":
            return [pltpu.make_async_copy(source[0].at[:, cols], target, sem)]
        copies = []
        for i, piece in enumerate(source):
            size = piece.shape[0]
            place = pl.ds(pl.multiple_of(starts[i], size), size)
            into = wbuf.at[j, place, pl.ds(side * part, part)]
            copies.append(pltpu.make_async_copy(piece.at[:, cols], into, sem))
        return copies

    def start_weights(j):
        def issue(kind, source):
            for side in range(2):
                for copy in weight_copies(kind, source, j, side):
                    copy.start()

        for (which, kind, _), source in zip(kinds, sources):
            if len(kinds) == 1:
                issue(kind, source)
            else:
                pl.when(turn == which)(functools.partial(issue, kind, source))

    def wait_weights(j):
        pltpu.make_async_copy(wbuf.at[j], wbuf.at[j], w_sem.at[j]).wait()

    def project(j, slot):
        both = jnp.dot(normed[...], wbuf[j], preferred_element_type=jnp.float32)
        gated = both[:, :part] * sigmoid(both[:, part:])
        gated = gated.astype(jnp.bfloat16).astype(jnp.float32)
        for sub in range(subs):
            glu[slot, sub, PAD : PAD + frames, :] = gated[:, sub * LANES : (sub + 1) * LANES]

    def mix(j, slot):
        for sub in range(subs):
            first = pl.multiple_of(j * part + sub * LANES, LANES)
            cols = pl.ds(first, LANES)
            scale = k_ref[turn, :, cols]
            for row in range(0, frames, rows):
                acc = jnp.zeros((rows, LANES), jnp.float32)
                for low in range(8):
                    highs = range(low, taps, 8)
                    begin = row + PAD - half + low
                    span = glu[slot, sub, begin : begin + rows + highs[-1] - low, :]
                    for tap in highs:
                        acc = acc + span[tap - low : tap - low + rows] * scale[tap : tap + 1]
                base = x_ref[row : row + rows, cols].astype(jnp.float32)
                out_ref[row : row + rows, cols] = (base + acc * sigmoid(acc)).astype(jnp.bfloat16)

    @pl.when(valid == 1)
    def _():
        ahead = min(3, chunks)
        if x_sem is not None:
            options = ([] if fresh is None else [fresh.at[fresh_slot]]) + recv
            first = base
            for i, option in enumerate(options):

                @pl.when(flags[entry, 2] == first + i)
                def _(option=option):
                    pltpu.make_async_copy(option, x_ref, x_sem).start()

        for j in range(ahead):
            start_weights(j)
        zeros = jnp.zeros((2, subs, PAD, LANES), jnp.float32)
        glu[:, :, 0:PAD, :] = zeros
        glu[:, :, PAD + frames :, :] = zeros
        if x_sem is not None:
            pltpu.make_async_copy(x_ref, x_ref, x_sem).wait()
        for row in range(0, frames, 64):
            values = x_ref[row : row + 64, :].astype(jnp.float32)
            center = jnp.mean(values, axis=1, keepdims=True)
            moved = values - center
            spread = jnp.mean(moved * moved, axis=1, keepdims=True)
            normed[row : row + 64, :] = (moved * lax.rsqrt(spread + 1e-05)).astype(jnp.bfloat16)
        wait_weights(0)
        project(0, 0)

        @pl.loop(0, chunks - 1)
        def _(j):
            wait_weights(j + 1)

            @pl.when(j + ahead < chunks)
            def _():
                start_weights(j + ahead)

            mix(j, j % 2)
            project(j + 1, (j + 1) % 2)

        mix(chunks - 1, (chunks - 1) % 2)

    mark_ref[...] = jnp.zeros(mark_ref.shape, mark_ref.dtype)


def layer(
    entry, flags, fresh, fresh_slot, recvs, weights, starts, kernels, taps, spare=(), base=0
):
    frames, width = recvs[0].shape if recvs else fresh.shape[1:]
    part = 256
    chunks = width // part
    anywhere = pl.BlockSpec(memory_space=pl.ANY)
    local = pl.BlockSpec(memory_space=pltpu.VMEM)
    smem = pl.BlockSpec(memory_space=pltpu.SMEM)
    select = fresh_slot is not None or len(recvs) > 1
    operands, specs = [flags], [smem]
    if fresh_slot is not None:
        operands.append(fresh)
        specs.append(anywhere)
    operands += recvs
    specs += [anywhere if select else local] * len(recvs)
    for _, _, arrays in weights:
        operands += arrays
        specs += [anywhere] * len(arrays)
    operands += [starts, kernels, *spare]
    specs += [smem, local] + [anywhere] * len(spare)
    scratch = [
        pltpu.VMEM((frames, width), jnp.bfloat16),
        pltpu.VMEM((chunks, width, 2 * part), jnp.bfloat16),
        pltpu.VMEM((2, part // LANES, frames + 2 * PAD, LANES), jnp.float32),
        pltpu.SemaphoreType.DMA((chunks,)),
    ]
    if select:
        scratch += [pltpu.VMEM((frames, width), jnp.bfloat16), pltpu.SemaphoreType.DMA]
    kinds = [(turn, kind, len(arrays)) for turn, kind, arrays in weights]
    return pl.pallas_call(
        functools.partial(
            layer_body, entry, taps, kinds, fresh_slot, len(recvs), len(spare), base
        ),
        in_specs=specs,
        out_specs=[local, local],
        out_shape=[
            jax.ShapeDtypeStruct((frames, width), jnp.bfloat16),
            jax.ShapeDtypeStruct((8, LANES), jnp.float32),
        ],
        scratch_shapes=scratch,
        compiler_params=pltpu.CompilerParams(vmem_limit_bytes=VMEM_LIMIT),
        cost_estimate=pl.CostEstimate(
            flops=4 * frames * width * width, bytes_accessed=4 * width * width, transcendentals=0
        ),
        name="layer",
    )(*operands)


def unit_rows(values):
    return (values * lax.rsqrt(jnp.sum(values * values, axis=-1, keepdims=True) + 1e-06)).astype(
        jnp.bfloat16
    )


def target_body(wanted, flags, feats, w_tgt, *refs):
    out, feats_ref, w_ref, out_ref, sems = refs[-5:]

    @pl.when(flags[0, 4] == wanted)
    def _():
        load_w = pltpu.make_async_copy(w_tgt, w_ref, sems.at[0])
        load_x = pltpu.make_async_copy(feats, feats_ref, sems.at[1])
        load_w.start()
        load_x.start()
        load_w.wait()
        load_x.wait()

        @pl.loop(0, feats_ref.shape[0])
        def _(slot):
            out_ref[slot] = unit_rows(
                jnp.dot(feats_ref[slot], w_ref[...], preferred_element_type=jnp.float32)
            )

        back = pltpu.make_async_copy(out_ref, out, sems.at[2])
        back.start()
        back.wait()


def targets(flags, feats, w_tgt, wanted, spare, earlier=None):
    operands = [flags, feats, w_tgt, spare] + ([] if earlier is None else [earlier])
    anywhere = pl.BlockSpec(memory_space=pl.ANY)
    shape = feats.shape[:2] + w_tgt.shape[1:]
    return pl.pallas_call(
        functools.partial(target_body, wanted),
        in_specs=[pl.BlockSpec(memory_space=pltpu.SMEM)] + [anywhere] * (len(operands) - 1),
        out_specs=anywhere,
        out_shape=jax.ShapeDtypeStruct(shape, jnp.bfloat16),
        scratch_shapes=[
            pltpu.VMEM(feats.shape, jnp.bfloat16),
            pltpu.VMEM(w_tgt.shape, jnp.bfloat16),
            pltpu.VMEM(shape, jnp.bfloat16),
            pltpu.SemaphoreType.DMA((3,)),
        ],
        input_output_aliases={} if earlier is None else {4: 0},
        compiler_params=pltpu.CompilerParams(vmem_limit_bytes=VMEM_LIMIT),
        cost_estimate=pl.CostEstimate(
            flops=2 * feats.size * w_tgt.shape[1],
            bytes_accessed=2 * (feats.size + w_tgt.size),
            transcendentals=0,
        ),
        name="targets",
    )(*operands)


def loss_body(slot, count, flags, x_ref, w_ref, tgt_ref, pick_ref, out_ref):
    frames = x_ref.shape[0]

    @pl.when(flags[0, 3] == 1)
    def _():
        ctx = unit_rows(jnp.dot(x_ref[...], w_ref[...], preferred_element_type=jnp.float32))
        sims = lax.dot_general(
            ctx, tgt_ref[slot], (((1,), (1,)), ((), ())), preferred_element_type=jnp.float32
        )
        row = lax.broadcasted_iota(jnp.int32, sims.shape, 0)
        col = lax.broadcasted_iota(jnp.int32, sims.shape, 1)
        positive = jnp.sum(jnp.where(row == col, sims, 0.0), axis=1, keepdims=True) * 10.0
        picks = pick_ref[slot]
        lane = picks % LANES
        block = picks // LANES
        negative = jnp.zeros(picks.shape, jnp.float32)
        for part in range(frames // LANES):
            found = jnp.take_along_axis(sims[:, part * LANES : (part + 1) * LANES], lane, axis=1)
            negative = jnp.where(block == part, found, negative)
        place = lax.broadcasted_iota(jnp.int32, picks.shape, 1)
        terms = jnp.where(place < count, jnp.exp(negative * 10.0), 0.0)
        total = jnp.exp(positive) + jnp.sum(terms, axis=1, keepdims=True)
        wide = jnp.broadcast_to(jnp.log(total) - positive, (frames, LANES))
        out_ref[...] = wide.T[0:1, :]


def loss_rows(slot, flags, x, w_ctx, tgt, picks, count):
    frames = x.shape[0]
    whole = pl.BlockSpec(memory_space=pltpu.VMEM)
    return pl.pallas_call(
        functools.partial(loss_body, slot, count),
        in_specs=[pl.BlockSpec(memory_space=pltpu.SMEM)] + [whole] * 4,
        out_specs=whole,
        out_shape=jax.ShapeDtypeStruct((1, frames), jnp.float32),
        compiler_params=pltpu.CompilerParams(vmem_limit_bytes=VMEM_LIMIT),
        name="loss",
    )(flags, x, w_ctx, tgt, picks)


def swap(block, axis, mask):
    return lax.ppermute(block, axis, [(i, i ^ mask) for i in range(lax.axis_size(axis))])


def doubled_rows(block, axis):
    me = lax.axis_index(axis)
    size = lax.axis_size(axis)
    if size & (size - 1):
        return lax.all_gather(block, axis, axis=0, tiled=True)
    mask = 1
    while mask < size:
        other = swap(block, axis, mask)
        upper = (me & mask) != 0
        block = jnp.concatenate(
            [jnp.where(upper, other, block), jnp.where(upper, block, other)], axis=0
        )
        mask *= 2
    return block


def crossed(block, axis):
    size = lax.axis_size(axis)
    me = lax.axis_index(axis)
    odd = me % 2
    ahead = [(i, i ^ (2 if i % 2 else 4)) for i in range(size)]
    other = [(i, i ^ (4 if i % 2 else 2)) for i in range(size)]
    near = lax.ppermute(block, axis, ahead)
    block, near = lax.optimization_barrier((block, near))
    far = lax.ppermute(near, axis, other)
    side = lax.ppermute(block, axis, other)
    first, second = 4 - 2 * odd, 2 + 2 * odd
    pieces = [block, near, side, far]
    masks = [0, first, second, 6]
    pieces += [swap(piece, axis, 1) for piece in pieces]
    masks += [1, second ^ 1, first ^ 1, 7]
    starts = jnp.stack([(me ^ mask) * block.shape[0] for mask in masks]).astype(jnp.int32)
    return pieces, starts, near


def on_device(feats, w_in, dw_kernel, mask_embed, w_ctx, w_tgt, mask_starts, distractors):
    sections = lax.axis_size("section")
    section = lax.axis_index("section")
    size = lax.axis_size("fsdp")
    odd = lax.axis_index("fsdp") % 2
    micro = feats.shape[0]
    frames = feats.shape[2]
    top = sections - 1
    feats_local = feats[:, 0]
    assert w_in.shape[0] == 2

    def mirrored(block):
        return lax.ppermute(block, "section", [(s, top - s) for s in range(sections)])

    slots = micro + 2 * top
    plans = [
        [[t - s if 0 <= t - s < micro else None for s in range(sections)] for t in range(slots)],
        [
            [m if 0 <= m < micro else None for m in (t - 2 * top + s for s in range(sections))]
            for t in range(slots)
        ],
    ]
    table = []
    for s in range(sections):
        rows = []
        for turn in range(2):
            for t in range(slots):
                rows.append([int(plans[turn][t][s] is not None), turn, 1, int(s == 0), 0])
                if s == (0, top)[turn]:
                    rows[-1][2] = 0
        table.append(rows + rows[:1])
    late = 2 * slots
    flags = lax.dynamic_index_in_dim(jnp.array(table, jnp.int32), section, 0, keepdims=False)
    lanes = lax.broadcasted_iota(jnp.int32, flags.shape, 1)
    entries = lax.broadcasted_iota(jnp.int32, flags.shape, 0)
    off = (lanes == 0) & (((entries == 0) & (odd == 1)) | ((entries == late) & (odd == 0)))
    flags = jnp.where(off, 0, flags)
    flags = jnp.where(lanes == 4, odd, flags)
    flags = jnp.where((entries == 1) & (lanes == 2) & (flags == 1), 1 + odd, flags)

    if size == 8:
        pieces, starts, near = crossed(w_in[0, 0], "fsdp")
        kind = "pieces"
        dw, near = lax.optimization_barrier((dw_kernel, near))
        pieces[1] = near
    else:
        pieces = [lax.all_gather(w_in[0, 0], "fsdp", axis=0, tiled=True)]
        starts = jnp.zeros((1,), jnp.int32)
        kind = "rows"
        dw = dw_kernel
    moved = mirrored(w_in[1, 0])

    taps = dw.shape[2]
    own = jnp.stack([dw[0, 0], mirrored(dw[1, 0])])
    own = jnp.transpose(jnp.pad(own, ((0, 0), (0, -taps % 8), (0, 0))), (2, 0, 1))
    full_k = doubled_rows(own.reshape(own.shape[0], -1), "fsdp")
    full_k = jnp.transpose(full_k.reshape(feats.shape[3], 2, -1), (1, 2, 0)).astype(jnp.float32)

    spots = jnp.arange(frames, dtype=jnp.int32)
    begins = mask_starts[:, 0][:, :, None]
    covered = jnp.any(
        (spots[None, None, :] >= begins) & (spots[None, None, :] < begins + MASK_LEN), axis=1
    )
    masked_in = jnp.where(covered[:, :, None], mask_embed[None, None, :], feats_local)

    beside = (full_k, masked_in, flags, starts, moved)
    pieces, beside = lax.optimization_barrier((pieces, beside))
    full_k, masked_in, flags, starts, moved = beside
    up = [(0, kind, pieces)]
    down = [(1, "rows", [lax.all_gather(moved, "fsdp", axis=0, tiled=True)])]

    def first_hop(block, parity):
        route = [(f, size + f) for f in range(parity, size, 2)]
        return lax.ppermute(block, ("section", "fsdp"), route)

    early, mark = layer(0, flags, masked_in, 0, [], up, starts, full_k, taps)
    token = lax.ppermute(mark, "fsdp", [(i, i + 1) for i in range(0, size, 2)])
    early = first_hop(early, 0)
    tgt = targets(flags, feats_local, w_tgt, 1, token)
    result, mark = layer(late, flags, masked_in, 0, [], up, starts, full_k, taps, (tgt,))
    rising = [early, first_hop(result, 1)]
    picks, mark = lax.optimization_barrier((distractors[:, 0], mark))
    tgt = targets(flags, feats_local, w_tgt, 0, mark, tgt)
    count = picks.shape[2]
    parts = [
        picks if s == 0 else lax.ppermute(picks, "section", [(s, 0)]) for s in range(sections)
    ]

    falling, losses = [], []
    for t in range(1, slots):
        result = None
        if any(m is not None for m in plans[0][t]):
            slot = plans[0][t][0]
            spare = (tgt, *parts) if t == 1 else ()
            result, _ = layer(t, flags, masked_in, slot, rising, up, starts, full_k, taps, spare)
            if t == 1:
                picks = jnp.concatenate(parts, axis=1)
                picks = jnp.pad(picks, ((0, 0), (0, 0), (0, -count % LANES)))
            route = [(s, s + 1) for s in range(top) if plans[0][t][s] is not None]
            if route:
                rising = [lax.ppermute(result, "section", route)]
        if any(m is not None for m in plans[1][t]):
            turning = [] if plans[1][t][top] is None else [result]
            entry = slots + t
            result, _ = layer(
                entry, flags, None, None, turning + falling, down, starts, full_k, taps
            )
            if plans[1][t][0] is not None:
                losses.append(
                    loss_rows(plans[1][t][0], flags, result, w_ctx, tgt, picks, count)
                )
            route = [(s, s - 1) for s in range(1, sections) if plans[1][t][s] is not None]
            if route:
                falling = [lax.ppermute(result, "section", route)]

    loss = jnp.concatenate(losses, axis=0)
    share = frames // sections
    mine = jnp.zeros((micro, share), jnp.float32)
    for s in range(sections):
        cut = loss[:, s * share : (s + 1) * share]
        if s == 0:
            mine = mine + jnp.where(section == 0, cut, 0.0)
        else:
            mine = mine + lax.ppermute(cut, "section", [(0, s)])
    return mine[:, None, :]


def solution(mesh):
    placed = (
        P(None, "fsdp", None, None),
        P(None, "section", "fsdp", None),
        P(None, "section", None, "fsdp"),
        P(),
        P(),
        P(),
        P(None, "fsdp", None),
        P(None, "fsdp", "section", None),
    )
    return jax.shard_map(
        on_device, mesh=mesh, in_specs=placed, out_specs=P(None, "fsdp", "section"), check_vma=False
    )
```

```python
import functools

import jax
import jax.numpy as jnp
from jax import lax
from jax.experimental import pallas as pl
from jax.experimental.pallas import tpu as pltpu
from jax.sharding import PartitionSpec as P

MASK_LEN = 10
LANES = 128
PAD = 16
VMEM_LIMIT = 48 * 1024 * 1024


def sigmoid(v):
    return 0.5 + 0.5 * jnp.tanh(0.5 * v)


def layer_body(entry, taps, kinds, fresh_slot, recvs, spare, base, flags, *refs):
    refs = list(refs)
    fresh = refs.pop(0) if fresh_slot is not None else None
    recv = [refs.pop(0) for _ in range(recvs)]
    sources = [[refs.pop(0) for _ in range(count)] for _, _, count in kinds]
    starts, k_ref = refs.pop(0), refs.pop(0)
    del refs[:spare]
    out_ref, mark_ref, normed, wbuf, glu, w_sem = (refs.pop(0) for _ in range(6))
    x_ref, x_sem = refs if refs else (recv[0], None)
    chunks, width, part = wbuf.shape
    part = part // 2
    frames = x_ref.shape[0]
    subs = part // LANES
    rows = min(128, frames)
    half = taps // 2
    valid = flags[entry, 0]
    turn = flags[entry, 1]

    def weight_copies(kind, source, j, side):
        target, sem = wbuf.at[j, :, pl.ds(side * part, part)], w_sem.at[j]
        cols = pl.ds(pl.multiple_of(side * width + j * part, part), part)
        if kind == "rows":
            return [pltpu.make_async_copy(source[0].at[:, cols], target, sem)]
        copies = []
        for i, piece in enumerate(source):
            size = piece.shape[0]
            place = pl.ds(pl.multiple_of(starts[i], size), size)
            into = wbuf.at[j, place, pl.ds(side * part, part)]
            copies.append(pltpu.make_async_copy(piece.at[:, cols], into, sem))
        return copies

    def start_weights(j):
        def issue(kind, source):
            for side in range(2):
                for copy in weight_copies(kind, source, j, side):
                    copy.start()

        for (which, kind, _), source in zip(kinds, sources):
            if len(kinds) == 1:
                issue(kind, source)
            else:
                pl.when(turn == which)(functools.partial(issue, kind, source))

    def wait_weights(j):
        pltpu.make_async_copy(wbuf.at[j], wbuf.at[j], w_sem.at[j]).wait()

    def project(j, slot):
        both = jnp.dot(normed[...], wbuf[j], preferred_element_type=jnp.float32)
        gated = both[:, :part] * sigmoid(both[:, part:])
        gated = gated.astype(jnp.bfloat16).astype(jnp.float32)
        for sub in range(subs):
            glu[slot, sub, PAD : PAD + frames, :] = gated[:, sub * LANES : (sub + 1) * LANES]

    def mix(j, slot):
        for sub in range(subs):
            first = pl.multiple_of(j * part + sub * LANES, LANES)
            cols = pl.ds(first, LANES)
            scale = k_ref[:, cols]
            for row in range(0, frames, rows):
                height = rows + 2 * PAD
                block = glu[slot, sub, row : row + height, :]
                acc = jnp.zeros((rows, LANES), jnp.float32)
                for low in range(8):
                    span = block if low == 0 else pltpu.roll(block, height - low, 0)
                    for high in range(0, 2 * PAD, 8):
                        tap = high + low - (PAD - half)
                        if 0 <= tap < taps:
                            acc = acc + span[high : high + rows] * scale[tap : tap + 1]
                base = x_ref[row : row + rows, cols].astype(jnp.float32)
                out_ref[row : row + rows, cols] = (base + acc * sigmoid(acc)).astype(jnp.bfloat16)

    @pl.when(valid == 1)
    def _():
        ahead = min(3, chunks)
        if x_sem is not None:
            options = ([] if fresh is None else [fresh.at[fresh_slot]]) + recv
            first = base
            for i, option in enumerate(options):

                @pl.when(flags[entry, 2] == first + i)
                def _(option=option):
                    pltpu.make_async_copy(option, x_ref, x_sem).start()

        for j in range(ahead):
            start_weights(j)
        zeros = jnp.zeros((2, subs, PAD, LANES), jnp.float32)
        glu[:, :, 0:PAD, :] = zeros
        glu[:, :, PAD + frames :, :] = zeros
        if x_sem is not None:
            pltpu.make_async_copy(x_ref, x_ref, x_sem).wait()
        for row in range(0, frames, 64):
            values = x_ref[row : row + 64, :].astype(jnp.float32)
            center = jnp.mean(values, axis=1, keepdims=True)
            moved = values - center
            spread = jnp.mean(moved * moved, axis=1, keepdims=True)
            normed[row : row + 64, :] = (moved * lax.rsqrt(spread + 1e-05)).astype(jnp.bfloat16)
        wait_weights(0)
        project(0, 0)

        @pl.loop(0, chunks - 1)
        def _(j):
            wait_weights(j + 1)

            @pl.when(j + ahead < chunks)
            def _():
                start_weights(j + ahead)

            mix(j, j % 2)
            project(j + 1, (j + 1) % 2)

        mix(chunks - 1, (chunks - 1) % 2)

    mark_ref[...] = jnp.zeros(mark_ref.shape, mark_ref.dtype)


def layer(
    entry, flags, fresh, fresh_slot, recvs, weights, starts, kernels, taps, spare=(), base=0
):
    frames, width = recvs[0].shape if recvs else fresh.shape[1:]
    part = 256
    chunks = width // part
    anywhere = pl.BlockSpec(memory_space=pl.ANY)
    local = pl.BlockSpec(memory_space=pltpu.VMEM)
    smem = pl.BlockSpec(memory_space=pltpu.SMEM)
    select = fresh_slot is not None or len(recvs) > 1
    operands, specs = [flags], [smem]
    if fresh_slot is not None:
        operands.append(fresh)
        specs.append(anywhere)
    operands += recvs
    specs += [anywhere if select else local] * len(recvs)
    for _, _, arrays in weights:
        operands += arrays
        specs += [anywhere] * len(arrays)
    operands += [starts, kernels, *spare]
    specs += [smem, local] + [anywhere] * len(spare)
    scratch = [
        pltpu.VMEM((frames, width), jnp.bfloat16),
        pltpu.VMEM((chunks, width, 2 * part), jnp.bfloat16),
        pltpu.VMEM((2, part // LANES, frames + 2 * PAD, LANES), jnp.float32),
        pltpu.SemaphoreType.DMA((chunks,)),
    ]
    if select:
        scratch += [pltpu.VMEM((frames, width), jnp.bfloat16), pltpu.SemaphoreType.DMA]
    kinds = [(turn, kind, len(arrays)) for turn, kind, arrays in weights]
    return pl.pallas_call(
        functools.partial(
            layer_body, entry, taps, kinds, fresh_slot, len(recvs), len(spare), base
        ),
        in_specs=specs,
        out_specs=[local, local],
        out_shape=[
            jax.ShapeDtypeStruct((frames, width), jnp.bfloat16),
            jax.ShapeDtypeStruct((8, LANES), jnp.float32),
        ],
        scratch_shapes=scratch,
        compiler_params=pltpu.CompilerParams(vmem_limit_bytes=VMEM_LIMIT),
        cost_estimate=pl.CostEstimate(
            flops=4 * frames * width * width, bytes_accessed=4 * width * width, transcendentals=0
        ),
        name="layer",
    )(*operands)


def unit_rows(values):
    return (values * lax.rsqrt(jnp.sum(values * values, axis=-1, keepdims=True) + 1e-06)).astype(
        jnp.bfloat16
    )


def target_body(feats_ref, w_ref, out_ref):
    out_ref[0] = unit_rows(jnp.dot(feats_ref[0], w_ref[...], preferred_element_type=jnp.float32))


def targets(feats, w_tgt):
    micro, frames, width = feats.shape
    wide = w_tgt.shape[1]
    return pl.pallas_call(
        target_body,
        grid=(micro,),
        in_specs=[
            pl.BlockSpec((1, frames, width), lambda i: (i, 0, 0)),
            pl.BlockSpec((width, wide), lambda i: (0, 0)),
        ],
        out_specs=pl.BlockSpec((1, frames, wide), lambda i: (i, 0, 0)),
        out_shape=jax.ShapeDtypeStruct((micro, frames, wide), jnp.bfloat16),
        compiler_params=pltpu.CompilerParams(vmem_limit_bytes=VMEM_LIMIT),
        cost_estimate=pl.CostEstimate(
            flops=2 * feats.size * wide,
            bytes_accessed=2 * (feats.size + w_tgt.size),
            transcendentals=0,
        ),
        name="targets",
    )(feats, w_tgt)


def loss_body(slot, count, flags, x_ref, w_ref, tgt_ref, pick_ref, out_ref):
    frames = x_ref.shape[0]

    @pl.when(flags[0, 3] == 1)
    def _():
        ctx = unit_rows(jnp.dot(x_ref[...], w_ref[...], preferred_element_type=jnp.float32))
        sims = lax.dot_general(
            ctx, tgt_ref[slot], (((1,), (1,)), ((), ())), preferred_element_type=jnp.float32
        )
        row = lax.broadcasted_iota(jnp.int32, sims.shape, 0)
        col = lax.broadcasted_iota(jnp.int32, sims.shape, 1)
        positive = jnp.sum(jnp.where(row == col, sims, 0.0), axis=1, keepdims=True) * 10.0
        picks = pick_ref[slot]
        lane = picks % LANES
        block = picks // LANES
        negative = jnp.zeros(picks.shape, jnp.float32)
        for part in range(frames // LANES):
            found = jnp.take_along_axis(sims[:, part * LANES : (part + 1) * LANES], lane, axis=1)
            negative = jnp.where(block == part, found, negative)
        place = lax.broadcasted_iota(jnp.int32, picks.shape, 1)
        terms = jnp.where(place < count, jnp.exp(negative * 10.0), 0.0)
        total = jnp.exp(positive) + jnp.sum(terms, axis=1, keepdims=True)
        wide = jnp.broadcast_to(jnp.log(total) - positive, (frames, LANES))
        out_ref[...] = wide.T[0:1, :]


def loss_rows(slot, flags, x, w_ctx, tgt, picks, count):
    frames = x.shape[0]
    whole = pl.BlockSpec(memory_space=pltpu.VMEM)
    return pl.pallas_call(
        functools.partial(loss_body, slot, count),
        in_specs=[pl.BlockSpec(memory_space=pltpu.SMEM)] + [whole] * 4,
        out_specs=whole,
        out_shape=jax.ShapeDtypeStruct((1, frames), jnp.float32),
        compiler_params=pltpu.CompilerParams(vmem_limit_bytes=VMEM_LIMIT),
        name="loss",
    )(flags, x, w_ctx, tgt, picks)


def swap(block, axis, mask):
    return lax.ppermute(block, axis, [(i, i ^ mask) for i in range(lax.axis_size(axis))])


def doubled_rows(block, axis):
    me = lax.axis_index(axis)
    size = lax.axis_size(axis)
    if size & (size - 1):
        return lax.all_gather(block, axis, axis=0, tiled=True)
    mask = 1
    while mask < size:
        other = swap(block, axis, mask)
        upper = (me & mask) != 0
        block = jnp.concatenate(
            [jnp.where(upper, other, block), jnp.where(upper, block, other)], axis=0
        )
        mask *= 2
    return block


def crossed(block, axis):
    size = lax.axis_size(axis)
    me = lax.axis_index(axis)
    odd = me % 2
    ahead = [(i, i ^ (2 if i % 2 else 4)) for i in range(size)]
    other = [(i, i ^ (4 if i % 2 else 2)) for i in range(size)]
    near = lax.ppermute(block, axis, ahead)
    block, near = lax.optimization_barrier((block, near))
    far = lax.ppermute(near, axis, other)
    side = lax.ppermute(block, axis, other)
    first, second = 4 - 2 * odd, 2 + 2 * odd
    pieces = [block, near, side, far]
    masks = [0, first, second, 6]
    pieces += [swap(piece, axis, 1) for piece in pieces]
    masks += [1, second ^ 1, first ^ 1, 7]
    starts = jnp.stack([(me ^ mask) * block.shape[0] for mask in masks]).astype(jnp.int32)
    return pieces, starts, near


def on_device(feats, w_in, dw_kernel, mask_embed, w_ctx, w_tgt, mask_starts, distractors):
    sections = lax.axis_size("section")
    section = lax.axis_index("section")
    size = lax.axis_size("fsdp")
    odd = lax.axis_index("fsdp") % 2
    micro = feats.shape[0]
    frames = feats.shape[2]
    top = sections - 1
    feats_local = feats[:, 0]
    assert w_in.shape[0] == 2

    def mirrored(block):
        return lax.ppermute(block, "section", [(s, top - s) for s in range(sections)])

    slots = micro + 2 * top
    plans = [
        [[t - s if 0 <= t - s < micro else None for s in range(sections)] for t in range(slots)],
        [
            [m if 0 <= m < micro else None for m in (t - 2 * top + s for s in range(sections))]
            for t in range(slots)
        ],
    ]
    table = []
    for s in range(sections):
        rows = []
        for turn in range(2):
            for t in range(slots):
                rows.append([int(plans[turn][t][s] is not None), turn, 1, int(s == 0)])
                if s == (0, top)[turn]:
                    rows[-1][2] = 0
        table.append(rows + rows[:1])
    late = 2 * slots
    flags = lax.dynamic_index_in_dim(jnp.array(table, jnp.int32), section, 0, keepdims=False)
    lanes = lax.broadcasted_iota(jnp.int32, flags.shape, 1)
    entries = lax.broadcasted_iota(jnp.int32, flags.shape, 0)
    off = (lanes == 0) & (((entries == 0) & (odd == 1)) | ((entries == late) & (odd == 0)))
    flags = jnp.where(off, 0, flags)
    flags = jnp.where((entries == 1) & (lanes == 2) & (flags == 1), 1 + odd, flags)

    if size == 8:
        pieces, starts, near = crossed(w_in[0, 0], "fsdp")
        kind = "pieces"
        feats_late, dw, near = lax.optimization_barrier((feats_local, dw_kernel, near))
        pieces[1] = near
    else:
        pieces = [lax.all_gather(w_in[0, 0], "fsdp", axis=0, tiled=True)]
        starts = jnp.zeros((1,), jnp.int32)
        kind = "rows"
        feats_late, dw = feats_local, dw_kernel
    moved = mirrored(w_in[1, 0])
    tgt = targets(feats_late, w_tgt)

    taps = dw.shape[2]
    own = jnp.pad(dw[:, 0], ((0, 0), (0, -taps % 8), (0, 0)))
    own = jnp.transpose(own, (2, 0, 1)).reshape(own.shape[2], -1)
    full_k = doubled_rows(own, "fsdp").reshape(feats.shape[3], 2, -1)
    full_k = jnp.transpose(full_k, (1, 2, 0))

    spots = jnp.arange(frames, dtype=jnp.int32)
    begins = mask_starts[:, 0][:, :, None]
    covered = jnp.any(
        (spots[None, None, :] >= begins) & (spots[None, None, :] < begins + MASK_LEN), axis=1
    )
    masked_in = jnp.where(covered[:, :, None], mask_embed[None, None, :], feats_local)

    beside = (full_k, masked_in, flags, starts, moved, tgt)
    pieces, beside = lax.optimization_barrier((pieces, beside))
    full_k, masked_in, flags, starts, moved, tgt = beside
    k_up = full_k[0].astype(jnp.float32)
    k_down = mirrored(full_k[1]).astype(jnp.float32)
    up = [(0, kind, pieces)]
    down = [(1, "rows", [lax.all_gather(moved, "fsdp", axis=0, tiled=True)])]

    def first_hop(block, parity):
        route = [(f, size + f) for f in range(parity, size, 2)]
        return lax.ppermute(block, ("section", "fsdp"), route)

    early, mark = layer(0, flags, masked_in, 0, [], up, starts, k_up, taps)
    token = lax.ppermute(mark, "fsdp", [(i, i + 1) for i in range(0, size, 2)])
    early = first_hop(early, 0)
    result, mark = layer(late, flags, masked_in, 0, [], up, starts, k_up, taps, (token,))
    rising = [early, first_hop(result, 1)]
    picks, mark = lax.optimization_barrier((distractors[:, 0], mark))
    count = picks.shape[2]
    parts = [
        picks if s == 0 else lax.ppermute(picks, "section", [(s, 0)]) for s in range(sections)
    ]

    falling, losses = [], []
    for t in range(1, slots):
        result = None
        if any(m is not None for m in plans[0][t]):
            slot = plans[0][t][0]
            spare = (mark, *parts) if t == 1 else ()
            result, _ = layer(t, flags, masked_in, slot, rising, up, starts, k_up, taps, spare)
            if t == 1:
                picks = jnp.concatenate(parts, axis=1)
                picks = jnp.pad(picks, ((0, 0), (0, 0), (0, -count % LANES)))
            route = [(s, s + 1) for s in range(top) if plans[0][t][s] is not None]
            if route:
                rising = [lax.ppermute(result, "section", route)]
        if any(m is not None for m in plans[1][t]):
            turning = [] if plans[1][t][top] is None else [result]
            entry = slots + t
            result, _ = layer(
                entry, flags, None, None, turning + falling, down, starts, k_down, taps
            )
            if plans[1][t][0] is not None:
                losses.append(
                    loss_rows(plans[1][t][0], flags, result, w_ctx, tgt, picks, count)
                )
            route = [(s, s - 1) for s in range(1, sections) if plans[1][t][s] is not None]
            if route:
                falling = [lax.ppermute(result, "section", route)]

    loss = jnp.concatenate(losses, axis=0)
    share = frames // sections
    mine = jnp.zeros((micro, share), jnp.float32)
    for s in range(sections):
        cut = loss[:, s * share : (s + 1) * share]
        if s == 0:
            mine = mine + jnp.where(section == 0, cut, 0.0)
        else:
            mine = mine + lax.ppermute(cut, "section", [(0, s)])
    return mine[:, None, :]


def solution(mesh):
    placed = (
        P(None, "fsdp", None, None),
        P(None, "section", "fsdp", None),
        P(None, "section", None, "fsdp"),
        P(),
        P(),
        P(),
        P(None, "fsdp", None),
        P(None, "fsdp", "section", None),
    )
    return jax.shard_map(
        on_device, mesh=mesh, in_specs=placed, out_specs=P(None, "fsdp", "section"), check_vma=False
    )
```

```python
import functools

import jax
import jax.numpy as jnp
import ml_dtypes
import numpy as np
from jax import lax
from jax.experimental import pallas as pl
from jax.experimental.pallas import tpu as pltpu
from jax.sharding import PartitionSpec as P

MASK_LEN = 10
LANES = 128
PAD = 16
VMEM_LIMIT = 48 * 1024 * 1024


BLOCK = 128
WINDOW = BLOCK + 2 * PAD
HALF = WINDOW // 2


def transforms(taps):
    freq = np.arange(HALF)[:, None] * (2 * np.pi / WINDOW)
    spot = np.arange(WINDOW)[None, :]
    forward = np.concatenate([np.cos(freq * spot), -np.sin(freq * spot)])
    forward[HALF] = (-1.0) ** np.arange(WINDOW)
    inverse = forward[:, :BLOCK].T
    at = np.arange(taps)[None, :] + PAD - taps // 2
    scale = np.full((HALF, 1), 2.0 / WINDOW)
    scale[0] = 1.0 / WINDOW
    real, imag = np.cos(freq * at) * scale, np.sin(freq * at) * scale
    last = real.copy()
    last[0] = (-1.0) ** at[0] / WINDOW
    return forward, inverse, np.concatenate([real, imag, last])


def sigmoid(v):
    return 0.5 + 0.5 * jnp.tanh(0.5 * v)


def layer_body(entry, kinds, fresh_slot, recvs, spare, base, flags, *refs):
    refs = list(refs)
    fresh = refs.pop(0) if fresh_slot is not None else None
    recv = [refs.pop(0) for _ in range(recvs)]
    sources = [[refs.pop(0) for _ in range(count)] for _, _, count in kinds]
    starts, k_ref, forward, inverse = (refs.pop(0) for _ in range(4))
    del refs[:spare]
    out_ref, mark_ref, normed, wbuf, glu, w_sem = (refs.pop(0) for _ in range(6))
    x_ref, x_sem = refs if refs else (recv[0], None)
    chunks, width, part = wbuf.shape
    part = part // 2
    frames = x_ref.shape[0]
    valid = flags[entry, 0]
    turn = flags[entry, 1]

    def weight_copies(kind, source, j, side):
        target, sem = wbuf.at[j, :, pl.ds(side * part, part)], w_sem.at[j]
        cols = pl.ds(pl.multiple_of(side * width + j * part, part), part)
        if kind == "rows":
            return [pltpu.make_async_copy(source[0].at[:, cols], target, sem)]
        copies = []
        for i, piece in enumerate(source):
            size = piece.shape[0]
            place = pl.ds(pl.multiple_of(starts[i], size), size)
            into = wbuf.at[j, place, pl.ds(side * part, part)]
            copies.append(pltpu.make_async_copy(piece.at[:, cols], into, sem))
        return copies

    def start_weights(j):
        def issue(kind, source):
            for side in range(2):
                for copy in weight_copies(kind, source, j, side):
                    copy.start()

        for (which, kind, _), source in zip(kinds, sources):
            if len(kinds) == 1:
                issue(kind, source)
            else:
                pl.when(turn == which)(functools.partial(issue, kind, source))

    def wait_weights(j):
        pltpu.make_async_copy(wbuf.at[j], wbuf.at[j], w_sem.at[j]).wait()

    def project(j, slot):
        both = jnp.dot(normed[...], wbuf[j], preferred_element_type=jnp.float32)
        gated = both[:, :part] * sigmoid(both[:, part:])
        glu[slot, PAD : PAD + frames, :] = gated.astype(jnp.bfloat16)

    def mix(j, slot):
        cols = pl.ds(pl.multiple_of(j * part, part), part)
        real, imag, last = (k_ref[HALF * i : HALF * (i + 1), cols] for i in range(3))
        for row in range(0, frames, BLOCK):
            window = glu[slot, row : row + WINDOW, :]
            freq = jnp.dot(forward[...], window, preferred_element_type=jnp.float32)
            up, low = freq[:HALF], freq[HALF:]
            freq = jnp.concatenate([up * real - low * imag, up * imag + low * last], axis=0)
            conv = jnp.dot(
                inverse[...], freq.astype(jnp.bfloat16), preferred_element_type=jnp.float32
            )
            base = x_ref[row : row + BLOCK, cols].astype(jnp.float32)
            out_ref[row : row + BLOCK, cols] = (base + conv * sigmoid(conv)).astype(jnp.bfloat16)

    @pl.when(valid == 1)
    def _():
        ahead = min(3, chunks)
        if x_sem is not None:
            options = ([] if fresh is None else [fresh.at[fresh_slot]]) + recv
            first = base
            for i, option in enumerate(options):

                @pl.when(flags[entry, 2] == first + i)
                def _(option=option):
                    pltpu.make_async_copy(option, x_ref, x_sem).start()

        for j in range(ahead):
            start_weights(j)
        zeros = jnp.zeros((2, PAD, part), jnp.bfloat16)
        glu[:, 0:PAD, :] = zeros
        glu[:, PAD + frames :, :] = zeros
        if x_sem is not None:
            pltpu.make_async_copy(x_ref, x_ref, x_sem).wait()
        for row in range(0, frames, 64):
            values = x_ref[row : row + 64, :].astype(jnp.float32)
            center = jnp.mean(values, axis=1, keepdims=True)
            moved = values - center
            spread = jnp.mean(moved * moved, axis=1, keepdims=True)
            normed[row : row + 64, :] = (moved * lax.rsqrt(spread + 1e-05)).astype(jnp.bfloat16)
        wait_weights(0)
        project(0, 0)

        @pl.loop(0, chunks - 1)
        def _(j):
            wait_weights(j + 1)

            @pl.when(j + ahead < chunks)
            def _():
                start_weights(j + ahead)

            mix(j, j % 2)
            project(j + 1, (j + 1) % 2)

        mix(chunks - 1, (chunks - 1) % 2)

    mark_ref[...] = jnp.zeros(mark_ref.shape, mark_ref.dtype)


def layer(
    entry, flags, fresh, fresh_slot, recvs, weights, starts, kernels, matrices, spare=(), base=0
):
    frames, width = recvs[0].shape if recvs else fresh.shape[1:]
    part = 256
    chunks = width // part
    anywhere = pl.BlockSpec(memory_space=pl.ANY)
    local = pl.BlockSpec(memory_space=pltpu.VMEM)
    smem = pl.BlockSpec(memory_space=pltpu.SMEM)
    select = fresh_slot is not None or len(recvs) > 1
    operands, specs = [flags], [smem]
    if fresh_slot is not None:
        operands.append(fresh)
        specs.append(anywhere)
    operands += recvs
    specs += [anywhere if select else local] * len(recvs)
    for _, _, arrays in weights:
        operands += arrays
        specs += [anywhere] * len(arrays)
    operands += [starts, kernels, *matrices, *spare]
    specs += [smem, local, local, local] + [anywhere] * len(spare)
    scratch = [
        pltpu.VMEM((frames, width), jnp.bfloat16),
        pltpu.VMEM((chunks, width, 2 * part), jnp.bfloat16),
        pltpu.VMEM((2, frames + 2 * PAD, part), jnp.bfloat16),
        pltpu.SemaphoreType.DMA((chunks,)),
    ]
    if select:
        scratch += [pltpu.VMEM((frames, width), jnp.bfloat16), pltpu.SemaphoreType.DMA]
    kinds = [(turn, kind, len(arrays)) for turn, kind, arrays in weights]
    return pl.pallas_call(
        functools.partial(
            layer_body, entry, kinds, fresh_slot, len(recvs), len(spare), base
        ),
        in_specs=specs,
        out_specs=[local, local],
        out_shape=[
            jax.ShapeDtypeStruct((frames, width), jnp.bfloat16),
            jax.ShapeDtypeStruct((8, LANES), jnp.float32),
        ],
        scratch_shapes=scratch,
        compiler_params=pltpu.CompilerParams(vmem_limit_bytes=VMEM_LIMIT),
        cost_estimate=pl.CostEstimate(
            flops=4 * frames * width * width, bytes_accessed=4 * width * width, transcendentals=0
        ),
        name="layer",
    )(*operands)


def transform_body(m_ref, k_ref, out_ref):
    total = jnp.dot(m_ref[0], k_ref[...], preferred_element_type=jnp.float32)
    for part in range(1, m_ref.shape[0]):
        total = total + jnp.dot(m_ref[part], k_ref[...], preferred_element_type=jnp.float32)
    out_ref[...] = total


def transformed(matrix, kernel):
    return pl.pallas_call(
        transform_body,
        out_shape=jax.ShapeDtypeStruct((matrix.shape[1], kernel.shape[1]), jnp.float32),
        compiler_params=pltpu.CompilerParams(vmem_limit_bytes=VMEM_LIMIT),
        name="transformed",
    )(matrix, kernel)


def unit_rows(values):
    return (values * lax.rsqrt(jnp.sum(values * values, axis=-1, keepdims=True) + 1e-06)).astype(
        jnp.bfloat16
    )


def target_body(feats_ref, w_ref, out_ref):
    out_ref[0] = unit_rows(jnp.dot(feats_ref[0], w_ref[...], preferred_element_type=jnp.float32))


def targets(feats, w_tgt):
    micro, frames, width = feats.shape
    wide = w_tgt.shape[1]
    return pl.pallas_call(
        target_body,
        grid=(micro,),
        in_specs=[
            pl.BlockSpec((1, frames, width), lambda i: (i, 0, 0)),
            pl.BlockSpec((width, wide), lambda i: (0, 0)),
        ],
        out_specs=pl.BlockSpec((1, frames, wide), lambda i: (i, 0, 0)),
        out_shape=jax.ShapeDtypeStruct((micro, frames, wide), jnp.bfloat16),
        compiler_params=pltpu.CompilerParams(vmem_limit_bytes=VMEM_LIMIT),
        cost_estimate=pl.CostEstimate(
            flops=2 * feats.size * wide,
            bytes_accessed=2 * (feats.size + w_tgt.size),
            transcendentals=0,
        ),
        name="targets",
    )(feats, w_tgt)


def loss_body(slot, count, flags, x_ref, w_ref, tgt_ref, pick_ref, out_ref):
    frames = x_ref.shape[0]

    @pl.when(flags[0, 3] == 1)
    def _():
        ctx = unit_rows(jnp.dot(x_ref[...], w_ref[...], preferred_element_type=jnp.float32))
        sims = lax.dot_general(
            ctx, tgt_ref[slot], (((1,), (1,)), ((), ())), preferred_element_type=jnp.float32
        )
        row = lax.broadcasted_iota(jnp.int32, sims.shape, 0)
        col = lax.broadcasted_iota(jnp.int32, sims.shape, 1)
        positive = jnp.sum(jnp.where(row == col, sims, 0.0), axis=1, keepdims=True) * 10.0
        picks = pick_ref[slot]
        lane = picks % LANES
        block = picks // LANES
        negative = jnp.zeros(picks.shape, jnp.float32)
        for part in range(frames // LANES):
            found = jnp.take_along_axis(sims[:, part * LANES : (part + 1) * LANES], lane, axis=1)
            negative = jnp.where(block == part, found, negative)
        place = lax.broadcasted_iota(jnp.int32, picks.shape, 1)
        terms = jnp.where(place < count, jnp.exp(negative * 10.0), 0.0)
        total = jnp.exp(positive) + jnp.sum(terms, axis=1, keepdims=True)
        wide = jnp.broadcast_to(jnp.log(total) - positive, (frames, LANES))
        out_ref[...] = wide.T[0:1, :]


def loss_rows(slot, flags, x, w_ctx, tgt, picks, count):
    frames = x.shape[0]
    whole = pl.BlockSpec(memory_space=pltpu.VMEM)
    return pl.pallas_call(
        functools.partial(loss_body, slot, count),
        in_specs=[pl.BlockSpec(memory_space=pltpu.SMEM)] + [whole] * 4,
        out_specs=whole,
        out_shape=jax.ShapeDtypeStruct((1, frames), jnp.float32),
        compiler_params=pltpu.CompilerParams(vmem_limit_bytes=VMEM_LIMIT),
        name="loss",
    )(flags, x, w_ctx, tgt, picks)


def swap(block, axis, mask):
    return lax.ppermute(block, axis, [(i, i ^ mask) for i in range(lax.axis_size(axis))])


def doubled_rows(block, axis):
    me = lax.axis_index(axis)
    size = lax.axis_size(axis)
    if size & (size - 1):
        return lax.all_gather(block, axis, axis=0, tiled=True)
    mask = 1
    while mask < size:
        other = swap(block, axis, mask)
        upper = (me & mask) != 0
        block = jnp.concatenate(
            [jnp.where(upper, other, block), jnp.where(upper, block, other)], axis=0
        )
        mask *= 2
    return block


def crossed(block, axis, beside):
    size = lax.axis_size(axis)
    me = lax.axis_index(axis)
    odd = me % 2
    ahead = [(i, i ^ (2 if i % 2 else 4)) for i in range(size)]
    other = [(i, i ^ (4 if i % 2 else 2)) for i in range(size)]
    near = lax.ppermute(block, axis, ahead)
    block, near, beside = lax.optimization_barrier((block, near, beside))
    far = lax.ppermute(near, axis, other)
    side = lax.ppermute(block, axis, other)
    first, second = 4 - 2 * odd, 2 + 2 * odd
    pieces = [block, near, side, far]
    masks = [0, first, second, 6]
    pieces += [swap(piece, axis, 1) for piece in pieces]
    masks += [1, second ^ 1, first ^ 1, 7]
    starts = jnp.stack([(me ^ mask) * block.shape[0] for mask in masks]).astype(jnp.int32)
    return pieces, starts, near, beside


def on_device(feats, w_in, dw_kernel, mask_embed, w_ctx, w_tgt, mask_starts, distractors):
    sections = lax.axis_size("section")
    section = lax.axis_index("section")
    size = lax.axis_size("fsdp")
    odd = lax.axis_index("fsdp") % 2
    micro = feats.shape[0]
    frames = feats.shape[2]
    top = sections - 1
    feats_local = feats[:, 0]
    assert w_in.shape[0] == 2

    def mirrored(block):
        return lax.ppermute(block, "section", [(s, top - s) for s in range(sections)])

    slots = micro + 2 * top
    plans = [
        [[t - s if 0 <= t - s < micro else None for s in range(sections)] for t in range(slots)],
        [
            [m if 0 <= m < micro else None for m in (t - 2 * top + s for s in range(sections))]
            for t in range(slots)
        ],
    ]
    table = []
    for s in range(sections):
        rows = []
        for turn in range(2):
            for t in range(slots):
                rows.append([int(plans[turn][t][s] is not None), turn, 1, int(s == 0)])
                if s == (0, top)[turn]:
                    rows[-1][2] = 0
        table.append(rows + rows[:1])
    late = 2 * slots
    flags = lax.dynamic_index_in_dim(jnp.array(table, jnp.int32), section, 0, keepdims=False)
    lanes = lax.broadcasted_iota(jnp.int32, flags.shape, 1)
    entries = lax.broadcasted_iota(jnp.int32, flags.shape, 0)
    off = (lanes == 0) & (((entries == 0) & (odd == 1)) | ((entries == late) & (odd == 0)))
    flags = jnp.where(off, 0, flags)
    flags = jnp.where((entries == 1) & (lanes == 2) & (flags == 1), 1 + odd, flags)

    spots = jnp.arange(frames, dtype=jnp.int32)
    begins = mask_starts[:, 0][:, :, None]
    covered = jnp.any(
        (spots[None, None, :] >= begins) & (spots[None, None, :] < begins + MASK_LEN), axis=1
    )
    masked_in = jnp.where(covered[:, :, None], mask_embed[None, None, :], feats_local)

    if size == 8:
        pieces, starts, near, masked_in = crossed(w_in[0, 0], "fsdp", masked_in)
        kind = "pieces"
        dw, near = lax.optimization_barrier((dw_kernel, near))
        pieces[1] = near
    else:
        pieces = [lax.all_gather(w_in[0, 0], "fsdp", axis=0, tiled=True)]
        starts = jnp.zeros((1,), jnp.int32)
        kind = "rows"
        dw = dw_kernel
    moved = mirrored(w_in[1, 0])

    taps = dw.shape[2]
    own = jnp.pad(dw[:, 0], ((0, 0), (0, -taps % 8), (0, 0)))
    own = jnp.transpose(own, (2, 0, 1)).reshape(own.shape[2], -1)
    full_k = doubled_rows(own, "fsdp").reshape(feats.shape[3], 2, -1)
    full_k = jnp.transpose(full_k, (1, 2, 0))
    forward, inverse, of_taps = transforms(taps)
    rest = np.pad(of_taps, ((0, 0), (0, -taps % 8)))
    of_taps = []
    for _ in range(3):
        of_taps.append(rest.astype(ml_dtypes.bfloat16))
        rest = rest - of_taps[-1].astype(np.float64)
    of_taps = jnp.asarray(np.stack(of_taps))
    mats = (jnp.asarray(forward, jnp.bfloat16), jnp.asarray(inverse, jnp.bfloat16))

    beside = (transformed(of_taps, full_k[0]), full_k[1], masked_in, flags, starts, moved, mats)
    pieces, beside = lax.optimization_barrier((pieces, beside))
    k_up, k_down, masked_in, flags, starts, moved, mats = beside
    up = [(0, kind, pieces)]
    down = [(1, "rows", [lax.all_gather(moved, "fsdp", axis=0, tiled=True)])]

    def first_hop(block, parity):
        route = [(f, size + f) for f in range(parity, size, 2)]
        return lax.ppermute(block, ("section", "fsdp"), route)

    early, mark = layer(0, flags, masked_in, 0, [], up, starts, k_up, mats)
    token = lax.ppermute(mark, "fsdp", [(i, i + 1) for i in range(0, size, 2)])
    early = first_hop(early, 0)
    result, mark = layer(late, flags, masked_in, 0, [], up, starts, k_up, mats, (token,))
    rising = [early, first_hop(result, 1)]
    falling, losses, parts, spare = [], [], [distractors[:, 0]], (mark,)
    for t in range(1, slots):
        result = None
        if any(m is not None for m in plans[0][t]):
            if t < sections:
                late_picks, mark = lax.optimization_barrier((distractors[:, 0], mark))
                parts.append(lax.ppermute(late_picks, "section", [(t, 0)]))
                spare = (mark, parts[-1])
            if t == 1:
                k_down, mark = lax.optimization_barrier((k_down, mark))
                k_down = transformed(of_taps, mirrored(k_down))
            if t == 2:
                late_feats, mark = lax.optimization_barrier((feats_local, mark))
                tgt = targets(late_feats, w_tgt)
                spare += (k_down, tgt)
            slot = plans[0][t][0]
            result, mark = layer(
                t, flags, masked_in, slot, rising, up, starts, k_up, mats, spare
            )
            spare = ()
            if len(parts) == sections and t + 1 == sections:
                picks = jnp.concatenate(parts, axis=1)
                count = picks.shape[2]
                picks = jnp.pad(picks, ((0, 0), (0, 0), (0, -count % LANES)))
            route = [(s, s + 1) for s in range(top) if plans[0][t][s] is not None]
            if route:
                rising = [lax.ppermute(result, "section", route)]
        if any(m is not None for m in plans[1][t]):
            turning = [] if plans[1][t][top] is None else [result]
            entry = slots + t
            result, _ = layer(
                entry, flags, None, None, turning + falling, down, starts, k_down, mats
            )
            if plans[1][t][0] is not None:
                losses.append(
                    loss_rows(plans[1][t][0], flags, result, w_ctx, tgt, picks, count)
                )
            route = [(s, s - 1) for s in range(1, sections) if plans[1][t][s] is not None]
            if route:
                falling = [lax.ppermute(result, "section", route)]

    loss = jnp.concatenate(losses, axis=0)
    share = frames // sections
    mine = jnp.zeros((micro, share), jnp.float32)
    for s in range(sections):
        cut = loss[:, s * share : (s + 1) * share]
        if s == 0:
            mine = mine + jnp.where(section == 0, cut, 0.0)
        else:
            mine = mine + lax.ppermute(cut, "section", [(0, s)])
    return mine[:, None, :]


def solution(mesh):
    placed = (
        P(None, "fsdp", None, None),
        P(None, "section", "fsdp", None),
        P(None, "section", None, "fsdp"),
        P(),
        P(),
        P(),
        P(None, "fsdp", None),
        P(None, "fsdp", "section", None),
    )
    return jax.shard_map(
        on_device, mesh=mesh, in_specs=placed, out_specs=P(None, "fsdp", "section"), check_vma=False
    )
```

```python
import functools

import jax
import jax.numpy as jnp
import ml_dtypes
import numpy as np
from jax import lax
from jax.experimental import pallas as pl
from jax.experimental.pallas import tpu as pltpu
from jax.sharding import PartitionSpec as P

MASK_LEN = 10
LANES = 128
PAD = 16
VMEM_LIMIT = 32 * 1024 * 1024


BLOCK = 128
WINDOW = BLOCK + 2 * PAD
HALF = WINDOW // 2


def transforms(taps):
    freq = np.arange(HALF)[:, None] * (2 * np.pi / WINDOW)
    spot = np.arange(WINDOW)[None, :]
    forward = np.concatenate([np.cos(freq * spot), -np.sin(freq * spot)])
    forward[HALF] = (-1.0) ** np.arange(WINDOW)
    inverse = forward[:, :BLOCK].T
    at = np.arange(taps)[None, :] + PAD - taps // 2
    scale = np.full((HALF, 1), 2.0 / WINDOW)
    scale[0] = 1.0 / WINDOW
    real, imag = np.cos(freq * at) * scale, np.sin(freq * at) * scale
    last = real.copy()
    last[0] = (-1.0) ** at[0] / WINDOW
    return forward, inverse, np.concatenate([real, imag, last])


def sigmoid(v):
    return 0.5 + 0.5 * jnp.tanh(0.5 * v)


def layer_body(entry, turns, fresh_slot, recvs, pieced, spare, flags, *refs):
    refs = list(refs)
    fresh = refs.pop(0) if fresh_slot is not None else None
    recv = [refs.pop(0) for _ in range(recvs)]
    pieces = [refs.pop(0) for _ in range(pieced)]
    starts = refs.pop(0) if pieced else None
    weights = [] if pieced else [refs.pop(0) for _ in turns]
    kernels = [refs.pop(0) for _ in turns]
    forward, inverse = refs.pop(0), refs.pop(0)
    del refs[:spare]
    out_ref, mark_ref = refs.pop(0), refs.pop(0)
    if pieced:
        weights = [refs.pop(0)]
    normed, glu = refs.pop(0), refs.pop(0)
    w_sem = refs.pop(0) if pieced else None
    x_ref, x_sem = refs if refs else (recv[0], None)
    frames, width = x_ref.shape
    part = glu.shape[2]
    chunks = width // part
    valid = flags[entry, 0]
    turn = flags[entry, 1]

    def column(j, side):
        return pl.ds(pl.multiple_of(side * width + j * part, part), part)

    def wait_weights(j):
        if pieced:
            for side in range(2):
                block = weights[0].at[:, column(j, side)]
                pltpu.make_async_copy(block, block, w_sem.at[j, side]).wait()

    def project(w_ref, j, slot):
        values = jnp.dot(normed[...], w_ref[:, column(j, 0)], preferred_element_type=jnp.float32)
        gates = jnp.dot(normed[...], w_ref[:, column(j, 1)], preferred_element_type=jnp.float32)
        glu[slot, PAD : PAD + frames, :] = (values * sigmoid(gates)).astype(jnp.bfloat16)

    def mix(k_ref, j, slot):
        cols = column(j, 0)
        real, imag, last = (k_ref[HALF * i : HALF * (i + 1), cols] for i in range(3))
        for row in range(0, frames, BLOCK):
            window = glu[slot, row : row + WINDOW, :]
            freq = jnp.dot(forward[...], window, preferred_element_type=jnp.float32)
            up, low = freq[:HALF], freq[HALF:]
            freq = jnp.concatenate([up * real - low * imag, up * imag + low * last], axis=0)
            conv = jnp.dot(
                inverse[...], freq.astype(jnp.bfloat16), preferred_element_type=jnp.float32
            )
            base = x_ref[row : row + BLOCK, cols].astype(jnp.float32)
            out_ref[row : row + BLOCK, cols] = (base + conv * sigmoid(conv)).astype(jnp.bfloat16)

    def compute(w_ref, k_ref):
        wait_weights(0)
        project(w_ref, 0, 0)

        @pl.loop(0, chunks - 1)
        def _(j):
            wait_weights(j + 1)
            mix(k_ref, j, j % 2)
            project(w_ref, j + 1, (j + 1) % 2)

        mix(k_ref, chunks - 1, (chunks - 1) % 2)

    @pl.when(valid == 1)
    def _():
        if x_sem is not None:
            options = ([] if fresh is None else [fresh.at[fresh_slot]]) + recv
            first = 0 if fresh is not None else 1
            for i, option in enumerate(options):

                @pl.when(flags[entry, 2] == first + i)
                def _(option=option):
                    pltpu.make_async_copy(option, x_ref, x_sem).start()

    for j in range(chunks if pieced else 0):
        for side in range(2):
            for i, piece in enumerate(pieces):
                size = piece.shape[0]
                rows = pl.ds(pl.multiple_of(starts[i], size), size)
                pltpu.make_async_copy(
                    piece.at[:, column(j, side)],
                    weights[0].at[rows, column(j, side)],
                    w_sem.at[j, side],
                ).start()

    @pl.when(valid == 1)
    def _():
        zeros = jnp.zeros((2, PAD, part), jnp.bfloat16)
        glu[:, 0:PAD, :] = zeros
        glu[:, PAD + frames :, :] = zeros
        if x_sem is not None:
            pltpu.make_async_copy(x_ref, x_ref, x_sem).wait()
        for row in range(0, frames, 64):
            values = x_ref[row : row + 64, :].astype(jnp.float32)
            center = jnp.mean(values, axis=1, keepdims=True)
            moved = values - center
            spread = jnp.mean(moved * moved, axis=1, keepdims=True)
            normed[row : row + 64, :] = (moved * lax.rsqrt(spread + 1e-05)).astype(jnp.bfloat16)
        for which, w_ref, k_ref in zip(turns, weights, kernels):
            if len(turns) == 1:
                compute(w_ref, k_ref)
            else:
                pl.when(turn == which)(functools.partial(compute, w_ref, k_ref))

    if pieced:

        @pl.when(valid == 0)
        def _():
            for j in range(chunks):
                wait_weights(j)

    mark_ref[...] = jnp.zeros(mark_ref.shape, mark_ref.dtype)


def layer(entry, turns, flags, fresh, fresh_slot, recvs, weights, kernels, matrices, spare=(), starts=None):
    frames, width = recvs[0].shape if recvs else fresh.shape[1:]
    part = 256
    chunks = width // part
    anywhere = pl.BlockSpec(memory_space=pl.ANY)
    local = pl.BlockSpec(memory_space=pltpu.VMEM)
    smem = pl.BlockSpec(memory_space=pltpu.SMEM)
    select = fresh_slot is not None or len(recvs) > 1
    operands, specs = [flags], [smem]
    if fresh_slot is not None:
        operands.append(fresh)
        specs.append(anywhere)
    operands += recvs
    specs += [anywhere if select else local] * len(recvs)
    operands += weights
    specs += [local if starts is None else anywhere] * len(weights)
    if starts is not None:
        operands.append(starts)
        specs.append(smem)
    operands += [*kernels, *matrices, *spare]
    specs += [local] * (len(kernels) + len(matrices)) + [anywhere] * len(spare)
    out_shape = [
        jax.ShapeDtypeStruct((frames, width), jnp.bfloat16),
        jax.ShapeDtypeStruct((8, LANES), jnp.float32),
    ]
    scratch = [
        pltpu.VMEM((frames, width), jnp.bfloat16),
        pltpu.VMEM((2, frames + 2 * PAD, part), jnp.bfloat16),
    ]
    if starts is not None:
        out_shape.append(jax.ShapeDtypeStruct((width, 2 * width), jnp.bfloat16))
        scratch.append(pltpu.SemaphoreType.DMA((chunks, 2)))
    if select:
        scratch += [pltpu.VMEM((frames, width), jnp.bfloat16), pltpu.SemaphoreType.DMA]
    pieced = 0 if starts is None else len(weights)
    return pl.pallas_call(
        functools.partial(
            layer_body, entry, turns, fresh_slot, len(recvs), pieced, len(spare)
        ),
        in_specs=specs,
        out_specs=[local] * len(out_shape),
        out_shape=out_shape,
        scratch_shapes=scratch,
        compiler_params=pltpu.CompilerParams(vmem_limit_bytes=VMEM_LIMIT),
        cost_estimate=pl.CostEstimate(
            flops=4 * frames * width * width, bytes_accessed=4 * width * width, transcendentals=0
        ),
        name="layer",
    )(*operands)


def transform_body(m_ref, k_ref, out_ref):
    total = jnp.dot(m_ref[0], k_ref[...], preferred_element_type=jnp.float32)
    for part in range(1, m_ref.shape[0]):
        total = total + jnp.dot(m_ref[part], k_ref[...], preferred_element_type=jnp.float32)
    out_ref[...] = total


def transformed(matrix, kernel):
    return pl.pallas_call(
        transform_body,
        out_shape=jax.ShapeDtypeStruct((matrix.shape[1], kernel.shape[1]), jnp.float32),
        compiler_params=pltpu.CompilerParams(vmem_limit_bytes=VMEM_LIMIT),
        name="transformed",
    )(matrix, kernel)


def unit_rows(values):
    return (values * lax.rsqrt(jnp.sum(values * values, axis=-1, keepdims=True) + 1e-06)).astype(
        jnp.bfloat16
    )


def target_body(wanted, flags, feats, w_tgt, *refs):
    out, feats_ref, w_ref, out_ref, sems = refs[-5:]

    @pl.when(flags[0, 4] == wanted)
    def _():
        load_w = pltpu.make_async_copy(w_tgt, w_ref, sems.at[0])
        load_x = pltpu.make_async_copy(feats, feats_ref, sems.at[1])
        load_w.start()
        load_x.start()
        load_w.wait()
        load_x.wait()

        @pl.loop(0, feats_ref.shape[0])
        def _(slot):
            out_ref[slot] = unit_rows(
                jnp.dot(feats_ref[slot], w_ref[...], preferred_element_type=jnp.float32)
            )

        back = pltpu.make_async_copy(out_ref, out, sems.at[2])
        back.start()
        back.wait()


def targets(flags, feats, w_tgt, wanted, spare, earlier=None):
    operands = [flags, feats, w_tgt, spare] + ([] if earlier is None else [earlier])
    anywhere = pl.BlockSpec(memory_space=pl.ANY)
    shape = feats.shape[:2] + w_tgt.shape[1:]
    return pl.pallas_call(
        functools.partial(target_body, wanted),
        in_specs=[pl.BlockSpec(memory_space=pltpu.SMEM)] + [anywhere] * (len(operands) - 1),
        out_specs=anywhere,
        out_shape=jax.ShapeDtypeStruct(shape, jnp.bfloat16),
        scratch_shapes=[
            pltpu.VMEM(feats.shape, jnp.bfloat16),
            pltpu.VMEM(w_tgt.shape, jnp.bfloat16),
            pltpu.VMEM(shape, jnp.bfloat16),
            pltpu.SemaphoreType.DMA((3,)),
        ],
        input_output_aliases={} if earlier is None else {4: 0},
        compiler_params=pltpu.CompilerParams(vmem_limit_bytes=VMEM_LIMIT),
        cost_estimate=pl.CostEstimate(
            flops=2 * feats.size * w_tgt.shape[1],
            bytes_accessed=2 * (feats.size + w_tgt.size),
            transcendentals=0,
        ),
        name="targets",
    )(*operands)


def loss_body(slot, count, flags, x_ref, w_ref, tgt_ref, pick_ref, out_ref):
    frames = x_ref.shape[0]

    @pl.when(flags[0, 3] == 1)
    def _():
        ctx = unit_rows(jnp.dot(x_ref[...], w_ref[...], preferred_element_type=jnp.float32))
        sims = lax.dot_general(
            ctx, tgt_ref[slot], (((1,), (1,)), ((), ())), preferred_element_type=jnp.float32
        )
        row = lax.broadcasted_iota(jnp.int32, sims.shape, 0)
        col = lax.broadcasted_iota(jnp.int32, sims.shape, 1)
        positive = jnp.sum(jnp.where(row == col, sims, 0.0), axis=1, keepdims=True) * 10.0
        picks = pick_ref[slot]
        lane = picks % LANES
        block = picks // LANES
        negative = jnp.zeros(picks.shape, jnp.float32)
        for part in range(frames // LANES):
            found = jnp.take_along_axis(sims[:, part * LANES : (part + 1) * LANES], lane, axis=1)
            negative = jnp.where(block == part, found, negative)
        place = lax.broadcasted_iota(jnp.int32, picks.shape, 1)
        terms = jnp.where(place < count, jnp.exp(negative * 10.0), 0.0)
        total = jnp.exp(positive) + jnp.sum(terms, axis=1, keepdims=True)
        wide = jnp.broadcast_to(jnp.log(total) - positive, (frames, LANES))
        out_ref[...] = wide.T[0:1, :]


def loss_rows(slot, flags, x, w_ctx, tgt, picks, count):
    frames = x.shape[0]
    whole = pl.BlockSpec(memory_space=pltpu.VMEM)
    return pl.pallas_call(
        functools.partial(loss_body, slot, count),
        in_specs=[pl.BlockSpec(memory_space=pltpu.SMEM)] + [whole] * 4,
        out_specs=whole,
        out_shape=jax.ShapeDtypeStruct((1, frames), jnp.float32),
        compiler_params=pltpu.CompilerParams(vmem_limit_bytes=VMEM_LIMIT),
        name="loss",
    )(flags, x, w_ctx, tgt, picks)


def swap(block, axis, mask):
    return lax.ppermute(block, axis, [(i, i ^ mask) for i in range(lax.axis_size(axis))])


def doubled_rows(block, axis):
    me = lax.axis_index(axis)
    size = lax.axis_size(axis)
    if size & (size - 1):
        return lax.all_gather(block, axis, axis=0, tiled=True)
    mask = 1
    while mask < size:
        other = swap(block, axis, mask)
        upper = (me & mask) != 0
        block = jnp.concatenate(
            [jnp.where(upper, other, block), jnp.where(upper, block, other)], axis=0
        )
        mask *= 2
    return block


def crossed(block, axis):
    size = lax.axis_size(axis)
    me = lax.axis_index(axis)
    odd = me % 2
    ahead = [(i, i ^ (2 if i % 2 else 4)) for i in range(size)]
    other = [(i, i ^ (4 if i % 2 else 2)) for i in range(size)]
    near = lax.ppermute(block, axis, ahead)
    block, near = lax.optimization_barrier((block, near))
    far = lax.ppermute(near, axis, other)
    side = lax.ppermute(block, axis, other)
    first, second = 4 - 2 * odd, 2 + 2 * odd
    pieces = [block, near, side, far]
    masks = [0, first, second, 6]
    pieces += [swap(piece, axis, 1) for piece in pieces]
    masks += [1, second ^ 1, first ^ 1, 7]
    starts = jnp.stack([(me ^ mask) * block.shape[0] for mask in masks]).astype(jnp.int32)
    return pieces, starts, near


def on_device(feats, w_in, dw_kernel, mask_embed, w_ctx, w_tgt, mask_starts, distractors):
    sections = lax.axis_size("section")
    section = lax.axis_index("section")
    micro = feats.shape[0]
    frames = feats.shape[2]
    repeats = w_in.shape[0]
    last = sections - 1
    feats_local = feats[:, 0]

    spots = jnp.arange(frames, dtype=jnp.int32)
    starts = mask_starts[:, 0][:, :, None]
    covered = jnp.any(
        (spots[None, None, :] >= starts) & (spots[None, None, :] < starts + MASK_LEN), axis=1
    )
    masked_in = jnp.where(covered[:, :, None], mask_embed[None, None, :], feats_local)

    def work(step, s):
        offset = step - s
        if offset < 0:
            return None
        turn, slot = offset // sections, offset % sections
        return (turn, slot) if slot < micro and turn < repeats else None

    steps = repeats * sections + micro - 1
    plans = [[work(step, s) for s in range(sections)] for step in range(steps)]
    table = [
        [
            [
                int(plan[s] is not None),
                0 if plan[s] is None else plan[s][0],
                int(not (s == 0 and plan[s] is not None and plan[s][0] == 0)),
                int(s == last),
                0,
            ]
            for plan in plans + plans[:1]
        ]
        for s in range(sections)
    ]
    odd = lax.axis_index("fsdp") % 2
    lanes = lax.broadcasted_iota(jnp.int32, (steps + 1, 5), 1)
    entries = lax.broadcasted_iota(jnp.int32, (steps + 1, 5), 0)
    off = (lanes == 0) & (((entries == 0) & (odd == 1)) | ((entries == steps) & (odd == 0)))
    flags = lax.dynamic_index_in_dim(jnp.array(table, jnp.int32), section, 0, keepdims=False)
    flags = jnp.where(off, 0, flags)
    flags = jnp.where(lanes == 4, odd, flags)
    flags = jnp.where((entries == 1) & (lanes == 2) & (flags == 1), 1 + odd, flags)

    size = lax.axis_size("fsdp")
    if size == 8:
        pieces, starts, near = crossed(w_in[0, 0], "fsdp")
        dw, near = lax.optimization_barrier((dw_kernel, near))
        pieces[1] = near
    else:
        pieces = [lax.all_gather(w_in[0, 0], "fsdp", axis=0, tiled=True)]
        starts = None
        dw = dw_kernel
    taps = dw.shape[2]
    own = jnp.swapaxes(jnp.pad(dw[:, 0], ((0, 0), (0, -taps % 8), (0, 0))), 1, 2)
    own = jnp.swapaxes(own, 0, 1).reshape(own.shape[1], -1)
    full_k = doubled_rows(own, "fsdp").reshape(feats.shape[3], repeats, -1)
    full_k = jnp.transpose(full_k, (1, 2, 0))
    forward, inverse, rest = transforms(taps)
    rest = np.pad(rest, ((0, 0), (0, -taps % 8)))
    of_taps = []
    for _ in range(3):
        of_taps.append(rest.astype(ml_dtypes.bfloat16))
        rest = rest - of_taps[-1].astype(np.float64)
    of_taps = jnp.asarray(np.stack(of_taps))
    mats = (jnp.asarray(forward, jnp.bfloat16), jnp.asarray(inverse, jnp.bfloat16))
    kernels = [transformed(of_taps, full_k[turn]) for turn in range(repeats)]

    beside = (kernels, masked_in, flags, starts, mats)
    pieces, beside = lax.optimization_barrier((pieces, beside))
    kernels, masked_in, flags, starts, mats = beside

    def first_hop(block, parity):
        route = [(f, size + f) for f in range(parity, size, 2)]
        return lax.ppermute(block, ("section", "fsdp"), route)

    early, mark, *whole = layer(
        0, [0], flags, masked_in, 0, [], pieces, kernels[:1], mats, (), starts
    )
    weights = whole or pieces
    token = lax.ppermute(mark, "fsdp", [(i, i + 1) for i in range(0, size, 2)])
    early = first_hop(early, 0)
    tgt = targets(flags, feats_local, w_tgt, 1, token)
    result, mark = layer(
        steps, [0], flags, masked_in, 0, [], weights, kernels[:1], mats, (tgt,)
    )
    state = [early, first_hop(result, 1)]
    w_late, picks, mark = lax.optimization_barrier((w_in, distractors[:, 0], mark))
    for turn in range(1, repeats):
        rows = w_late[turn, 0]
        weights.append(lax.all_gather(rows, "fsdp", axis=0, tiled=True))
    tgt = targets(flags, feats_local, w_tgt, 0, mark, tgt)
    count = picks.shape[2]
    parts = [
        picks if s == last else lax.ppermute(picks, "section", [(s, last)]) for s in range(sections)
    ]

    losses = []
    for step, plan in enumerate(plans):
        if step == 0:
            continue
        turns = sorted({item[0] for item in plan if item is not None})
        slot = plan[0][1] if plan[0] is not None and plan[0][0] == 0 else None
        used = [weights[turn] for turn in turns]
        k_used = [kernels[turn] for turn in turns]
        spare = (tgt, *parts) if step == 1 else ()
        result, _ = layer(step, turns, flags, masked_in, slot, state, used, k_used, mats, spare)
        if step == 1:
            picks = jnp.pad(jnp.concatenate(parts, axis=1), ((0, 0), (0, 0), (0, -count % LANES)))
        ends = plan[last]
        if ends is not None and ends[0] == repeats - 1:
            losses.append(loss_rows(ends[1], flags, result, w_ctx, tgt, picks, count))
        route = []
        for s, item in enumerate(plan):
            if item is not None and not (s == last and item[0] == repeats - 1):
                route.append((s, (s + 1) % sections))
        if route:
            state = [lax.ppermute(result, "section", route)]

    loss = jnp.concatenate(losses, axis=0)
    share = frames // sections
    mine = jnp.zeros((micro, share), jnp.float32)
    for s in range(sections):
        cut = loss[:, s * share : (s + 1) * share]
        if s == last:
            mine = mine + jnp.where(section == last, cut, 0.0)
        else:
            mine = mine + lax.ppermute(cut, "section", [(last, s)])
    return mine[:, None, :]


def solution(mesh):
    placed = (
        P(None, "fsdp", None, None),
        P(None, "section", "fsdp", None),
        P(None, "section", None, "fsdp"),
        P(),
        P(),
        P(),
        P(None, "fsdp", None),
        P(None, "fsdp", "section", None),
    )
    return jax.shard_map(
        on_device, mesh=mesh, in_specs=placed, out_specs=P(None, "fsdp", "section"), check_vma=False
    )
```

```python
import functools

import jax
import jax.numpy as jnp
import ml_dtypes
import numpy as np
from jax import lax
from jax.experimental import pallas as pl
from jax.experimental.pallas import tpu as pltpu
from jax.sharding import PartitionSpec as P

MASK_LEN = 10
LANES = 128
PAD = 16
VMEM_LIMIT = 32 * 1024 * 1024


BLOCK = 128
WINDOW = BLOCK + 2 * PAD
HALF = WINDOW // 2


def transforms(taps):
    freq = np.arange(HALF)[:, None] * (2 * np.pi / WINDOW)
    spot = np.arange(WINDOW)[None, :]
    forward = np.concatenate([np.cos(freq * spot), -np.sin(freq * spot)])
    forward[HALF] = (-1.0) ** np.arange(WINDOW)
    inverse = forward[:, :BLOCK].T
    at = np.arange(taps)[None, :] + PAD - taps // 2
    scale = np.full((HALF, 1), 2.0 / WINDOW)
    scale[0] = 1.0 / WINDOW
    real, imag = np.cos(freq * at) * scale, np.sin(freq * at) * scale
    last = real.copy()
    last[0] = (-1.0) ** at[0] / WINDOW
    return forward, inverse, np.concatenate([real, imag, last])


def sigmoid(v):
    return 0.5 + 0.5 * jnp.tanh(0.5 * v)


def layer_body(entry, turns, held, fresh_slot, recvs, pieced, spare, flags, *refs):
    refs = list(refs)
    fresh = refs.pop(0) if fresh_slot is not None else None
    recv = [refs.pop(0) for _ in range(recvs)]
    pieces = [refs.pop(0) for _ in range(pieced)]
    starts = refs.pop(0) if pieced else None
    weights = [] if pieced else [refs.pop(0) for _ in turns]
    kernels = [refs.pop(0) for _ in turns]
    forward, inverse = refs.pop(0), refs.pop(0)
    del refs[:spare]
    out_ref, mark_ref = refs.pop(0), refs.pop(0)
    if pieced:
        weights = [refs.pop(0)]
    normed, glu = refs.pop(0), refs.pop(0)
    copied = any(not mine for mine in held)
    w_sem = refs.pop(0) if pieced or copied else None
    w_buf = refs.pop(0) if copied else None
    x_ref, x_sem = refs if refs else (recv[0], None)
    frames, width = x_ref.shape
    part = glu.shape[2]
    chunks = width // part
    valid = flags[entry, 0]
    turn = flags[entry, 1]

    def column(j, side):
        return pl.ds(pl.multiple_of(side * width + j * part, part), part)

    def wait_weights(w_ref, j):
        if pieced:
            for side in range(2):
                block = w_ref.at[:, column(j, side)]
                pltpu.make_async_copy(block, block, w_sem.at[j, side]).wait()
        elif w_ref is w_buf:
            for side in range(2):
                block = w_buf.at[j, side]
                pltpu.make_async_copy(block, block, w_sem.at[j, side]).wait()

    def project(w_ref, j, slot):
        if w_ref is w_buf:
            left, right = w_buf[j, 0], w_buf[j, 1]
        else:
            left, right = w_ref[:, column(j, 0)], w_ref[:, column(j, 1)]
        values = jnp.dot(normed[...], left, preferred_element_type=jnp.float32)
        gates = jnp.dot(normed[...], right, preferred_element_type=jnp.float32)
        glu[slot, PAD : PAD + frames, :] = (values * sigmoid(gates)).astype(jnp.bfloat16)

    def mix(k_ref, j, slot):
        cols = column(j, 0)
        real, imag, last = (k_ref[HALF * i : HALF * (i + 1), cols] for i in range(3))
        for row in range(0, frames, BLOCK):
            window = glu[slot, row : row + WINDOW, :]
            freq = jnp.dot(forward[...], window, preferred_element_type=jnp.float32)
            up, low = freq[:HALF], freq[HALF:]
            freq = jnp.concatenate([up * real - low * imag, up * imag + low * last], axis=0)
            conv = jnp.dot(
                inverse[...], freq.astype(jnp.bfloat16), preferred_element_type=jnp.float32
            )
            base = x_ref[row : row + BLOCK, cols].astype(jnp.float32)
            out_ref[row : row + BLOCK, cols] = (base + conv * sigmoid(conv)).astype(jnp.bfloat16)

    def compute(w_ref, k_ref):
        wait_weights(w_ref, 0)
        project(w_ref, 0, 0)

        @pl.loop(0, chunks - 1)
        def _(j):
            wait_weights(w_ref, j + 1)
            mix(k_ref, j, j % 2)
            project(w_ref, j + 1, (j + 1) % 2)

        mix(k_ref, chunks - 1, (chunks - 1) % 2)

    @pl.when(valid == 1)
    def _():
        if x_sem is not None:
            options = ([] if fresh is None else [fresh.at[fresh_slot]]) + recv
            first = 0 if fresh is not None else 1
            for i, option in enumerate(options):

                @pl.when(flags[entry, 2] == first + i)
                def _(option=option):
                    pltpu.make_async_copy(option, x_ref, x_sem).start()

        for i, which in enumerate(turns):
            if not held[i]:

                def load(source=weights[i]):
                    for j in range(chunks):
                        for side in range(2):
                            pltpu.make_async_copy(
                                source.at[:, column(j, side)], w_buf.at[j, side], w_sem.at[j, side]
                            ).start()

                if len(turns) == 1:
                    load()
                else:
                    pl.when(turn == which)(load)

    for j in range(chunks if pieced else 0):
        for side in range(2):
            for i, piece in enumerate(pieces):
                size = piece.shape[0]
                rows = pl.ds(pl.multiple_of(starts[i], size), size)
                pltpu.make_async_copy(
                    piece.at[:, column(j, side)],
                    weights[0].at[rows, column(j, side)],
                    w_sem.at[j, side],
                ).start()

    @pl.when(valid == 1)
    def _():
        zeros = jnp.zeros((2, PAD, part), jnp.bfloat16)
        glu[:, 0:PAD, :] = zeros
        glu[:, PAD + frames :, :] = zeros
        if x_sem is not None:
            pltpu.make_async_copy(x_ref, x_ref, x_sem).wait()
        for row in range(0, frames, 64):
            values = x_ref[row : row + 64, :].astype(jnp.float32)
            center = jnp.mean(values, axis=1, keepdims=True)
            moved = values - center
            spread = jnp.mean(moved * moved, axis=1, keepdims=True)
            normed[row : row + 64, :] = (moved * lax.rsqrt(spread + 1e-05)).astype(jnp.bfloat16)
        for which, w_ref, mine, k_ref in zip(turns, weights, held, kernels):
            w_ref = w_ref if mine else w_buf
            if len(turns) == 1:
                compute(w_ref, k_ref)
            else:
                pl.when(turn == which)(functools.partial(compute, w_ref, k_ref))

    if pieced:

        @pl.when(valid == 0)
        def _():
            for j in range(chunks):
                wait_weights(weights[0], j)

    mark_ref[...] = jnp.zeros(mark_ref.shape, mark_ref.dtype)


def layer(
    entry, turns, held, flags, fresh, fresh_slot, recvs, weights, kernels, matrices, spare=(), starts=None
):
    frames, width = recvs[0].shape if recvs else fresh.shape[1:]
    part = 256
    chunks = width // part
    anywhere = pl.BlockSpec(memory_space=pl.ANY)
    local = pl.BlockSpec(memory_space=pltpu.VMEM)
    smem = pl.BlockSpec(memory_space=pltpu.SMEM)
    select = fresh_slot is not None or len(recvs) > 1
    operands, specs = [flags], [smem]
    if fresh_slot is not None:
        operands.append(fresh)
        specs.append(anywhere)
    operands += recvs
    specs += [anywhere if select else local] * len(recvs)
    operands += weights
    specs += [local if starts is None and mine else anywhere for mine in held]
    specs += [anywhere] * (len(weights) - len(held))
    if starts is not None:
        operands.append(starts)
        specs.append(smem)
    operands += [*kernels, *matrices, *spare]
    specs += [local] * (len(kernels) + len(matrices)) + [anywhere] * len(spare)
    out_shape = [
        jax.ShapeDtypeStruct((frames, width), jnp.bfloat16),
        jax.ShapeDtypeStruct((8, LANES), jnp.float32),
    ]
    scratch = [
        pltpu.VMEM((frames, width), jnp.bfloat16),
        pltpu.VMEM((2, frames + 2 * PAD, part), jnp.bfloat16),
    ]
    if starts is not None:
        out_shape.append(jax.ShapeDtypeStruct((width, 2 * width), jnp.bfloat16))
        scratch.append(pltpu.SemaphoreType.DMA((chunks, 2)))
    elif not all(held):
        scratch.append(pltpu.SemaphoreType.DMA((chunks, 2)))
        scratch.append(pltpu.VMEM((chunks, 2, width, part), jnp.bfloat16))
    if select:
        scratch += [pltpu.VMEM((frames, width), jnp.bfloat16), pltpu.SemaphoreType.DMA]
    pieced = 0 if starts is None else len(weights)
    return pl.pallas_call(
        functools.partial(
            layer_body, entry, turns, held, fresh_slot, len(recvs), pieced, len(spare)
        ),
        in_specs=specs,
        out_specs=[local] * len(out_shape),
        out_shape=out_shape,
        scratch_shapes=scratch,
        compiler_params=pltpu.CompilerParams(vmem_limit_bytes=VMEM_LIMIT),
        cost_estimate=pl.CostEstimate(
            flops=4 * frames * width * width, bytes_accessed=4 * width * width, transcendentals=0
        ),
        name="layer",
    )(*operands)


def transform_body(m_ref, k_ref, out_ref):
    total = jnp.dot(m_ref[0], k_ref[...], preferred_element_type=jnp.float32)
    for part in range(1, m_ref.shape[0]):
        total = total + jnp.dot(m_ref[part], k_ref[...], preferred_element_type=jnp.float32)
    out_ref[...] = total


def transformed(matrix, kernel):
    return pl.pallas_call(
        transform_body,
        out_shape=jax.ShapeDtypeStruct((matrix.shape[1], kernel.shape[1]), jnp.float32),
        compiler_params=pltpu.CompilerParams(vmem_limit_bytes=VMEM_LIMIT),
        name="transformed",
    )(matrix, kernel)


def unit_rows(values):
    return (values * lax.rsqrt(jnp.sum(values * values, axis=-1, keepdims=True) + 1e-06)).astype(
        jnp.bfloat16
    )


def target_body(wanted, flags, feats, w_tgt, *refs):
    out, feats_ref, w_ref, out_ref, sems = refs[-5:]

    @pl.when(flags[0, 4] == wanted)
    def _():
        load_w = pltpu.make_async_copy(w_tgt, w_ref, sems.at[0])
        load_x = pltpu.make_async_copy(feats, feats_ref, sems.at[1])
        load_w.start()
        load_x.start()
        load_w.wait()
        load_x.wait()

        @pl.loop(0, feats_ref.shape[0])
        def _(slot):
            out_ref[slot] = unit_rows(
                jnp.dot(feats_ref[slot], w_ref[...], preferred_element_type=jnp.float32)
            )

        back = pltpu.make_async_copy(out_ref, out, sems.at[2])
        back.start()
        back.wait()


def targets(flags, feats, w_tgt, wanted, spare, earlier=None):
    operands = [flags, feats, w_tgt, spare] + ([] if earlier is None else [earlier])
    anywhere = pl.BlockSpec(memory_space=pl.ANY)
    shape = feats.shape[:2] + w_tgt.shape[1:]
    return pl.pallas_call(
        functools.partial(target_body, wanted),
        in_specs=[pl.BlockSpec(memory_space=pltpu.SMEM)] + [anywhere] * (len(operands) - 1),
        out_specs=anywhere,
        out_shape=jax.ShapeDtypeStruct(shape, jnp.bfloat16),
        scratch_shapes=[
            pltpu.VMEM(feats.shape, jnp.bfloat16),
            pltpu.VMEM(w_tgt.shape, jnp.bfloat16),
            pltpu.VMEM(shape, jnp.bfloat16),
            pltpu.SemaphoreType.DMA((3,)),
        ],
        input_output_aliases={} if earlier is None else {4: 0},
        compiler_params=pltpu.CompilerParams(vmem_limit_bytes=VMEM_LIMIT),
        cost_estimate=pl.CostEstimate(
            flops=2 * feats.size * w_tgt.shape[1],
            bytes_accessed=2 * (feats.size + w_tgt.size),
            transcendentals=0,
        ),
        name="targets",
    )(*operands)


def loss_body(slot, count, flags, x_ref, w_ref, tgt_ref, pick_ref, out_ref):
    frames = x_ref.shape[0]

    @pl.when(flags[0, 3] == 1)
    def _():
        ctx = unit_rows(jnp.dot(x_ref[...], w_ref[...], preferred_element_type=jnp.float32))
        sims = lax.dot_general(
            ctx, tgt_ref[slot], (((1,), (1,)), ((), ())), preferred_element_type=jnp.float32
        )
        row = lax.broadcasted_iota(jnp.int32, sims.shape, 0)
        col = lax.broadcasted_iota(jnp.int32, sims.shape, 1)
        positive = jnp.sum(jnp.where(row == col, sims, 0.0), axis=1, keepdims=True) * 10.0
        picks = pick_ref[slot]
        lane = picks % LANES
        block = picks // LANES
        negative = jnp.zeros(picks.shape, jnp.float32)
        for part in range(frames // LANES):
            found = jnp.take_along_axis(sims[:, part * LANES : (part + 1) * LANES], lane, axis=1)
            negative = jnp.where(block == part, found, negative)
        place = lax.broadcasted_iota(jnp.int32, picks.shape, 1)
        terms = jnp.where(place < count, jnp.exp(negative * 10.0), 0.0)
        total = jnp.exp(positive) + jnp.sum(terms, axis=1, keepdims=True)
        wide = jnp.broadcast_to(jnp.log(total) - positive, (frames, LANES))
        out_ref[...] = wide.T[0:1, :]


def loss_rows(slot, flags, x, w_ctx, tgt, picks, count):
    frames = x.shape[0]
    whole = pl.BlockSpec(memory_space=pltpu.VMEM)
    return pl.pallas_call(
        functools.partial(loss_body, slot, count),
        in_specs=[pl.BlockSpec(memory_space=pltpu.SMEM)] + [whole] * 4,
        out_specs=whole,
        out_shape=jax.ShapeDtypeStruct((1, frames), jnp.float32),
        compiler_params=pltpu.CompilerParams(vmem_limit_bytes=VMEM_LIMIT),
        name="loss",
    )(flags, x, w_ctx, tgt, picks)


def swap(block, axis, mask):
    return lax.ppermute(block, axis, [(i, i ^ mask) for i in range(lax.axis_size(axis))])


def doubled_rows(block, axis):
    me = lax.axis_index(axis)
    size = lax.axis_size(axis)
    if size & (size - 1):
        return lax.all_gather(block, axis, axis=0, tiled=True)
    mask = 1
    while mask < size:
        other = swap(block, axis, mask)
        upper = (me & mask) != 0
        block = jnp.concatenate(
            [jnp.where(upper, other, block), jnp.where(upper, block, other)], axis=0
        )
        mask *= 2
    return block


def crossed(block, axis):
    size = lax.axis_size(axis)
    me = lax.axis_index(axis)
    odd = me % 2
    ahead = [(i, i ^ (2 if i % 2 else 4)) for i in range(size)]
    other = [(i, i ^ (4 if i % 2 else 2)) for i in range(size)]
    near = lax.ppermute(block, axis, ahead)
    block, near = lax.optimization_barrier((block, near))
    far = lax.ppermute(near, axis, other)
    side = lax.ppermute(block, axis, other)
    first, second = 4 - 2 * odd, 2 + 2 * odd
    pieces = [block, near, side, far]
    masks = [0, first, second, 6]
    pieces += [swap(piece, axis, 1) for piece in pieces]
    masks += [1, second ^ 1, first ^ 1, 7]
    starts = jnp.stack([(me ^ mask) * block.shape[0] for mask in masks]).astype(jnp.int32)
    return pieces, starts, near


def on_device(feats, w_in, dw_kernel, mask_embed, w_ctx, w_tgt, mask_starts, distractors):
    sections = lax.axis_size("section")
    section = lax.axis_index("section")
    micro = feats.shape[0]
    frames = feats.shape[2]
    repeats = w_in.shape[0]
    last = sections - 1
    feats_local = feats[:, 0]

    spots = jnp.arange(frames, dtype=jnp.int32)
    starts = mask_starts[:, 0][:, :, None]
    covered = jnp.any(
        (spots[None, None, :] >= starts) & (spots[None, None, :] < starts + MASK_LEN), axis=1
    )
    masked_in = jnp.where(covered[:, :, None], mask_embed[None, None, :], feats_local)

    def work(step, s):
        offset = step - s
        if offset < 0:
            return None
        turn, slot = offset // sections, offset % sections
        return (turn, slot) if slot < micro and turn < repeats else None

    steps = repeats * sections + micro - 1
    plans = [[work(step, s) for s in range(sections)] for step in range(steps)]
    table = [
        [
            [
                int(plan[s] is not None),
                0 if plan[s] is None else plan[s][0],
                int(not (s == 0 and plan[s] is not None and plan[s][0] == 0)),
                int(s == last),
                0,
            ]
            for plan in plans
        ]
        for s in range(sections)
    ]
    odd = lax.axis_index("fsdp") % 2
    flags = lax.dynamic_index_in_dim(jnp.array(table, jnp.int32), section, 0, keepdims=False)
    lanes = lax.broadcasted_iota(jnp.int32, flags.shape, 1)
    entries = lax.broadcasted_iota(jnp.int32, flags.shape, 0)
    flags = jnp.where(lanes == 4, odd, flags)
    flags = jnp.where((entries == 1) & (lanes == 2) & (flags == 1), 1 + odd, flags)

    size = lax.axis_size("fsdp")
    if size == 8:
        pieces, starts, near = crossed(w_in[0, 0], "fsdp")
        dw, near = lax.optimization_barrier((dw_kernel, near))
        pieces[1] = near
    else:
        pieces = [lax.all_gather(w_in[0, 0], "fsdp", axis=0, tiled=True)]
        starts = None
        dw = dw_kernel
    taps = dw.shape[2]
    own = jnp.swapaxes(jnp.pad(dw[:, 0], ((0, 0), (0, -taps % 8), (0, 0))), 1, 2)
    own = jnp.swapaxes(own, 0, 1).reshape(own.shape[1], -1)
    full_k = doubled_rows(own, "fsdp").reshape(feats.shape[3], repeats, -1)
    full_k = jnp.transpose(full_k, (1, 2, 0))
    forward, inverse, rest = transforms(taps)
    rest = np.pad(rest, ((0, 0), (0, -taps % 8)))
    of_taps = []
    for _ in range(3):
        of_taps.append(rest.astype(ml_dtypes.bfloat16))
        rest = rest - of_taps[-1].astype(np.float64)
    of_taps = jnp.asarray(np.stack(of_taps))
    mats = (jnp.asarray(forward, jnp.bfloat16), jnp.asarray(inverse, jnp.bfloat16))
    kernels = [transformed(of_taps, full_k[turn]) for turn in range(repeats)]

    beside = (kernels, masked_in, flags, starts, mats)
    pieces, beside = lax.optimization_barrier((pieces, beside))
    kernels, masked_in, flags, starts, mats = beside

    def first_hop(block, parity):
        route = [(f, size + f) for f in range(parity, size, 2)]
        return lax.ppermute(block, ("section", "fsdp"), route)

    w_late, pieces = lax.optimization_barrier((w_in, pieces))
    late = [
        lax.all_gather(w_late[turn, 0], "fsdp", axis=0, tiled=True) for turn in range(1, repeats)
    ]
    held = [True] + [False] * (repeats - 1)
    result, mark, *whole = layer(
        0, [0], [True], flags, masked_in, 0, [], pieces, kernels[:1], mats, (), starts
    )
    weights = (whole or pieces) + late

    token = lax.ppermute(mark, "fsdp", [(i, i + 1) for i in range(0, size, 2)])
    early = first_hop(result, 0)
    tgt = targets(flags, feats_local, w_tgt, 1, token)
    picks, tgt = lax.optimization_barrier((distractors[:, 0], tgt))
    parts = [lax.ppermute(picks, "section", [(0, last)])]
    result, tgt, parts = lax.optimization_barrier((result, tgt, parts))
    state = [early, first_hop(result, 1)]
    count = distractors.shape[3]

    losses = []
    for step, plan in enumerate(plans):
        if step == 0:
            continue
        turns = sorted({item[0] for item in plan if item is not None})
        slot = plan[0][1] if plan[0] is not None and plan[0][0] == 0 else None
        used = [weights[turn] for turn in turns]
        k_used = [kernels[turn] for turn in turns]
        mine = [held[turn] for turn in turns]
        spare = ()
        if step < last:
            picks, mark = lax.optimization_barrier((distractors[:, 0], mark))
            parts.append(lax.ppermute(picks, "section", [(step, last)]))
            spare = (mark, parts[-1])
        if step == 2:
            tgt = targets(flags, feats_local, w_tgt, 0, mark, tgt)
            spare += (tgt,)
        result, mark = layer(
            step, turns, mine, flags, masked_in, slot, state, used, k_used, mats, spare
        )
        if step == last:
            picks = jnp.concatenate(parts + [distractors[:, 0]], axis=1)
            picks = jnp.pad(picks, ((0, 0), (0, 0), (0, -count % LANES)))
        ends = plan[last]
        if ends is not None and ends[0] == repeats - 1:
            losses.append(loss_rows(ends[1], flags, result, w_ctx, tgt, picks, count))
        route = []
        for s, item in enumerate(plan):
            if item is not None and not (s == last and item[0] == repeats - 1):
                route.append((s, (s + 1) % sections))
        if route:
            state = [lax.ppermute(result, "section", route)]

    loss = jnp.concatenate(losses, axis=0)
    share = frames // sections
    mine = jnp.zeros((micro, share), jnp.float32)
    for s in range(sections):
        cut = loss[:, s * share : (s + 1) * share]
        if s == last:
            mine = mine + jnp.where(section == last, cut, 0.0)
        else:
            mine = mine + lax.ppermute(cut, "section", [(last, s)])
    return mine[:, None, :]


def solution(mesh):
    placed = (
        P(None, "fsdp", None, None),
        P(None, "section", "fsdp", None),
        P(None, "section", None, "fsdp"),
        P(),
        P(),
        P(),
        P(None, "fsdp", None),
        P(None, "fsdp", "section", None),
    )
    return jax.shard_map(
        on_device, mesh=mesh, in_specs=placed, out_specs=P(None, "fsdp", "section"), check_vma=False
    )
```

```python
import functools

import jax
import jax.numpy as jnp
import ml_dtypes
import numpy as np
from jax import lax
from jax.experimental import pallas as pl
from jax.experimental.pallas import tpu as pltpu
from jax.sharding import PartitionSpec as P

MASK_LEN = 10
LANES = 128
PAD = 16
VMEM_LIMIT = 48 * 1024 * 1024


BLOCK = 128
WINDOW = BLOCK + 2 * PAD
HALF = WINDOW // 2


def transforms(taps):
    freq = np.arange(HALF)[:, None] * (2 * np.pi / WINDOW)
    spot = np.arange(WINDOW)[None, :]
    forward = np.concatenate([np.cos(freq * spot), -np.sin(freq * spot)])
    forward[HALF] = (-1.0) ** np.arange(WINDOW)
    inverse = forward[:, :BLOCK].T
    at = np.arange(taps)[None, :] + PAD - taps // 2
    scale = np.full((HALF, 1), 2.0 / WINDOW)
    scale[0] = 1.0 / WINDOW
    real, imag = np.cos(freq * at) * scale, np.sin(freq * at) * scale
    last = real.copy()
    last[0] = (-1.0) ** at[0] / WINDOW
    return forward, inverse, np.concatenate([real, imag, last])


def sigmoid(v):
    return 0.5 + 0.5 * jnp.tanh(0.5 * v)


def layer_body(entry, kinds, fresh_slot, recvs, spare, base, flags, *refs):
    refs = list(refs)
    fresh = refs.pop(0) if fresh_slot is not None else None
    recv = [refs.pop(0) for _ in range(recvs)]
    sources = [[refs.pop(0) for _ in range(count)] for _, _, count in kinds]
    starts = refs.pop(0)
    k_refs = [refs.pop(0) for _ in kinds]
    forward, inverse = refs.pop(0), refs.pop(0)
    del refs[:spare]
    out_ref, mark_ref, normed, wbuf, glu, w_sem = (refs.pop(0) for _ in range(6))
    x_ref, x_sem = refs if refs else (recv[0], None)
    chunks, width, part = wbuf.shape
    part = part // 2
    frames = x_ref.shape[0]
    valid = flags[entry, 0]
    turn = flags[entry, 1]

    def weight_copies(kind, source, j, side):
        target, sem = wbuf.at[j, :, pl.ds(side * part, part)], w_sem.at[j]
        cols = pl.ds(pl.multiple_of(side * width + j * part, part), part)
        if kind == "rows":
            return [pltpu.make_async_copy(source[0].at[:, cols], target, sem)]
        copies = []
        for i, piece in enumerate(source):
            size = piece.shape[0]
            place = pl.ds(pl.multiple_of(starts[i], size), size)
            into = wbuf.at[j, place, pl.ds(side * part, part)]
            copies.append(pltpu.make_async_copy(piece.at[:, cols], into, sem))
        return copies

    def start_weights(j):
        def issue(kind, source):
            for side in range(2):
                for copy in weight_copies(kind, source, j, side):
                    copy.start()

        for (which, kind, _), source in zip(kinds, sources):
            if len(kinds) == 1:
                issue(kind, source)
            else:
                pl.when(turn == which)(functools.partial(issue, kind, source))

    def wait_weights(j):
        pltpu.make_async_copy(wbuf.at[j], wbuf.at[j], w_sem.at[j]).wait()

    def project(j, slot):
        both = jnp.dot(normed[...], wbuf[j], preferred_element_type=jnp.float32)
        gated = both[:, :part] * sigmoid(both[:, part:])
        glu[slot, PAD : PAD + frames, :] = gated.astype(jnp.bfloat16)

    def taps(i, cols):
        rows = slice(HALF * i, HALF * (i + 1))
        chosen = k_refs[0][rows, cols]
        for (which, _, _), k_ref in zip(kinds[1:], k_refs[1:]):
            chosen = jnp.where(turn == which, k_ref[rows, cols], chosen)
        return chosen

    def mix(j, slot):
        cols = pl.ds(pl.multiple_of(j * part, part), part)
        real, imag, last = (taps(i, cols) for i in range(3))
        for row in range(0, frames, BLOCK):
            window = glu[slot, row : row + WINDOW, :]
            freq = jnp.dot(forward[...], window, preferred_element_type=jnp.float32)
            up, low = freq[:HALF], freq[HALF:]
            freq = jnp.concatenate([up * real - low * imag, up * imag + low * last], axis=0)
            conv = jnp.dot(
                inverse[...], freq.astype(jnp.bfloat16), preferred_element_type=jnp.float32
            )
            base = x_ref[row : row + BLOCK, cols].astype(jnp.float32)
            out_ref[row : row + BLOCK, cols] = (base + conv * sigmoid(conv)).astype(jnp.bfloat16)

    @pl.when(valid == 1)
    def _():
        ahead = min(3, chunks)
        if x_sem is not None:
            options = ([] if fresh is None else [fresh.at[fresh_slot]]) + recv
            first = base
            for i, option in enumerate(options):

                @pl.when(flags[entry, 2] == first + i)
                def _(option=option):
                    pltpu.make_async_copy(option, x_ref, x_sem).start()

        for j in range(ahead):
            start_weights(j)
        zeros = jnp.zeros((2, PAD, part), jnp.bfloat16)
        glu[:, 0:PAD, :] = zeros
        glu[:, PAD + frames :, :] = zeros
        if x_sem is not None:
            pltpu.make_async_copy(x_ref, x_ref, x_sem).wait()
        for row in range(0, frames, 64):
            values = x_ref[row : row + 64, :].astype(jnp.float32)
            center = jnp.mean(values, axis=1, keepdims=True)
            moved = values - center
            spread = jnp.mean(moved * moved, axis=1, keepdims=True)
            normed[row : row + 64, :] = (moved * lax.rsqrt(spread + 1e-05)).astype(jnp.bfloat16)
        wait_weights(0)
        project(0, 0)

        @pl.loop(0, chunks - 1)
        def _(j):
            wait_weights(j + 1)

            @pl.when(j + ahead < chunks)
            def _():
                start_weights(j + ahead)

            mix(j, j % 2)
            project(j + 1, (j + 1) % 2)

        mix(chunks - 1, (chunks - 1) % 2)

    mark_ref[...] = jnp.zeros(mark_ref.shape, mark_ref.dtype)


def layer(
    entry, flags, fresh, fresh_slot, recvs, weights, starts, kernels, matrices, spare=(), base=0
):
    frames, width = recvs[0].shape if recvs else fresh.shape[1:]
    part = 256
    chunks = width // part
    anywhere = pl.BlockSpec(memory_space=pl.ANY)
    local = pl.BlockSpec(memory_space=pltpu.VMEM)
    smem = pl.BlockSpec(memory_space=pltpu.SMEM)
    select = fresh_slot is not None or len(recvs) > 1
    operands, specs = [flags], [smem]
    if fresh_slot is not None:
        operands.append(fresh)
        specs.append(anywhere)
    operands += recvs
    specs += [anywhere if select else local] * len(recvs)
    for _, _, arrays in weights:
        operands += arrays
        specs += [anywhere] * len(arrays)
    operands += [starts, *kernels, *matrices, *spare]
    specs += [smem] + [local] * (len(kernels) + len(matrices)) + [anywhere] * len(spare)
    scratch = [
        pltpu.VMEM((frames, width), jnp.bfloat16),
        pltpu.VMEM((chunks, width, 2 * part), jnp.bfloat16),
        pltpu.VMEM((2, frames + 2 * PAD, part), jnp.bfloat16),
        pltpu.SemaphoreType.DMA((chunks,)),
    ]
    if select:
        scratch += [pltpu.VMEM((frames, width), jnp.bfloat16), pltpu.SemaphoreType.DMA]
    kinds = [(turn, kind, len(arrays)) for turn, kind, arrays in weights]
    return pl.pallas_call(
        functools.partial(
            layer_body, entry, kinds, fresh_slot, len(recvs), len(spare), base
        ),
        in_specs=specs,
        out_specs=[local, local],
        out_shape=[
            jax.ShapeDtypeStruct((frames, width), jnp.bfloat16),
            jax.ShapeDtypeStruct((8, LANES), jnp.float32),
        ],
        scratch_shapes=scratch,
        compiler_params=pltpu.CompilerParams(vmem_limit_bytes=VMEM_LIMIT),
        cost_estimate=pl.CostEstimate(
            flops=4 * frames * width * width, bytes_accessed=4 * width * width, transcendentals=0
        ),
        name="layer",
    )(*operands)


def transform_body(m_ref, k_ref, out_ref):
    total = jnp.dot(m_ref[0], k_ref[...], preferred_element_type=jnp.float32)
    for part in range(1, m_ref.shape[0]):
        total = total + jnp.dot(m_ref[part], k_ref[...], preferred_element_type=jnp.float32)
    out_ref[...] = total


def transformed(matrix, kernel):
    return pl.pallas_call(
        transform_body,
        out_shape=jax.ShapeDtypeStruct((matrix.shape[1], kernel.shape[1]), jnp.float32),
        compiler_params=pltpu.CompilerParams(vmem_limit_bytes=VMEM_LIMIT),
        name="transformed",
    )(matrix, kernel)


def unit_rows(values):
    return (values * lax.rsqrt(jnp.sum(values * values, axis=-1, keepdims=True) + 1e-06)).astype(
        jnp.bfloat16
    )


def target_body(wanted, flags, feats, w_tgt, *refs):
    out, feats_ref, w_ref, out_ref, sems = refs[-5:]

    @pl.when(flags[0, 4] == wanted)
    def _():
        load_w = pltpu.make_async_copy(w_tgt, w_ref, sems.at[0])
        load_x = pltpu.make_async_copy(feats, feats_ref, sems.at[1])
        load_w.start()
        load_x.start()
        load_w.wait()
        load_x.wait()

        @pl.loop(0, feats_ref.shape[0])
        def _(slot):
            out_ref[slot] = unit_rows(
                jnp.dot(feats_ref[slot], w_ref[...], preferred_element_type=jnp.float32)
            )

        back = pltpu.make_async_copy(out_ref, out, sems.at[2])
        back.start()
        back.wait()


def targets(flags, feats, w_tgt, wanted, spare, earlier=None):
    operands = [flags, feats, w_tgt, spare] + ([] if earlier is None else [earlier])
    anywhere = pl.BlockSpec(memory_space=pl.ANY)
    shape = feats.shape[:2] + w_tgt.shape[1:]
    return pl.pallas_call(
        functools.partial(target_body, wanted),
        in_specs=[pl.BlockSpec(memory_space=pltpu.SMEM)] + [anywhere] * (len(operands) - 1),
        out_specs=anywhere,
        out_shape=jax.ShapeDtypeStruct(shape, jnp.bfloat16),
        scratch_shapes=[
            pltpu.VMEM(feats.shape, jnp.bfloat16),
            pltpu.VMEM(w_tgt.shape, jnp.bfloat16),
            pltpu.VMEM(shape, jnp.bfloat16),
            pltpu.SemaphoreType.DMA((3,)),
        ],
        input_output_aliases={} if earlier is None else {4: 0},
        compiler_params=pltpu.CompilerParams(vmem_limit_bytes=VMEM_LIMIT),
        cost_estimate=pl.CostEstimate(
            flops=2 * feats.size * w_tgt.shape[1],
            bytes_accessed=2 * (feats.size + w_tgt.size),
            transcendentals=0,
        ),
        name="targets",
    )(*operands)


def loss_body(slot, count, flags, x_ref, w_ref, tgt_ref, pick_ref, out_ref):
    frames = x_ref.shape[0]

    @pl.when(flags[0, 3] == 1)
    def _():
        ctx = unit_rows(jnp.dot(x_ref[...], w_ref[...], preferred_element_type=jnp.float32))
        sims = lax.dot_general(
            ctx, tgt_ref[slot], (((1,), (1,)), ((), ())), preferred_element_type=jnp.float32
        )
        row = lax.broadcasted_iota(jnp.int32, sims.shape, 0)
        col = lax.broadcasted_iota(jnp.int32, sims.shape, 1)
        positive = jnp.sum(jnp.where(row == col, sims, 0.0), axis=1, keepdims=True) * 10.0
        picks = pick_ref[slot]
        lane = picks % LANES
        block = picks // LANES
        negative = jnp.zeros(picks.shape, jnp.float32)
        for part in range(frames // LANES):
            found = jnp.take_along_axis(sims[:, part * LANES : (part + 1) * LANES], lane, axis=1)
            negative = jnp.where(block == part, found, negative)
        place = lax.broadcasted_iota(jnp.int32, picks.shape, 1)
        terms = jnp.where(place < count, jnp.exp(negative * 10.0), 0.0)
        total = jnp.exp(positive) + jnp.sum(terms, axis=1, keepdims=True)
        wide = jnp.broadcast_to(jnp.log(total) - positive, (frames, LANES))
        out_ref[...] = wide.T[0:1, :]


def loss_rows(slot, flags, x, w_ctx, tgt, picks, count):
    frames = x.shape[0]
    whole = pl.BlockSpec(memory_space=pltpu.VMEM)
    return pl.pallas_call(
        functools.partial(loss_body, slot, count),
        in_specs=[pl.BlockSpec(memory_space=pltpu.SMEM)] + [whole] * 4,
        out_specs=whole,
        out_shape=jax.ShapeDtypeStruct((1, frames), jnp.float32),
        compiler_params=pltpu.CompilerParams(vmem_limit_bytes=VMEM_LIMIT),
        name="loss",
    )(flags, x, w_ctx, tgt, picks)


def swap(block, axis, mask):
    return lax.ppermute(block, axis, [(i, i ^ mask) for i in range(lax.axis_size(axis))])


def doubled_rows(block, axis):
    me = lax.axis_index(axis)
    size = lax.axis_size(axis)
    if size & (size - 1):
        return lax.all_gather(block, axis, axis=0, tiled=True)
    mask = 1
    while mask < size:
        other = swap(block, axis, mask)
        upper = (me & mask) != 0
        block = jnp.concatenate(
            [jnp.where(upper, other, block), jnp.where(upper, block, other)], axis=0
        )
        mask *= 2
    return block


def crossed(block, axis):
    size = lax.axis_size(axis)
    me = lax.axis_index(axis)
    odd = me % 2
    ahead = [(i, i ^ (2 if i % 2 else 4)) for i in range(size)]
    other = [(i, i ^ (4 if i % 2 else 2)) for i in range(size)]
    near = lax.ppermute(block, axis, ahead)
    block, near = lax.optimization_barrier((block, near))
    far = lax.ppermute(near, axis, other)
    side = lax.ppermute(block, axis, other)
    first, second = 4 - 2 * odd, 2 + 2 * odd
    pieces = [block, near, side, far]
    masks = [0, first, second, 6]
    pieces += [swap(piece, axis, 1) for piece in pieces]
    masks += [1, second ^ 1, first ^ 1, 7]
    starts = jnp.stack([(me ^ mask) * block.shape[0] for mask in masks]).astype(jnp.int32)
    return pieces, starts, near


def on_device(feats, w_in, dw_kernel, mask_embed, w_ctx, w_tgt, mask_starts, distractors):
    sections = lax.axis_size("section")
    section = lax.axis_index("section")
    micro = feats.shape[0]
    frames = feats.shape[2]
    repeats = w_in.shape[0]
    last = sections - 1
    feats_local = feats[:, 0]

    spots = jnp.arange(frames, dtype=jnp.int32)
    starts = mask_starts[:, 0][:, :, None]
    covered = jnp.any(
        (spots[None, None, :] >= starts) & (spots[None, None, :] < starts + MASK_LEN), axis=1
    )
    masked_in = jnp.where(covered[:, :, None], mask_embed[None, None, :], feats_local)

    def work(step, s):
        offset = step - s
        if offset < 0:
            return None
        turn, slot = offset // sections, offset % sections
        return (turn, slot) if slot < micro and turn < repeats else None

    steps = repeats * sections + micro - 1
    plans = [[work(step, s) for s in range(sections)] for step in range(steps)]
    table = [
        [
            [
                int(plan[s] is not None),
                0 if plan[s] is None else plan[s][0],
                int(not (s == 0 and plan[s] is not None and plan[s][0] == 0)),
                int(s == last),
                0,
            ]
            for plan in plans + plans[:1]
        ]
        for s in range(sections)
    ]
    odd = lax.axis_index("fsdp") % 2
    flags = lax.dynamic_index_in_dim(jnp.array(table, jnp.int32), section, 0, keepdims=False)
    lanes = lax.broadcasted_iota(jnp.int32, flags.shape, 1)
    entries = lax.broadcasted_iota(jnp.int32, flags.shape, 0)
    off = (lanes == 0) & (((entries == 0) & (odd == 1)) | ((entries == steps) & (odd == 0)))
    flags = jnp.where(lanes == 4, odd, jnp.where(off, 0, flags))
    flags = jnp.where((entries == 1) & (lanes == 2) & (flags == 1), 1 + odd, flags)

    size = lax.axis_size("fsdp")
    if size == 8:
        pieces, starts, near = crossed(w_in[0, 0], "fsdp")
        kind = "pieces"
        dw, near = lax.optimization_barrier((dw_kernel, near))
        pieces[1] = near
    else:
        pieces = [lax.all_gather(w_in[0, 0], "fsdp", axis=0, tiled=True)]
        starts = jnp.zeros((1,), jnp.int32)
        kind = "rows"
        dw = dw_kernel
    taps = dw.shape[2]
    own = jnp.swapaxes(jnp.pad(dw[:, 0], ((0, 0), (0, -taps % 8), (0, 0))), 1, 2)
    own = jnp.swapaxes(own, 0, 1).reshape(own.shape[1], -1)
    full_k = doubled_rows(own, "fsdp").reshape(feats.shape[3], repeats, -1)
    full_k = jnp.transpose(full_k, (1, 2, 0))
    forward, inverse, rest = transforms(taps)
    rest = np.pad(rest, ((0, 0), (0, -taps % 8)))
    of_taps = []
    for _ in range(3):
        of_taps.append(rest.astype(ml_dtypes.bfloat16))
        rest = rest - of_taps[-1].astype(np.float64)
    of_taps = jnp.asarray(np.stack(of_taps))
    mats = (jnp.asarray(forward, jnp.bfloat16), jnp.asarray(inverse, jnp.bfloat16))
    kernels = [transformed(of_taps, full_k[turn]) for turn in range(repeats)]

    later = [w_in[turn, 0] for turn in range(1, repeats)]
    beside = (kernels, masked_in, flags, starts, mats, later)
    pieces, beside = lax.optimization_barrier((pieces, beside))
    kernels, masked_in, flags, starts, mats, later = beside

    def first_hop(block, parity):
        route = [(f, size + f) for f in range(parity, size, 2)]
        return lax.ppermute(block, ("section", "fsdp"), route)

    weights = [(0, kind, pieces)]
    for turn in range(1, repeats):
        rows = lax.all_gather(later[turn - 1], "fsdp", axis=0, tiled=True)
        weights.append((turn, "rows", [rows]))

    early, mark = layer(
        0, flags, masked_in, 0, [], weights[:1], starts, kernels[:1], mats
    )
    token = lax.ppermute(mark, "fsdp", [(i, i + 1) for i in range(0, size, 2)])
    early = first_hop(early, 0)
    tgt = targets(flags, feats_local, w_tgt, 1, token)
    result, mark = layer(
        steps, flags, masked_in, 0, [], weights[:1], starts, kernels[:1], mats, (tgt,)
    )
    state = [early, first_hop(result, 1)]
    count = distractors.shape[3]
    parts = []

    losses = []
    for step, plan in enumerate(plans):
        if step == 0:
            continue
        turns = sorted({item[0] for item in plan if item is not None})
        slot = plan[0][1] if plan[0] is not None and plan[0][0] == 0 else None
        used = [weights[turn] for turn in turns]
        k_used = [kernels[turn] for turn in turns]
        spare = ()
        if step <= last:
            picks, mark = lax.optimization_barrier((distractors[:, 0], mark))
            parts.append(lax.ppermute(picks, "section", [(step - 1, last)]))
            spare = (mark, parts[-1])
        if step == 2:
            tgt = targets(flags, feats_local, w_tgt, 0, mark, tgt)
            spare += (tgt,)
        result, mark = layer(
            step, flags, masked_in, slot, state, used, starts, k_used, mats, spare
        )
        if step == last:
            picks = jnp.concatenate(parts + [distractors[:, 0]], axis=1)
            picks = jnp.pad(picks, ((0, 0), (0, 0), (0, -count % LANES)))
        ends = plan[last]
        if ends is not None and ends[0] == repeats - 1:
            losses.append(loss_rows(ends[1], flags, result, w_ctx, tgt, picks, count))
        route = []
        for s, item in enumerate(plan):
            if item is not None and not (s == last and item[0] == repeats - 1):
                route.append((s, (s + 1) % sections))
        if route:
            state = [lax.ppermute(result, "section", route)]

    loss = jnp.concatenate(losses, axis=0)
    share = frames // sections
    mine = jnp.zeros((micro, share), jnp.float32)
    for s in range(sections):
        cut = loss[:, s * share : (s + 1) * share]
        if s == last:
            mine = mine + jnp.where(section == last, cut, 0.0)
        else:
            mine = mine + lax.ppermute(cut, "section", [(last, s)])
    return mine[:, None, :]


def solution(mesh):
    placed = (
        P(None, "fsdp", None, None),
        P(None, "section", "fsdp", None),
        P(None, "section", None, "fsdp"),
        P(),
        P(),
        P(),
        P(None, "fsdp", None),
        P(None, "fsdp", "section", None),
    )
    return jax.shard_map(
        on_device, mesh=mesh, in_specs=placed, out_specs=P(None, "fsdp", "section"), check_vma=False
    )
```

```python
import functools

import jax
import jax.numpy as jnp
import ml_dtypes
import numpy as np
from jax import lax
from jax.experimental import pallas as pl
from jax.experimental.pallas import tpu as pltpu
from jax.sharding import PartitionSpec as P

MASK_LEN = 10
LANES = 128
PAD = 16
VMEM_LIMIT = 28 * 1024 * 1024


BLOCK = 128
WINDOW = BLOCK + 2 * PAD
HALF = WINDOW // 2


def transforms(taps):
    freq = np.arange(HALF)[:, None] * (2 * np.pi / WINDOW)
    spot = np.arange(WINDOW)[None, :]
    forward = np.concatenate([np.cos(freq * spot), -np.sin(freq * spot)])
    forward[HALF] = (-1.0) ** np.arange(WINDOW)
    inverse = forward[:, :BLOCK].T
    at = np.arange(taps)[None, :] + PAD - taps // 2
    scale = np.full((HALF, 1), 2.0 / WINDOW)
    scale[0] = 1.0 / WINDOW
    real, imag = np.cos(freq * at) * scale, np.sin(freq * at) * scale
    last = real.copy()
    last[0] = (-1.0) ** at[0] / WINDOW
    return forward, inverse, np.concatenate([real, imag, last])


def sigmoid(v):
    return 0.5 + 0.5 * jnp.tanh(0.5 * v)


def layer_body(entry, kinds, fresh_slot, recvs, spare, base, flags, *refs):
    refs = list(refs)
    fresh = refs.pop(0) if fresh_slot is not None else None
    recv = [refs.pop(0) for _ in range(recvs)]
    sources = [[refs.pop(0) for _ in range(count)] for _, _, count in kinds]
    starts = refs.pop(0)
    k_refs = [refs.pop(0) for _ in kinds]
    forward, inverse = refs.pop(0), refs.pop(0)
    del refs[:spare]
    out_ref, mark_ref, normed, wbuf, glu, w_sem = (refs.pop(0) for _ in range(6))
    x_ref, x_sem = refs if refs else (recv[0], None)
    chunks, width, part = wbuf.shape
    part = part // 2
    frames = x_ref.shape[0]
    valid = flags[entry, 0]
    turn = flags[entry, 1]

    def weight_copies(kind, source, j, side):
        target, sem = wbuf.at[j, :, pl.ds(side * part, part)], w_sem.at[j]
        cols = pl.ds(pl.multiple_of(side * width + j * part, part), part)
        if kind == "rows":
            return [pltpu.make_async_copy(source[0].at[:, cols], target, sem)]
        copies = []
        for i, piece in enumerate(source):
            size = piece.shape[0]
            place = pl.ds(pl.multiple_of(starts[i], size), size)
            into = wbuf.at[j, place, pl.ds(side * part, part)]
            copies.append(pltpu.make_async_copy(piece.at[:, cols], into, sem))
        return copies

    def start_weights(j):
        def issue(kind, source):
            for side in range(2):
                for copy in weight_copies(kind, source, j, side):
                    copy.start()

        for (which, kind, _), source in zip(kinds, sources):
            if len(kinds) == 1:
                issue(kind, source)
            else:
                pl.when(turn == which)(functools.partial(issue, kind, source))

    def wait_weights(j):
        pltpu.make_async_copy(wbuf.at[j], wbuf.at[j], w_sem.at[j]).wait()

    def project(j, slot):
        both = jnp.dot(normed[...], wbuf[j], preferred_element_type=jnp.float32)
        gated = both[:, :part] * sigmoid(both[:, part:])
        glu[slot, PAD : PAD + frames, :] = gated.astype(jnp.bfloat16)

    def taps(i, cols):
        rows = slice(HALF * i, HALF * (i + 1))
        chosen = k_refs[0][rows, cols]
        for (which, _, _), k_ref in zip(kinds[1:], k_refs[1:]):
            chosen = jnp.where(turn == which, k_ref[rows, cols], chosen)
        return chosen

    def mix(j, slot):
        cols = pl.ds(pl.multiple_of(j * part, part), part)
        real, imag, last = (taps(i, cols) for i in range(3))
        for row in range(0, frames, BLOCK):
            window = glu[slot, row : row + WINDOW, :]
            freq = jnp.dot(forward[...], window, preferred_element_type=jnp.float32)
            up, low = freq[:HALF], freq[HALF:]
            freq = jnp.concatenate([up * real - low * imag, up * imag + low * last], axis=0)
            conv = jnp.dot(
                inverse[...], freq.astype(jnp.bfloat16), preferred_element_type=jnp.float32
            )
            base = x_ref[row : row + BLOCK, cols].astype(jnp.float32)
            out_ref[row : row + BLOCK, cols] = (base + conv * sigmoid(conv)).astype(jnp.bfloat16)

    @pl.when(valid == 1)
    def _():
        ahead = min(3, chunks)
        if x_sem is not None:
            options = ([] if fresh is None else [fresh.at[fresh_slot]]) + recv
            first = base
            for i, option in enumerate(options):

                @pl.when(flags[entry, 2] == first + i)
                def _(option=option):
                    pltpu.make_async_copy(option, x_ref, x_sem).start()

        for j in range(ahead):
            start_weights(j)
        zeros = jnp.zeros((2, PAD, part), jnp.bfloat16)
        glu[:, 0:PAD, :] = zeros
        glu[:, PAD + frames :, :] = zeros
        if x_sem is not None:
            pltpu.make_async_copy(x_ref, x_ref, x_sem).wait()
        for row in range(0, frames, 64):
            values = x_ref[row : row + 64, :].astype(jnp.float32)
            center = jnp.mean(values, axis=1, keepdims=True)
            moved = values - center
            spread = jnp.mean(moved * moved, axis=1, keepdims=True)
            normed[row : row + 64, :] = (moved * lax.rsqrt(spread + 1e-05)).astype(jnp.bfloat16)
        wait_weights(0)
        project(0, 0)

        @pl.loop(0, chunks - 1)
        def _(j):
            wait_weights(j + 1)

            @pl.when(j + ahead < chunks)
            def _():
                start_weights(j + ahead)

            mix(j, j % 2)
            project(j + 1, (j + 1) % 2)

        mix(chunks - 1, (chunks - 1) % 2)

    mark_ref[...] = jnp.zeros(mark_ref.shape, mark_ref.dtype)


def layer(
    entry, flags, fresh, fresh_slot, recvs, weights, starts, kernels, matrices, spare=(), base=0
):
    frames, width = recvs[0].shape if recvs else fresh.shape[1:]
    part = 256
    chunks = width // part
    anywhere = pl.BlockSpec(memory_space=pl.ANY)
    local = pl.BlockSpec(memory_space=pltpu.VMEM)
    smem = pl.BlockSpec(memory_space=pltpu.SMEM)
    select = fresh_slot is not None or len(recvs) > 1
    operands, specs = [flags], [smem]
    if fresh_slot is not None:
        operands.append(fresh)
        specs.append(anywhere)
    operands += recvs
    specs += [anywhere if select else local] * len(recvs)
    for _, _, arrays in weights:
        operands += arrays
        specs += [anywhere] * len(arrays)
    operands += [starts, *kernels, *matrices, *spare]
    specs += [smem] + [local] * (len(kernels) + len(matrices)) + [anywhere] * len(spare)
    scratch = [
        pltpu.VMEM((frames, width), jnp.bfloat16),
        pltpu.VMEM((chunks, width, 2 * part), jnp.bfloat16),
        pltpu.VMEM((2, frames + 2 * PAD, part), jnp.bfloat16),
        pltpu.SemaphoreType.DMA((chunks,)),
    ]
    if select:
        scratch += [pltpu.VMEM((frames, width), jnp.bfloat16), pltpu.SemaphoreType.DMA]
    kinds = [(turn, kind, len(arrays)) for turn, kind, arrays in weights]
    return pl.pallas_call(
        functools.partial(
            layer_body, entry, kinds, fresh_slot, len(recvs), len(spare), base
        ),
        in_specs=specs,
        out_specs=[local, local],
        out_shape=[
            jax.ShapeDtypeStruct((frames, width), jnp.bfloat16),
            jax.ShapeDtypeStruct((8, LANES), jnp.float32),
        ],
        scratch_shapes=scratch,
        compiler_params=pltpu.CompilerParams(vmem_limit_bytes=VMEM_LIMIT),
        cost_estimate=pl.CostEstimate(
            flops=4 * frames * width * width, bytes_accessed=4 * width * width, transcendentals=0
        ),
        name="layer",
    )(*operands)


def transform_body(m_ref, k_ref, out_ref):
    total = jnp.dot(m_ref[0], k_ref[...], preferred_element_type=jnp.float32)
    for part in range(1, m_ref.shape[0]):
        total = total + jnp.dot(m_ref[part], k_ref[...], preferred_element_type=jnp.float32)
    out_ref[...] = total


def transformed(matrix, kernel):
    return pl.pallas_call(
        transform_body,
        out_shape=jax.ShapeDtypeStruct((matrix.shape[1], kernel.shape[1]), jnp.float32),
        compiler_params=pltpu.CompilerParams(vmem_limit_bytes=VMEM_LIMIT),
        name="transformed",
    )(matrix, kernel)


def unit_rows(values):
    return (values * lax.rsqrt(jnp.sum(values * values, axis=-1, keepdims=True) + 1e-06)).astype(
        jnp.bfloat16
    )


def target_body(wanted, flags, feats, w_tgt, *refs):
    out, feats_ref, w_ref, out_ref, sems = refs[-5:]

    @pl.when(flags[0, 4] == wanted)
    def _():
        load_w = pltpu.make_async_copy(w_tgt, w_ref, sems.at[0])
        load_x = pltpu.make_async_copy(feats, feats_ref, sems.at[1])
        load_w.start()
        load_x.start()
        load_w.wait()
        load_x.wait()

        @pl.loop(0, feats_ref.shape[0])
        def _(slot):
            out_ref[slot] = unit_rows(
                jnp.dot(feats_ref[slot], w_ref[...], preferred_element_type=jnp.float32)
            )

        back = pltpu.make_async_copy(out_ref, out, sems.at[2])
        back.start()
        back.wait()


def targets(flags, feats, w_tgt, wanted, spare, earlier=None):
    operands = [flags, feats, w_tgt, spare] + ([] if earlier is None else [earlier])
    anywhere = pl.BlockSpec(memory_space=pl.ANY)
    shape = feats.shape[:2] + w_tgt.shape[1:]
    return pl.pallas_call(
        functools.partial(target_body, wanted),
        in_specs=[pl.BlockSpec(memory_space=pltpu.SMEM)] + [anywhere] * (len(operands) - 1),
        out_specs=anywhere,
        out_shape=jax.ShapeDtypeStruct(shape, jnp.bfloat16),
        scratch_shapes=[
            pltpu.VMEM(feats.shape, jnp.bfloat16),
            pltpu.VMEM(w_tgt.shape, jnp.bfloat16),
            pltpu.VMEM(shape, jnp.bfloat16),
            pltpu.SemaphoreType.DMA((3,)),
        ],
        input_output_aliases={} if earlier is None else {4: 0},
        compiler_params=pltpu.CompilerParams(vmem_limit_bytes=VMEM_LIMIT),
        cost_estimate=pl.CostEstimate(
            flops=2 * feats.size * w_tgt.shape[1],
            bytes_accessed=2 * (feats.size + w_tgt.size),
            transcendentals=0,
        ),
        name="targets",
    )(*operands)


def loss_body(slot, count, flags, x_ref, w_ref, tgt_ref, pick_ref, out_ref):
    frames = x_ref.shape[0]

    @pl.when(flags[0, 3] == 1)
    def _():
        ctx = unit_rows(jnp.dot(x_ref[...], w_ref[...], preferred_element_type=jnp.float32))
        sims = lax.dot_general(
            ctx, tgt_ref[slot], (((1,), (1,)), ((), ())), preferred_element_type=jnp.float32
        )
        row = lax.broadcasted_iota(jnp.int32, sims.shape, 0)
        col = lax.broadcasted_iota(jnp.int32, sims.shape, 1)
        positive = jnp.sum(jnp.where(row == col, sims, 0.0), axis=1, keepdims=True) * 10.0
        picks = pick_ref[slot]
        lane = picks % LANES
        block = picks // LANES
        negative = jnp.zeros(picks.shape, jnp.float32)
        for part in range(frames // LANES):
            found = jnp.take_along_axis(sims[:, part * LANES : (part + 1) * LANES], lane, axis=1)
            negative = jnp.where(block == part, found, negative)
        place = lax.broadcasted_iota(jnp.int32, picks.shape, 1)
        terms = jnp.where(place < count, jnp.exp(negative * 10.0), 0.0)
        total = jnp.exp(positive) + jnp.sum(terms, axis=1, keepdims=True)
        wide = jnp.broadcast_to(jnp.log(total) - positive, (frames, LANES))
        out_ref[...] = wide.T[0:1, :]


def loss_rows(slot, flags, x, w_ctx, tgt, picks, count):
    frames = x.shape[0]
    whole = pl.BlockSpec(memory_space=pltpu.VMEM)
    return pl.pallas_call(
        functools.partial(loss_body, slot, count),
        in_specs=[pl.BlockSpec(memory_space=pltpu.SMEM)] + [whole] * 4,
        out_specs=whole,
        out_shape=jax.ShapeDtypeStruct((1, frames), jnp.float32),
        compiler_params=pltpu.CompilerParams(vmem_limit_bytes=VMEM_LIMIT),
        name="loss",
    )(flags, x, w_ctx, tgt, picks)


def swap(block, axis, mask):
    return lax.ppermute(block, axis, [(i, i ^ mask) for i in range(lax.axis_size(axis))])


def ring_pieces(block, axis):
    size = lax.axis_size(axis)
    pieces = [block]
    for far in range(1, size):
        route = [(i, (i + far) % size) for i in range(size)]
        pieces.insert(0, lax.ppermute(block, axis, route))
    return pieces


def in_order(pieces, axis):
    me = lax.axis_index(axis)
    size = lax.axis_size(axis)
    ring = jnp.concatenate(pieces + pieces[:-1], axis=0)
    rows = pieces[0].shape[0]
    return lax.dynamic_slice_in_dim(ring, (size - 1 - me) * rows, size * rows, 0)


def crossed(block, axis, beside):
    size = lax.axis_size(axis)
    me = lax.axis_index(axis)
    odd = me % 2
    ahead = [(i, i ^ (2 if i % 2 else 4)) for i in range(size)]
    other = [(i, i ^ (4 if i % 2 else 2)) for i in range(size)]
    near = lax.ppermute(block, axis, ahead)
    block, near, beside = lax.optimization_barrier((block, near, beside))
    far = lax.ppermute(near, axis, other)
    side = lax.ppermute(block, axis, other)
    first, second = 4 - 2 * odd, 2 + 2 * odd
    pieces = [block, near, side, far]
    masks = [0, first, second, 6]
    pieces += [swap(piece, axis, 1) for piece in pieces]
    masks += [1, second ^ 1, first ^ 1, 7]
    starts = jnp.stack([(me ^ mask) * block.shape[0] for mask in masks]).astype(jnp.int32)
    return pieces, starts, near, beside


def on_device(feats, w_in, dw_kernel, mask_embed, w_ctx, w_tgt, mask_starts, distractors):
    sections = lax.axis_size("section")
    section = lax.axis_index("section")
    micro = feats.shape[0]
    frames = feats.shape[2]
    repeats = w_in.shape[0]
    last = sections - 1
    feats_local = feats[:, 0]


    def work(step, s):
        offset = step - s
        if offset < 0:
            return None
        turn, slot = offset // sections, offset % sections
        return (turn, slot) if slot < micro and turn < repeats else None

    steps = repeats * sections + micro - 1
    plans = [[work(step, s) for s in range(sections)] for step in range(steps)]
    table = [
        [
            [
                int(plan[s] is not None),
                0 if plan[s] is None else plan[s][0],
                int(not (s == 0 and plan[s] is not None and plan[s][0] == 0)),
                int(s == last),
                0,
            ]
            for plan in plans + plans[:1]
        ]
        for s in range(sections)
    ]
    odd = lax.axis_index("fsdp") % 2
    flags = lax.dynamic_index_in_dim(jnp.array(table, jnp.int32), section, 0, keepdims=False)
    lanes = lax.broadcasted_iota(jnp.int32, flags.shape, 1)
    entries = lax.broadcasted_iota(jnp.int32, flags.shape, 0)
    off = (lanes == 0) & (((entries == 0) & (odd == 1)) | ((entries == steps) & (odd == 0)))
    flags = jnp.where(lanes == 4, odd, jnp.where(off, 0, flags))
    flags = jnp.where((entries == 1) & (lanes == 2) & (flags == 1), 1 + odd, flags)

    own = jnp.pad(dw_kernel[:, 0], ((0, 0), (0, -dw_kernel.shape[2] % 8), (0, 0)))
    own = jnp.transpose(own, (2, 0, 1))
    ring = ring_pieces(own.reshape(own.shape[0], -1), "fsdp")
    size = lax.axis_size("fsdp")
    if size == 8:
        pieces, starts, near, ring = crossed(w_in[0, 0], "fsdp", ring)
        kind = "pieces"
        w_late, near = lax.optimization_barrier((w_in, near))
        pieces[1] = near
    else:
        pieces = [lax.all_gather(w_in[0, 0], "fsdp", axis=0, tiled=True)]
        starts = jnp.zeros((1,), jnp.int32)
        kind = "rows"
        w_late = w_in
    spots = jnp.arange(frames, dtype=jnp.int32)
    begins = mask_starts[:, 0][:, :, None]
    covered = jnp.any(
        (spots[None, None, :] >= begins) & (spots[None, None, :] < begins + MASK_LEN), axis=1
    )
    masked_in = jnp.where(covered[:, :, None], mask_embed[None, None, :], feats_local)

    taps = dw_kernel.shape[2]
    full_k = in_order(ring, "fsdp").reshape(feats.shape[3], repeats, -1)
    full_k = jnp.transpose(full_k, (1, 2, 0))
    forward, inverse, rest = transforms(taps)
    rest = np.pad(rest, ((0, 0), (0, -taps % 8)))
    of_taps = []
    for _ in range(3):
        of_taps.append(rest.astype(ml_dtypes.bfloat16))
        rest = rest - of_taps[-1].astype(np.float64)
    of_taps = jnp.asarray(np.stack(of_taps))
    mats = (jnp.asarray(forward, jnp.bfloat16), jnp.asarray(inverse, jnp.bfloat16))
    kernels = [transformed(of_taps, full_k[turn]) for turn in range(repeats)]

    later = [w_late[turn, 0] for turn in range(1, repeats)]
    beside = (kernels, masked_in, flags, starts, mats, later)
    pieces, beside = lax.optimization_barrier((pieces, beside))
    kernels, masked_in, flags, starts, mats, later = beside

    def first_hop(block, parity):
        route = [(f, size + f) for f in range(parity, size, 2)]
        return lax.ppermute(block, ("section", "fsdp"), route)

    weights = [(0, kind, pieces)]
    for turn in range(1, repeats):
        rows = lax.all_gather(later[turn - 1], "fsdp", axis=0, tiled=True)
        weights.append((turn, "rows", [rows]))

    early, mark = layer(
        0, flags, masked_in, 0, [], weights[:1], starts, kernels[:1], mats
    )
    token = lax.ppermute(mark, "fsdp", [(i, i + 1) for i in range(0, size, 2)])
    early = first_hop(early, 0)
    tgt = targets(flags, feats_local, w_tgt, 1, token)
    result, mark = layer(
        steps, flags, masked_in, 0, [], weights[:1], starts, kernels[:1], mats, (tgt,)
    )
    state = [early, first_hop(result, 1)]
    count = distractors.shape[3]
    parts = []

    losses = []
    for step, plan in enumerate(plans):
        if step == 0:
            continue
        turns = sorted({item[0] for item in plan if item is not None})
        slot = plan[0][1] if plan[0] is not None and plan[0][0] == 0 else None
        used = [weights[turn] for turn in turns]
        k_used = [kernels[turn] for turn in turns]
        spare = ()
        if step <= last:
            picks, mark = lax.optimization_barrier((distractors[:, 0], mark))
            parts.append(lax.ppermute(picks, "section", [(step - 1, last)]))
            spare = (mark, parts[-1])
        if step == 2:
            tgt = targets(flags, feats_local, w_tgt, 0, mark, tgt)
            spare += (tgt,)
        result, mark = layer(
            step, flags, masked_in, slot, state, used, starts, k_used, mats, spare
        )
        if step == last:
            picks = jnp.concatenate(parts + [distractors[:, 0]], axis=1)
            picks = jnp.pad(picks, ((0, 0), (0, 0), (0, -count % LANES)))
        ends = plan[last]
        if ends is not None and ends[0] == repeats - 1:
            losses.append(loss_rows(ends[1], flags, result, w_ctx, tgt, picks, count))
        route = []
        for s, item in enumerate(plan):
            if item is not None and not (s == last and item[0] == repeats - 1):
                route.append((s, (s + 1) % sections))
        if route:
            state = [lax.ppermute(result, "section", route)]

    loss = jnp.concatenate(losses, axis=0)
    share = frames // sections
    mine = jnp.zeros((micro, share), jnp.float32)
    for s in range(sections):
        cut = loss[:, s * share : (s + 1) * share]
        if s == last:
            mine = mine + jnp.where(section == last, cut, 0.0)
        else:
            mine = mine + lax.ppermute(cut, "section", [(last, s)])
    return mine[:, None, :]


def solution(mesh):
    placed = (
        P(None, "fsdp", None, None),
        P(None, "section", "fsdp", None),
        P(None, "section", None, "fsdp"),
        P(),
        P(),
        P(),
        P(None, "fsdp", None),
        P(None, "fsdp", "section", None),
    )
    return jax.shard_map(
        on_device, mesh=mesh, in_specs=placed, out_specs=P(None, "fsdp", "section"), check_vma=False
    )
```

```python
import functools

import jax
import jax.numpy as jnp
import ml_dtypes
import numpy as np
from jax import lax
from jax.experimental import pallas as pl
from jax.experimental.pallas import tpu as pltpu
from jax.sharding import PartitionSpec as P

MASK_LEN = 10
LANES = 128
PAD = 16
VMEM_LIMIT = 20 * 1024 * 1024


BLOCK = 128
WINDOW = BLOCK + 2 * PAD
HALF = WINDOW // 2


def transforms(taps):
    freq = np.arange(HALF)[:, None] * (2 * np.pi / WINDOW)
    spot = np.arange(WINDOW)[None, :]
    forward = np.concatenate([np.cos(freq * spot), -np.sin(freq * spot)])
    forward[HALF] = (-1.0) ** np.arange(WINDOW)
    inverse = forward[:, :BLOCK].T
    at = np.arange(taps)[None, :] + PAD - taps // 2
    scale = np.full((HALF, 1), 2.0 / WINDOW)
    scale[0] = 1.0 / WINDOW
    real, imag = np.cos(freq * at) * scale, np.sin(freq * at) * scale
    last = real.copy()
    last[0] = (-1.0) ** at[0] / WINDOW
    return forward, inverse, np.concatenate([real, imag, last])


def sigmoid(v):
    return 0.5 + 0.5 * jnp.tanh(0.5 * v)


def layer_body(entry, kinds, fresh_slot, recvs, spare, base, flags, *refs):
    refs = list(refs)
    fresh = refs.pop(0) if fresh_slot is not None else None
    recv = [refs.pop(0) for _ in range(recvs)]
    sources = [[refs.pop(0) for _ in range(count)] for _, _, count in kinds]
    starts = refs.pop(0)
    k_refs = [refs.pop(0) for _ in kinds]
    forward, inverse = refs.pop(0), refs.pop(0)
    del refs[:spare]
    out_ref, mark_ref, normed, wbuf, glu, w_sem = (refs.pop(0) for _ in range(6))
    x_ref, x_sem = refs if refs else (recv[0], None)
    chunks, width, part = wbuf.shape
    part = part // 2
    frames = x_ref.shape[0]
    valid = flags[entry, 0]
    turn = flags[entry, 1]

    def weight_copies(kind, source, j, side):
        target, sem = wbuf.at[j, :, pl.ds(side * part, part)], w_sem.at[j]
        cols = pl.ds(pl.multiple_of(side * width + j * part, part), part)
        if kind == "rows":
            return [pltpu.make_async_copy(source[0].at[:, cols], target, sem)]
        copies = []
        for i, piece in enumerate(source):
            size = piece.shape[0]
            place = pl.ds(pl.multiple_of(starts[i], size), size)
            into = wbuf.at[j, place, pl.ds(side * part, part)]
            copies.append(pltpu.make_async_copy(piece.at[:, cols], into, sem))
        return copies

    def start_weights(j):
        def issue(kind, source):
            for side in range(2):
                for copy in weight_copies(kind, source, j, side):
                    copy.start()

        for (which, kind, _), source in zip(kinds, sources):
            if len(kinds) == 1:
                issue(kind, source)
            else:
                pl.when(turn == which)(functools.partial(issue, kind, source))

    def wait_weights(j):
        pltpu.make_async_copy(wbuf.at[j], wbuf.at[j], w_sem.at[j]).wait()

    def project(j, slot):
        both = jnp.dot(normed[...], wbuf[j], preferred_element_type=jnp.float32)
        gated = both[:, :part] * sigmoid(both[:, part:])
        glu[slot, PAD : PAD + frames, :] = gated.astype(jnp.bfloat16)

    def taps(i, cols):
        rows = slice(HALF * i, HALF * (i + 1))
        chosen = k_refs[0][rows, cols]
        for (which, _, _), k_ref in zip(kinds[1:], k_refs[1:]):
            chosen = jnp.where(turn == which, k_ref[rows, cols], chosen)
        return chosen

    def mix(j, slot):
        cols = pl.ds(pl.multiple_of(j * part, part), part)
        real, imag, last = (taps(i, cols) for i in range(3))
        for row in range(0, frames, BLOCK):
            window = glu[slot, row : row + WINDOW, :]
            freq = jnp.dot(forward[...], window, preferred_element_type=jnp.float32)
            up, low = freq[:HALF], freq[HALF:]
            freq = jnp.concatenate([up * real - low * imag, up * imag + low * last], axis=0)
            conv = jnp.dot(
                inverse[...], freq.astype(jnp.bfloat16), preferred_element_type=jnp.float32
            )
            base = x_ref[row : row + BLOCK, cols].astype(jnp.float32)
            out_ref[row : row + BLOCK, cols] = (base + conv * sigmoid(conv)).astype(jnp.bfloat16)

    @pl.when(valid == 1)
    def _():
        ahead = min(3, chunks)
        if x_sem is not None:
            options = ([] if fresh is None else [fresh.at[fresh_slot]]) + recv
            first = base
            for i, option in enumerate(options):

                @pl.when(flags[entry, 2] == first + i)
                def _(option=option):
                    pltpu.make_async_copy(option, x_ref, x_sem).start()

        for j in range(ahead):
            start_weights(j)
        zeros = jnp.zeros((2, PAD, part), jnp.bfloat16)
        glu[:, 0:PAD, :] = zeros
        glu[:, PAD + frames :, :] = zeros
        if x_sem is not None:
            pltpu.make_async_copy(x_ref, x_ref, x_sem).wait()
        for row in range(0, frames, 64):
            values = x_ref[row : row + 64, :].astype(jnp.float32)
            center = jnp.mean(values, axis=1, keepdims=True)
            moved = values - center
            spread = jnp.mean(moved * moved, axis=1, keepdims=True)
            normed[row : row + 64, :] = (moved * lax.rsqrt(spread + 1e-05)).astype(jnp.bfloat16)
        wait_weights(0)
        project(0, 0)

        @pl.loop(0, chunks - 1)
        def _(j):
            wait_weights(j + 1)

            @pl.when(j + ahead < chunks)
            def _():
                start_weights(j + ahead)

            mix(j, j % 2)
            project(j + 1, (j + 1) % 2)

        mix(chunks - 1, (chunks - 1) % 2)

    mark_ref[...] = jnp.zeros(mark_ref.shape, mark_ref.dtype)


def layer(
    entry, flags, fresh, fresh_slot, recvs, weights, starts, kernels, matrices, spare=(), base=0
):
    frames, width = recvs[0].shape if recvs else fresh.shape[1:]
    part = 256
    chunks = width // part
    anywhere = pl.BlockSpec(memory_space=pl.ANY)
    local = pl.BlockSpec(memory_space=pltpu.VMEM)
    smem = pl.BlockSpec(memory_space=pltpu.SMEM)
    select = fresh_slot is not None or len(recvs) > 1
    operands, specs = [flags], [smem]
    if fresh_slot is not None:
        operands.append(fresh)
        specs.append(anywhere)
    operands += recvs
    specs += [anywhere if select else local] * len(recvs)
    for _, _, arrays in weights:
        operands += arrays
        specs += [anywhere] * len(arrays)
    operands += [starts, *kernels, *matrices, *spare]
    specs += [smem] + [local] * (len(kernels) + len(matrices)) + [anywhere] * len(spare)
    scratch = [
        pltpu.VMEM((frames, width), jnp.bfloat16),
        pltpu.VMEM((chunks, width, 2 * part), jnp.bfloat16),
        pltpu.VMEM((2, frames + 2 * PAD, part), jnp.bfloat16),
        pltpu.SemaphoreType.DMA((chunks,)),
    ]
    if select:
        scratch += [pltpu.VMEM((frames, width), jnp.bfloat16), pltpu.SemaphoreType.DMA]
    kinds = [(turn, kind, len(arrays)) for turn, kind, arrays in weights]
    return pl.pallas_call(
        functools.partial(
            layer_body, entry, kinds, fresh_slot, len(recvs), len(spare), base
        ),
        in_specs=specs,
        out_specs=[local, local],
        out_shape=[
            jax.ShapeDtypeStruct((frames, width), jnp.bfloat16),
            jax.ShapeDtypeStruct((8, LANES), jnp.float32),
        ],
        scratch_shapes=scratch,
        compiler_params=pltpu.CompilerParams(vmem_limit_bytes=VMEM_LIMIT),
        cost_estimate=pl.CostEstimate(
            flops=4 * frames * width * width, bytes_accessed=4 * width * width, transcendentals=0
        ),
        name="layer",
    )(*operands)


def transform_body(m_ref, k_ref, out_ref):
    total = jnp.dot(m_ref[0], k_ref[...], preferred_element_type=jnp.float32)
    for part in range(1, m_ref.shape[0]):
        total = total + jnp.dot(m_ref[part], k_ref[...], preferred_element_type=jnp.float32)
    out_ref[...] = total


def transformed(matrix, kernel):
    return pl.pallas_call(
        transform_body,
        out_shape=jax.ShapeDtypeStruct((matrix.shape[1], kernel.shape[1]), jnp.float32),
        compiler_params=pltpu.CompilerParams(vmem_limit_bytes=VMEM_LIMIT),
        name="transformed",
    )(matrix, kernel)


def unit_rows(values):
    return (values * lax.rsqrt(jnp.sum(values * values, axis=-1, keepdims=True) + 1e-06)).astype(
        jnp.bfloat16
    )


def target_body(wanted, flags, feats, w_tgt, *refs):
    out, feats_ref, w_ref, out_ref, sems = refs[-5:]

    @pl.when(flags[0, 4] == wanted)
    def _():
        load_w = pltpu.make_async_copy(w_tgt, w_ref, sems.at[0])
        load_x = pltpu.make_async_copy(feats, feats_ref, sems.at[1])
        load_w.start()
        load_x.start()
        load_w.wait()
        load_x.wait()

        @pl.loop(0, feats_ref.shape[0])
        def _(slot):
            out_ref[slot] = unit_rows(
                jnp.dot(feats_ref[slot], w_ref[...], preferred_element_type=jnp.float32)
            )

        back = pltpu.make_async_copy(out_ref, out, sems.at[2])
        back.start()
        back.wait()


def targets(flags, feats, w_tgt, wanted, spare, earlier=None):
    operands = [flags, feats, w_tgt, spare] + ([] if earlier is None else [earlier])
    anywhere = pl.BlockSpec(memory_space=pl.ANY)
    shape = feats.shape[:2] + w_tgt.shape[1:]
    return pl.pallas_call(
        functools.partial(target_body, wanted),
        in_specs=[pl.BlockSpec(memory_space=pltpu.SMEM)] + [anywhere] * (len(operands) - 1),
        out_specs=anywhere,
        out_shape=jax.ShapeDtypeStruct(shape, jnp.bfloat16),
        scratch_shapes=[
            pltpu.VMEM(feats.shape, jnp.bfloat16),
            pltpu.VMEM(w_tgt.shape, jnp.bfloat16),
            pltpu.VMEM(shape, jnp.bfloat16),
            pltpu.SemaphoreType.DMA((3,)),
        ],
        input_output_aliases={} if earlier is None else {4: 0},
        compiler_params=pltpu.CompilerParams(vmem_limit_bytes=VMEM_LIMIT),
        cost_estimate=pl.CostEstimate(
            flops=2 * feats.size * w_tgt.shape[1],
            bytes_accessed=2 * (feats.size + w_tgt.size),
            transcendentals=0,
        ),
        name="targets",
    )(*operands)


def loss_body(slot, count, flags, x_ref, w_ref, tgt_ref, pick_ref, out_ref):
    frames = x_ref.shape[0]

    @pl.when(flags[0, 3] == 1)
    def _():
        ctx = unit_rows(jnp.dot(x_ref[...], w_ref[...], preferred_element_type=jnp.float32))
        sims = lax.dot_general(
            ctx, tgt_ref[slot], (((1,), (1,)), ((), ())), preferred_element_type=jnp.float32
        )
        row = lax.broadcasted_iota(jnp.int32, sims.shape, 0)
        col = lax.broadcasted_iota(jnp.int32, sims.shape, 1)
        positive = jnp.sum(jnp.where(row == col, sims, 0.0), axis=1, keepdims=True) * 10.0
        picks = pick_ref[slot]
        lane = picks % LANES
        block = picks // LANES
        negative = jnp.zeros(picks.shape, jnp.float32)
        for part in range(frames // LANES):
            found = jnp.take_along_axis(sims[:, part * LANES : (part + 1) * LANES], lane, axis=1)
            negative = jnp.where(block == part, found, negative)
        place = lax.broadcasted_iota(jnp.int32, picks.shape, 1)
        terms = jnp.where(place < count, jnp.exp(negative * 10.0), 0.0)
        total = jnp.exp(positive) + jnp.sum(terms, axis=1, keepdims=True)
        wide = jnp.broadcast_to(jnp.log(total) - positive, (frames, LANES))
        out_ref[...] = wide.T[0:1, :]


def loss_rows(slot, flags, x, w_ctx, tgt, picks, count):
    frames = x.shape[0]
    whole = pl.BlockSpec(memory_space=pltpu.VMEM)
    return pl.pallas_call(
        functools.partial(loss_body, slot, count),
        in_specs=[pl.BlockSpec(memory_space=pltpu.SMEM)] + [whole] * 4,
        out_specs=whole,
        out_shape=jax.ShapeDtypeStruct((1, frames), jnp.float32),
        compiler_params=pltpu.CompilerParams(vmem_limit_bytes=VMEM_LIMIT),
        name="loss",
    )(flags, x, w_ctx, tgt, picks)


def swap(block, axis, mask):
    return lax.ppermute(block, axis, [(i, i ^ mask) for i in range(lax.axis_size(axis))])


def chip_pieces(block, axis):
    size = lax.axis_size(axis)
    other = swap(block, axis, 1)
    odd = lax.axis_index(axis) % 2 == 1
    both = jnp.concatenate([jnp.where(odd, other, block), jnp.where(odd, block, other)], axis=0)
    return [swap(both, axis, mask) if mask else both for mask in range(0, size, 2)]


def in_order(pieces, axis):
    chip = lax.axis_index(axis) // 2
    mask = 1
    while mask < len(pieces):
        upper = chip // mask % 2 == 1
        pieces = [jnp.where(upper, pieces[i ^ mask], pieces[i]) for i in range(len(pieces))]
        mask *= 2
    return jnp.concatenate(pieces, axis=0)


def crossed(block, axis, small, prepare):
    size = lax.axis_size(axis)
    me = lax.axis_index(axis)
    odd = me % 2
    ahead = [(i, i ^ (2 if i % 2 else 4)) for i in range(size)]
    other = [(i, i ^ (4 if i % 2 else 2)) for i in range(size)]
    near = lax.ppermute(block, axis, ahead)
    block, near, small = lax.optimization_barrier((block, near, small))
    far = lax.ppermute(near, axis, other)
    side = lax.ppermute(block, axis, other)
    small = prepare(small)
    first, second = 4 - 2 * odd, 2 + 2 * odd
    pieces = [block, near, side, far]
    masks = [0, first, second, 6]
    pieces += [swap(piece, axis, 1) for piece in pieces]
    masks += [1, second ^ 1, first ^ 1, 7]
    starts = jnp.stack([(me ^ mask) * block.shape[0] for mask in masks]).astype(jnp.int32)
    return pieces, starts, small


def on_device(feats, w_in, dw_kernel, mask_embed, w_ctx, w_tgt, mask_starts, distractors):
    sections = lax.axis_size("section")
    section = lax.axis_index("section")
    size = lax.axis_size("fsdp")
    micro = feats.shape[0]
    frames = feats.shape[2]
    repeats = w_in.shape[0]
    last = sections - 1
    feats_local = feats[:, 0]


    def work(step, s):
        offset = step - s
        if offset < 0:
            return None
        turn, slot = offset // sections, offset % sections
        return (turn, slot) if slot < micro and turn < repeats else None

    steps = repeats * sections + micro - 1
    plans = [[work(step, s) for s in range(sections)] for step in range(steps)]
    table = [
        [
            [
                int(plan[s] is not None),
                0 if plan[s] is None else plan[s][0],
                int(not (s == 0 and plan[s] is not None and plan[s][0] == 0)),
                int(s == last),
                0,
            ]
            for plan in plans + plans[:1]
        ]
        for s in range(sections)
    ]
    odd = lax.axis_index("fsdp") % 2
    flags = lax.dynamic_index_in_dim(jnp.array(table, jnp.int32), section, 0, keepdims=False)
    lanes = lax.broadcasted_iota(jnp.int32, flags.shape, 1)
    entries = lax.broadcasted_iota(jnp.int32, flags.shape, 0)
    off = (lanes == 0) & (((entries == 0) & (odd == 1)) | ((entries == steps) & (odd == 0)))
    flags = jnp.where(lanes == 4, odd, jnp.where(off, 0, flags))
    middle = micro + 1
    split = (entries == 1) | (entries == middle + 1)
    flags = jnp.where(split & (lanes == 2) & (flags == 1), 1 + odd, flags)

    spots = jnp.arange(frames, dtype=jnp.int32)
    begins = mask_starts[:, 0][:, :, None]
    covered = jnp.any(
        (spots[None, None, :] >= begins) & (spots[None, None, :] < begins + MASK_LEN), axis=1
    )
    masked_in = jnp.where(covered[:, :, None], mask_embed[None, None, :], feats_local)

    taps = dw_kernel.shape[2]
    own = jnp.pad(dw_kernel[:, 0], ((0, 0), (0, -taps % 8), (0, 0)))
    own = jnp.transpose(own, (2, 0, 1))
    ring = chip_pieces(own.reshape(own.shape[0], -1), "fsdp")
    forward, inverse, rest = transforms(taps)
    rest = np.pad(rest, ((0, 0), (0, -taps % 8)))
    of_taps = []
    for _ in range(3):
        of_taps.append(rest.astype(ml_dtypes.bfloat16))
        rest = rest - of_taps[-1].astype(np.float64)
    of_taps = jnp.asarray(np.stack(of_taps))
    mats = (jnp.asarray(forward, jnp.bfloat16), jnp.asarray(inverse, jnp.bfloat16))

    def prepare(small):
        ring, w_late = small
        full_k = in_order(ring, "fsdp").reshape(feats.shape[3], repeats, -1)
        full_k = jnp.transpose(full_k, (1, 2, 0))
        kernels = [transformed(of_taps, full_k[turn]) for turn in range(repeats)]
        later = [w_late[turn, 0] for turn in range(1, repeats)]
        return kernels, masked_in, flags, mats, later

    small = (ring, w_in)
    if size == 8:
        pieces, starts, small = crossed(w_in[0, 0], "fsdp", small, prepare)
        kind = "pieces"
    else:
        pieces = [lax.all_gather(w_in[0, 0], "fsdp", axis=0, tiled=True)]
        starts = jnp.zeros((1,), jnp.int32)
        kind = "rows"
        small = prepare(small)
    pieces, (starts, small) = lax.optimization_barrier((pieces, (starts, small)))
    kernels, masked_in, flags, mats, later = small

    def hop_of(block, route, parity):
        route = [(a * size + f, b * size + f) for a, b in route for f in range(parity, size, 2)]
        return lax.ppermute(block, ("section", "fsdp"), route)

    weights = [(0, kind, pieces)]
    for turn in range(1, repeats):
        rows = lax.all_gather(later[turn - 1], "fsdp", axis=0, tiled=True)
        weights.append((turn, "rows", [rows]))

    early, mark = layer(
        0, flags, masked_in, 0, [], weights[:1], starts, kernels[:1], mats
    )
    token = lax.ppermute(mark, "fsdp", [(i, i + 1) for i in range(0, size, 2)])
    early = hop_of(early, [(0, 1)], 0)
    tgt = targets(flags, feats_local, w_tgt, 1, token)
    result, mark = layer(
        steps, flags, masked_in, 0, [], weights[:1], starts, kernels[:1], mats, (tgt,)
    )
    state = [early, hop_of(result, [(0, 1)], 1)]
    count = distractors.shape[3]
    parts = []

    losses = []
    for step, plan in enumerate(plans):
        if step == 0:
            continue
        turns = sorted({item[0] for item in plan if item is not None})
        slot = plan[0][1] if plan[0] is not None and plan[0][0] == 0 else None
        used = [weights[turn] for turn in turns]
        k_used = [kernels[turn] for turn in turns]
        spare = ()
        if step <= last:
            picks, mark = lax.optimization_barrier((distractors[:, 0], mark))
            parts.append(lax.ppermute(picks, "section", [(step - 1, last)]))
            spare = (mark, parts[-1])
        if step == 2:
            tgt = targets(flags, feats_local, w_tgt, 0, mark, tgt)
            spare += (tgt,)
        base = 0
        if step == middle + 1:
            spare, base = (token,), 1
        result, mark = layer(
            step, flags, masked_in, slot, state, used, starts, k_used, mats, spare, base
        )
        if step == last:
            picks = jnp.concatenate(parts + [distractors[:, 0]], axis=1)
            picks = jnp.pad(picks, ((0, 0), (0, 0), (0, -count % LANES)))
        ends = plan[last]
        if ends is not None and ends[0] == repeats - 1:
            losses.append(loss_rows(ends[1], flags, result, w_ctx, tgt, picks, count))
        state = []
        route = []
        for s, item in enumerate(plan):
            if item is not None and not (s == last and item[0] == repeats - 1):
                route.append((s, (s + 1) % sections))
        if route and step == middle:
            state = [hop_of(result, route, 0)]
            token = lax.ppermute(
                state[0][:16, :LANES], "fsdp", [(i, i + 1) for i in range(0, size, 2)]
            )
            result, token = lax.optimization_barrier((result, token))
            state.append(hop_of(result, route, 1))
        elif route:
            state = [lax.ppermute(result, "section", route)]

    loss = jnp.concatenate(losses, axis=0)
    share = frames // sections
    mine = jnp.zeros((micro, share), jnp.float32)
    for s in range(sections):
        cut = loss[:, s * share : (s + 1) * share]
        if s == last:
            mine = mine + jnp.where(section == last, cut, 0.0)
        else:
            mine = mine + lax.ppermute(cut, "section", [(last, s)])
    return mine[:, None, :]


def solution(mesh):
    placed = (
        P(None, "fsdp", None, None),
        P(None, "section", "fsdp", None),
        P(None, "section", None, "fsdp"),
        P(),
        P(),
        P(),
        P(None, "fsdp", None),
        P(None, "fsdp", "section", None),
    )
    return jax.shard_map(
        on_device, mesh=mesh, in_specs=placed, out_specs=P(None, "fsdp", "section"), check_vma=False
    )
```

```python
import functools

import jax
import jax.numpy as jnp
import ml_dtypes
import numpy as np
from jax import lax
from jax.experimental import pallas as pl
from jax.experimental.pallas import tpu as pltpu
from jax.sharding import PartitionSpec as P

MASK_LEN = 10
LANES = 128
PAD = 16
VMEM_LIMIT = 20 * 1024 * 1024


BLOCK = 128
WINDOW = BLOCK + 2 * PAD
HALF = WINDOW // 2


def transforms(taps):
    freq = np.arange(HALF)[:, None] * (2 * np.pi / WINDOW)
    spot = np.arange(WINDOW)[None, :]
    forward = np.concatenate([np.cos(freq * spot), -np.sin(freq * spot)])
    forward[HALF] = (-1.0) ** np.arange(WINDOW)
    inverse = forward[:, :BLOCK].T
    at = np.arange(taps)[None, :] + PAD - taps // 2
    scale = np.full((HALF, 1), 2.0 / WINDOW)
    scale[0] = 1.0 / WINDOW
    real, imag = np.cos(freq * at) * scale, np.sin(freq * at) * scale
    last = real.copy()
    last[0] = (-1.0) ** at[0] / WINDOW
    return forward, inverse, np.concatenate([real, imag, last])


def sigmoid(v):
    return 0.5 + 0.5 * jnp.tanh(0.5 * v)


def layer_body(entry, kinds, fresh_slot, recvs, spare, base, flags, *refs):
    refs = list(refs)
    fresh = refs.pop(0) if fresh_slot is not None else None
    recv = [refs.pop(0) for _ in range(recvs)]
    sources = [[refs.pop(0) for _ in range(count)] for _, _, count in kinds]
    starts = refs.pop(0)
    k_refs = [refs.pop(0) for _ in kinds]
    forward, inverse = refs.pop(0), refs.pop(0)
    del refs[:spare]
    out_ref, mark_ref, normed, wbuf, glu, w_sem = (refs.pop(0) for _ in range(6))
    x_ref, x_sem = refs if refs else (recv[0], None)
    chunks, width, part = wbuf.shape
    part = part // 2
    frames = x_ref.shape[0]
    valid = flags[entry, 0]
    turn = flags[entry, 1]

    def weight_copies(kind, source, j, side):
        target, sem = wbuf.at[j, :, pl.ds(side * part, part)], w_sem.at[j]
        cols = pl.ds(pl.multiple_of(side * width + j * part, part), part)
        if kind == "rows":
            return [pltpu.make_async_copy(source[0].at[:, cols], target, sem)]
        copies = []
        for i, piece in enumerate(source):
            size = piece.shape[0]
            place = pl.ds(pl.multiple_of(starts[i], size), size)
            into = wbuf.at[j, place, pl.ds(side * part, part)]
            copies.append(pltpu.make_async_copy(piece.at[:, cols], into, sem))
        return copies

    def start_weights(j):
        def issue(kind, source):
            for side in range(2):
                for copy in weight_copies(kind, source, j, side):
                    copy.start()

        for (which, kind, _), source in zip(kinds, sources):
            if len(kinds) == 1:
                issue(kind, source)
            else:
                pl.when(turn == which)(functools.partial(issue, kind, source))

    def wait_weights(j):
        pltpu.make_async_copy(wbuf.at[j], wbuf.at[j], w_sem.at[j]).wait()

    def project(j, slot):
        both = jnp.dot(normed[...], wbuf[j], preferred_element_type=jnp.float32)
        gated = both[:, :part] * sigmoid(both[:, part:])
        glu[slot, PAD : PAD + frames, :] = gated.astype(jnp.bfloat16)

    def taps(i, cols):
        rows = slice(HALF * i, HALF * (i + 1))
        chosen = k_refs[0][rows, cols]
        for (which, _, _), k_ref in zip(kinds[1:], k_refs[1:]):
            chosen = jnp.where(turn == which, k_ref[rows, cols], chosen)
        return chosen

    def mix(j, slot):
        cols = pl.ds(pl.multiple_of(j * part, part), part)
        real, imag, last = (taps(i, cols) for i in range(3))
        for row in range(0, frames, BLOCK):
            window = glu[slot, row : row + WINDOW, :]
            freq = jnp.dot(forward[...], window, preferred_element_type=jnp.float32)
            up, low = freq[:HALF], freq[HALF:]
            freq = jnp.concatenate([up * real - low * imag, up * imag + low * last], axis=0)
            conv = jnp.dot(
                inverse[...], freq.astype(jnp.bfloat16), preferred_element_type=jnp.float32
            )
            base = x_ref[row : row + BLOCK, cols].astype(jnp.float32)
            out_ref[row : row + BLOCK, cols] = (base + conv * sigmoid(conv)).astype(jnp.bfloat16)

    @pl.when(valid == 1)
    def _():
        ahead = min(3, chunks)
        if x_sem is not None:
            options = ([] if fresh is None else [fresh.at[fresh_slot]]) + recv
            first = base
            for i, option in enumerate(options):

                @pl.when(flags[entry, 2] == first + i)
                def _(option=option):
                    pltpu.make_async_copy(option, x_ref, x_sem).start()

        for j in range(ahead):
            start_weights(j)
        zeros = jnp.zeros((2, PAD, part), jnp.bfloat16)
        glu[:, 0:PAD, :] = zeros
        glu[:, PAD + frames :, :] = zeros
        if x_sem is not None:
            pltpu.make_async_copy(x_ref, x_ref, x_sem).wait()
        for row in range(0, frames, 64):
            values = x_ref[row : row + 64, :].astype(jnp.float32)
            center = jnp.mean(values, axis=1, keepdims=True)
            moved = values - center
            spread = jnp.mean(moved * moved, axis=1, keepdims=True)
            normed[row : row + 64, :] = (moved * lax.rsqrt(spread + 1e-05)).astype(jnp.bfloat16)
        wait_weights(0)
        project(0, 0)

        @pl.loop(0, chunks - 1)
        def _(j):
            wait_weights(j + 1)

            @pl.when(j + ahead < chunks)
            def _():
                start_weights(j + ahead)

            mix(j, j % 2)
            project(j + 1, (j + 1) % 2)

        mix(chunks - 1, (chunks - 1) % 2)

    mark_ref[...] = jnp.zeros(mark_ref.shape, mark_ref.dtype)


def layer(
    entry, flags, fresh, fresh_slot, recvs, weights, starts, kernels, matrices, spare=(), base=0,
    outside=False,
):
    frames, width = recvs[0].shape if recvs else fresh.shape[1:]
    part = 256
    chunks = width // part
    anywhere = pl.BlockSpec(memory_space=pl.ANY)
    local = pl.BlockSpec(memory_space=pltpu.VMEM)
    smem = pl.BlockSpec(memory_space=pltpu.SMEM)
    far = pl.BlockSpec(memory_space=pltpu.HBM)
    select = fresh_slot is not None or len(recvs) > 1 or outside
    operands, specs = [flags], [smem]
    if fresh_slot is not None:
        operands.append(fresh)
        specs.append(far)
    operands += recvs
    specs += [far if outside else anywhere if select else local] * len(recvs)
    for _, kind, arrays in weights:
        operands += arrays
        specs += [far if kind == "rows" else anywhere] * len(arrays)
    operands += [starts, *kernels, *matrices, *spare]
    specs += [smem] + [local] * (len(kernels) + len(matrices)) + [anywhere] * len(spare)
    scratch = [
        pltpu.VMEM((frames, width), jnp.bfloat16),
        pltpu.VMEM((chunks, width, 2 * part), jnp.bfloat16),
        pltpu.VMEM((2, frames + 2 * PAD, part), jnp.bfloat16),
        pltpu.SemaphoreType.DMA((chunks,)),
    ]
    if select:
        scratch += [pltpu.VMEM((frames, width), jnp.bfloat16), pltpu.SemaphoreType.DMA]
    kinds = [(turn, kind, len(arrays)) for turn, kind, arrays in weights]
    return pl.pallas_call(
        functools.partial(
            layer_body, entry, kinds, fresh_slot, len(recvs), len(spare), base
        ),
        in_specs=specs,
        out_specs=[local, local],
        out_shape=[
            jax.ShapeDtypeStruct((frames, width), jnp.bfloat16),
            jax.ShapeDtypeStruct((8, LANES), jnp.float32),
        ],
        scratch_shapes=scratch,
        compiler_params=pltpu.CompilerParams(vmem_limit_bytes=VMEM_LIMIT),
        cost_estimate=pl.CostEstimate(
            flops=4 * frames * width * width, bytes_accessed=4 * width * width, transcendentals=0
        ),
        name="layer",
    )(*operands)


def transform_body(m_ref, k_ref, out_ref):
    total = jnp.dot(m_ref[0], k_ref[...], preferred_element_type=jnp.float32)
    for part in range(1, m_ref.shape[0]):
        total = total + jnp.dot(m_ref[part], k_ref[...], preferred_element_type=jnp.float32)
    out_ref[...] = total


def transformed(matrix, kernel):
    return pl.pallas_call(
        transform_body,
        out_shape=jax.ShapeDtypeStruct((matrix.shape[1], kernel.shape[1]), jnp.float32),
        compiler_params=pltpu.CompilerParams(vmem_limit_bytes=VMEM_LIMIT),
        name="transformed",
    )(matrix, kernel)


def unit_rows(values):
    return (values * lax.rsqrt(jnp.sum(values * values, axis=-1, keepdims=True) + 1e-06)).astype(
        jnp.bfloat16
    )


def target_body(wanted, flags, feats, w_tgt, *refs):
    out, feats_ref, w_ref, out_ref, sems = refs[-5:]

    @pl.when(flags[0, 4] == wanted)
    def _():
        load_w = pltpu.make_async_copy(w_tgt, w_ref, sems.at[0])
        load_x = pltpu.make_async_copy(feats, feats_ref, sems.at[1])
        load_w.start()
        load_x.start()
        load_w.wait()
        load_x.wait()

        @pl.loop(0, feats_ref.shape[0])
        def _(slot):
            out_ref[slot] = unit_rows(
                jnp.dot(feats_ref[slot], w_ref[...], preferred_element_type=jnp.float32)
            )

        back = pltpu.make_async_copy(out_ref, out, sems.at[2])
        back.start()
        back.wait()


def targets(flags, feats, w_tgt, wanted, spare, earlier=None):
    operands = [flags, feats, w_tgt, spare] + ([] if earlier is None else [earlier])
    anywhere = pl.BlockSpec(memory_space=pl.ANY)
    shape = feats.shape[:2] + w_tgt.shape[1:]
    return pl.pallas_call(
        functools.partial(target_body, wanted),
        in_specs=[pl.BlockSpec(memory_space=pltpu.SMEM)] + [anywhere] * (len(operands) - 1),
        out_specs=anywhere,
        out_shape=jax.ShapeDtypeStruct(shape, jnp.bfloat16),
        scratch_shapes=[
            pltpu.VMEM(feats.shape, jnp.bfloat16),
            pltpu.VMEM(w_tgt.shape, jnp.bfloat16),
            pltpu.VMEM(shape, jnp.bfloat16),
            pltpu.SemaphoreType.DMA((3,)),
        ],
        input_output_aliases={} if earlier is None else {4: 0},
        compiler_params=pltpu.CompilerParams(vmem_limit_bytes=VMEM_LIMIT),
        cost_estimate=pl.CostEstimate(
            flops=2 * feats.size * w_tgt.shape[1],
            bytes_accessed=2 * (feats.size + w_tgt.size),
            transcendentals=0,
        ),
        name="targets",
    )(*operands)


def loss_body(slot, count, flags, x_ref, w_ref, tgt_ref, pick_ref, out_ref):
    frames = x_ref.shape[0]

    @pl.when(flags[0, 3] == 1)
    def _():
        ctx = unit_rows(jnp.dot(x_ref[...], w_ref[...], preferred_element_type=jnp.float32))
        sims = lax.dot_general(
            ctx, tgt_ref[slot], (((1,), (1,)), ((), ())), preferred_element_type=jnp.float32
        )
        row = lax.broadcasted_iota(jnp.int32, sims.shape, 0)
        col = lax.broadcasted_iota(jnp.int32, sims.shape, 1)
        positive = jnp.sum(jnp.where(row == col, sims, 0.0), axis=1, keepdims=True) * 10.0
        picks = pick_ref[slot]
        lane = picks % LANES
        block = picks // LANES
        negative = jnp.zeros(picks.shape, jnp.float32)
        for part in range(frames // LANES):
            found = jnp.take_along_axis(sims[:, part * LANES : (part + 1) * LANES], lane, axis=1)
            negative = jnp.where(block == part, found, negative)
        place = lax.broadcasted_iota(jnp.int32, picks.shape, 1)
        terms = jnp.where(place < count, jnp.exp(negative * 10.0), 0.0)
        total = jnp.exp(positive) + jnp.sum(terms, axis=1, keepdims=True)
        wide = jnp.broadcast_to(jnp.log(total) - positive, (frames, LANES))
        out_ref[...] = wide.T[0:1, :]


def loss_rows(slot, flags, x, w_ctx, tgt, picks, count):
    frames = x.shape[0]
    whole = pl.BlockSpec(memory_space=pltpu.VMEM)
    return pl.pallas_call(
        functools.partial(loss_body, slot, count),
        in_specs=[pl.BlockSpec(memory_space=pltpu.SMEM)] + [whole] * 4,
        out_specs=whole,
        out_shape=jax.ShapeDtypeStruct((1, frames), jnp.float32),
        compiler_params=pltpu.CompilerParams(vmem_limit_bytes=VMEM_LIMIT),
        name="loss",
    )(flags, x, w_ctx, tgt, picks)


def swap(block, axis, mask):
    return lax.ppermute(block, axis, [(i, i ^ mask) for i in range(lax.axis_size(axis))])


def chip_pieces(block, axis):
    size = lax.axis_size(axis)
    other = swap(block, axis, 1)
    odd = lax.axis_index(axis) % 2 == 1
    both = jnp.concatenate([jnp.where(odd, other, block), jnp.where(odd, block, other)], axis=0)
    return [swap(both, axis, mask) if mask else both for mask in range(0, size, 2)]


def in_order(pieces, axis):
    chip = lax.axis_index(axis) // 2
    mask = 1
    while mask < len(pieces):
        upper = chip // mask % 2 == 1
        pieces = [jnp.where(upper, pieces[i ^ mask], pieces[i]) for i in range(len(pieces))]
        mask *= 2
    return jnp.concatenate(pieces, axis=0)


def crossed(block, axis, small, prepare):
    size = lax.axis_size(axis)
    me = lax.axis_index(axis)
    odd = me % 2
    ahead = [(i, i ^ (2 if i % 2 else 4)) for i in range(size)]
    other = [(i, i ^ (4 if i % 2 else 2)) for i in range(size)]
    near = lax.ppermute(block, axis, ahead)
    block, near, small = lax.optimization_barrier((block, near, small))
    far = lax.ppermute(near, axis, other)
    side = lax.ppermute(block, axis, other)
    small = prepare(small)
    first, second = 4 - 2 * odd, 2 + 2 * odd
    pieces = [block, near, side, far]
    masks = [0, first, second, 6]
    pieces += [swap(piece, axis, 1) for piece in pieces]
    masks += [1, second ^ 1, first ^ 1, 7]
    starts = jnp.stack([(me ^ mask) * block.shape[0] for mask in masks]).astype(jnp.int32)
    return pieces, starts, small


def on_device(feats, w_in, dw_kernel, mask_embed, w_ctx, w_tgt, mask_starts, distractors):
    sections = lax.axis_size("section")
    section = lax.axis_index("section")
    size = lax.axis_size("fsdp")
    micro = feats.shape[0]
    frames = feats.shape[2]
    repeats = w_in.shape[0]
    last = sections - 1
    feats_local = feats[:, 0]


    def work(step, s):
        offset = step - s
        if offset < 0:
            return None
        turn, slot = offset // sections, offset % sections
        return (turn, slot) if slot < micro and turn < repeats else None

    steps = repeats * sections + micro - 1
    plans = [[work(step, s) for s in range(sections)] for step in range(steps)]
    table = [
        [
            [
                int(plan[s] is not None),
                0 if plan[s] is None else plan[s][0],
                int(not (s == 0 and plan[s] is not None and plan[s][0] == 0)),
                int(s == last),
                0,
            ]
            for plan in plans + plans[:1]
        ]
        for s in range(sections)
    ]
    odd = lax.axis_index("fsdp") % 2
    flags = lax.dynamic_index_in_dim(jnp.array(table, jnp.int32), section, 0, keepdims=False)
    lanes = lax.broadcasted_iota(jnp.int32, flags.shape, 1)
    entries = lax.broadcasted_iota(jnp.int32, flags.shape, 0)
    off = (lanes == 0) & (((entries == 0) & (odd == 1)) | ((entries == steps) & (odd == 0)))
    flags = jnp.where(lanes == 4, odd, jnp.where(off, 0, flags))
    middle = micro + 1
    split = (entries == 1) | (entries == middle + 1)
    flags = jnp.where(split & (lanes == 2) & (flags == 1), 1 + odd, flags)

    spots = jnp.arange(frames, dtype=jnp.int32)
    begins = mask_starts[:, 0][:, :, None]
    covered = jnp.any(
        (spots[None, None, :] >= begins) & (spots[None, None, :] < begins + MASK_LEN), axis=1
    )
    masked_in = jnp.where(covered[:, :, None], mask_embed[None, None, :], feats_local)

    taps = dw_kernel.shape[2]
    own = jnp.pad(dw_kernel[:, 0], ((0, 0), (0, -taps % 8), (0, 0)))
    own = jnp.transpose(own, (2, 0, 1))
    ring = chip_pieces(own.reshape(own.shape[0], -1), "fsdp")
    forward, inverse, rest = transforms(taps)
    rest = np.pad(rest, ((0, 0), (0, -taps % 8)))
    of_taps = []
    for _ in range(3):
        of_taps.append(rest.astype(ml_dtypes.bfloat16))
        rest = rest - of_taps[-1].astype(np.float64)
    of_taps = jnp.asarray(np.stack(of_taps))
    mats = (jnp.asarray(forward, jnp.bfloat16), jnp.asarray(inverse, jnp.bfloat16))

    def prepare(small):
        ring, w_late = small
        full_k = in_order(ring, "fsdp").reshape(feats.shape[3], repeats, -1)
        full_k = jnp.transpose(full_k, (1, 2, 0))
        kernels = [transformed(of_taps, full_k[0])] + [full_k[turn] for turn in range(1, repeats)]
        later = [w_late[turn, 0] for turn in range(1, repeats)]
        return kernels, masked_in, flags, mats, later

    small = (ring, w_in)
    if size == 8:
        pieces, starts, small = crossed(w_in[0, 0], "fsdp", small, prepare)
        kind = "pieces"
    else:
        pieces = [lax.all_gather(w_in[0, 0], "fsdp", axis=0, tiled=True)]
        starts = jnp.zeros((1,), jnp.int32)
        kind = "rows"
        small = prepare(small)
    pieces, (starts, small) = lax.optimization_barrier((pieces, (starts, small)))
    kernels, masked_in, flags, mats, later = small

    def hop_of(block, route, parity):
        route = [(a * size + f, b * size + f) for a, b in route for f in range(parity, size, 2)]
        return lax.ppermute(block, ("section", "fsdp"), route)

    weights = [(0, kind, pieces)]
    for turn in range(1, repeats):
        rows = lax.all_gather(later[turn - 1], "fsdp", axis=0, tiled=True)
        weights.append((turn, "rows", [rows]))

    early, mark = layer(
        0, flags, masked_in, 0, [], weights[:1], starts, kernels[:1], mats
    )
    token = lax.ppermute(mark, "fsdp", [(i, i + 1) for i in range(0, size, 2)])
    early = hop_of(early, [(0, 1)], 0)
    tgt = targets(flags, feats_local, w_tgt, 1, token)
    result, mark = layer(
        steps, flags, masked_in, 0, [], weights[:1], starts, kernels[:1], mats, (tgt,)
    )
    state = [early, hop_of(result, [(0, 1)], 1)]
    count = distractors.shape[3]
    parts = []

    losses = []
    for step, plan in enumerate(plans):
        if step == 0:
            continue
        turns = sorted({item[0] for item in plan if item is not None})
        slot = plan[0][1] if plan[0] is not None and plan[0][0] == 0 else None
        used = [weights[turn] for turn in turns]
        k_used = [kernels[turn] for turn in turns]
        spare = ()
        if step <= last:
            picks, mark = lax.optimization_barrier((distractors[:, 0], mark))
            parts.append(lax.ppermute(picks, "section", [(step - 1, last)]))
            spare = (mark, parts[-1])
        if step == 2:
            tgt = targets(flags, feats_local, w_tgt, 0, mark, tgt)
            spare += (tgt,)
        if step == micro:
            rows = [arrays for _, _, arrays in weights[1:]]
            kernels[1:], rows = lax.optimization_barrier((kernels[1:], rows))
            kernels[1:] = [transformed(of_taps, kernel) for kernel in kernels[1:]]
            weights[1:] = [(turn + 1, "rows", arrays) for turn, arrays in enumerate(rows)]
            used = [weights[turn] for turn in turns]
            k_used = [kernels[turn] for turn in turns]
        base = int(step == micro)
        if step == middle + 1:
            spare, base = (token,), 1
        result, mark = layer(
            step, flags, masked_in, slot, state, used, starts, k_used, mats, spare, base, step == micro
        )
        if step == last:
            picks = jnp.concatenate(parts + [distractors[:, 0]], axis=1)
            picks = jnp.pad(picks, ((0, 0), (0, 0), (0, -count % LANES)))
        ends = plan[last]
        if ends is not None and ends[0] == repeats - 1:
            losses.append(loss_rows(ends[1], flags, result, w_ctx, tgt, picks, count))
        state = []
        route = []
        for s, item in enumerate(plan):
            if item is not None and not (s == last and item[0] == repeats - 1):
                route.append((s, (s + 1) % sections))
        if route and step == middle:
            state = [hop_of(result, route, 0)]
            token = lax.ppermute(
                state[0][:16, :LANES], "fsdp", [(i, i + 1) for i in range(0, size, 2)]
            )
            result, token = lax.optimization_barrier((result, token))
            state.append(hop_of(result, route, 1))
        elif route:
            state = [lax.ppermute(result, "section", route)]

    loss = jnp.concatenate(losses, axis=0)
    share = frames // sections
    mine = jnp.zeros((micro, share), jnp.float32)
    for s in range(sections):
        cut = loss[:, s * share : (s + 1) * share]
        if s == last:
            mine = mine + jnp.where(section == last, cut, 0.0)
        else:
            mine = mine + lax.ppermute(cut, "section", [(last, s)])
    return mine[:, None, :]


def solution(mesh):
    placed = (
        P(None, "fsdp", None, None),
        P(None, "section", "fsdp", None),
        P(None, "section", None, "fsdp"),
        P(),
        P(),
        P(),
        P(None, "fsdp", None),
        P(None, "fsdp", "section", None),
    )
    return jax.shard_map(
        on_device, mesh=mesh, in_specs=placed, out_specs=P(None, "fsdp", "section"), check_vma=False
    )
```

```python
import functools

import jax
import jax.numpy as jnp
import ml_dtypes
import numpy as np
from jax import lax
from jax.experimental import pallas as pl
from jax.experimental.pallas import tpu as pltpu
from jax.sharding import PartitionSpec as P

MASK_LEN = 10
LANES = 128
PAD = 16
VMEM_LIMIT = 20 * 1024 * 1024
LATE_VMEM_LIMIT = 48 * 1024 * 1024


BLOCK = 128
WINDOW = BLOCK + 2 * PAD
HALF = WINDOW // 2


def transforms(taps):
    freq = np.arange(HALF)[:, None] * (2 * np.pi / WINDOW)
    spot = np.arange(WINDOW)[None, :]
    forward = np.concatenate([np.cos(freq * spot), -np.sin(freq * spot)])
    forward[HALF] = (-1.0) ** np.arange(WINDOW)
    inverse = forward[:, :BLOCK].T
    at = np.arange(taps)[None, :] + PAD - taps // 2
    scale = np.full((HALF, 1), 2.0 / WINDOW)
    scale[0] = 1.0 / WINDOW
    real, imag = np.cos(freq * at) * scale, np.sin(freq * at) * scale
    last = real.copy()
    last[0] = (-1.0) ** at[0] / WINDOW
    return forward, inverse, np.concatenate([real, imag, last])


def sigmoid(v):
    return 0.5 + 0.5 * jnp.tanh(0.5 * v)


def layer_body(entry, kinds, fresh_slot, recvs, spare, base, flags, *refs):
    refs = list(refs)
    fresh = refs.pop(0) if fresh_slot is not None else None
    recv = [refs.pop(0) for _ in range(recvs)]
    sources = [[refs.pop(0) for _ in range(count)] for _, _, count in kinds]
    starts = refs.pop(0)
    k_refs = [refs.pop(0) for _ in kinds]
    forward, inverse = refs.pop(0), refs.pop(0)
    del refs[:spare]
    out_ref, mark_ref, normed, wbuf, glu, w_sem = (refs.pop(0) for _ in range(6))
    x_ref, x_sem = refs if refs else (recv[0], None)
    chunks, width, part = wbuf.shape
    part = part // 2
    frames = x_ref.shape[0]
    valid = flags[entry, 0]
    turn = flags[entry, 1]

    def weight_copies(kind, source, j, side):
        target, sem = wbuf.at[j, :, pl.ds(side * part, part)], w_sem.at[j]
        cols = pl.ds(pl.multiple_of(side * width + j * part, part), part)
        if kind == "rows":
            return [pltpu.make_async_copy(source[0].at[:, cols], target, sem)]
        copies = []
        for i, piece in enumerate(source):
            size = piece.shape[0]
            place = pl.ds(pl.multiple_of(starts[i], size), size)
            into = wbuf.at[j, place, pl.ds(side * part, part)]
            copies.append(pltpu.make_async_copy(piece.at[:, cols], into, sem))
        return copies

    def start_weights(j):
        def issue(kind, source):
            for side in range(2):
                for copy in weight_copies(kind, source, j, side):
                    copy.start()

        for (which, kind, _), source in zip(kinds, sources):
            if len(kinds) == 1:
                issue(kind, source)
            else:
                pl.when(turn == which)(functools.partial(issue, kind, source))

    def wait_weights(j):
        pltpu.make_async_copy(wbuf.at[j], wbuf.at[j], w_sem.at[j]).wait()

    def project(j, slot):
        both = jnp.dot(normed[...], wbuf[j], preferred_element_type=jnp.float32)
        gated = both[:, :part] * sigmoid(both[:, part:])
        glu[slot, PAD : PAD + frames, :] = gated.astype(jnp.bfloat16)

    def taps(i, cols):
        rows = slice(HALF * i, HALF * (i + 1))
        chosen = k_refs[0][rows, cols]
        for (which, _, _), k_ref in zip(kinds[1:], k_refs[1:]):
            chosen = jnp.where(turn == which, k_ref[rows, cols], chosen)
        return chosen

    def mix(j, slot):
        cols = pl.ds(pl.multiple_of(j * part, part), part)
        real, imag, last = (taps(i, cols) for i in range(3))
        for row in range(0, frames, BLOCK):
            window = glu[slot, row : row + WINDOW, :]
            freq = jnp.dot(forward[...], window, preferred_element_type=jnp.float32)
            up, low = freq[:HALF], freq[HALF:]
            freq = jnp.concatenate([up * real - low * imag, up * imag + low * last], axis=0)
            conv = jnp.dot(
                inverse[...], freq.astype(jnp.bfloat16), preferred_element_type=jnp.float32
            )
            base = x_ref[row : row + BLOCK, cols].astype(jnp.float32)
            out_ref[row : row + BLOCK, cols] = (base + conv * sigmoid(conv)).astype(jnp.bfloat16)

    @pl.when(valid == 1)
    def _():
        ahead = min(3, chunks)
        if x_sem is not None:
            options = ([] if fresh is None else [fresh]) + recv
            first = base
            for i, option in enumerate(options):

                @pl.when(flags[entry, 2] == first + i)
                def _(option=option):
                    pltpu.make_async_copy(option, x_ref, x_sem).start()

        for j in range(ahead):
            start_weights(j)
        zeros = jnp.zeros((2, PAD, part), jnp.bfloat16)
        glu[:, 0:PAD, :] = zeros
        glu[:, PAD + frames :, :] = zeros
        if x_sem is not None:
            pltpu.make_async_copy(x_ref, x_ref, x_sem).wait()
        for row in range(0, frames, 64):
            values = x_ref[row : row + 64, :].astype(jnp.float32)
            center = jnp.mean(values, axis=1, keepdims=True)
            moved = values - center
            spread = jnp.mean(moved * moved, axis=1, keepdims=True)
            normed[row : row + 64, :] = (moved * lax.rsqrt(spread + 1e-05)).astype(jnp.bfloat16)
        wait_weights(0)
        project(0, 0)

        @pl.loop(0, chunks - 1)
        def _(j):
            wait_weights(j + 1)

            @pl.when(j + ahead < chunks)
            def _():
                start_weights(j + ahead)

            mix(j, j % 2)
            project(j + 1, (j + 1) % 2)

        mix(chunks - 1, (chunks - 1) % 2)

    mark_ref[...] = jnp.zeros(mark_ref.shape, mark_ref.dtype)


def layer(
    entry, flags, fresh, fresh_slot, recvs, weights, starts, kernels, matrices, spare=(), base=0,
    outside=False, limit=VMEM_LIMIT,
):
    frames, width = recvs[0].shape if recvs else fresh.shape
    part = 256
    chunks = width // part
    anywhere = pl.BlockSpec(memory_space=pl.ANY)
    local = pl.BlockSpec(memory_space=pltpu.VMEM)
    smem = pl.BlockSpec(memory_space=pltpu.SMEM)
    far = pl.BlockSpec(memory_space=pltpu.HBM)
    select = fresh_slot is not None or len(recvs) > 1 or outside
    operands, specs = [flags], [smem]
    if fresh_slot is not None:
        operands.append(fresh)
        specs.append(far)
    operands += recvs
    specs += [far if outside else anywhere if select else local] * len(recvs)
    for _, kind, arrays in weights:
        operands += arrays
        specs += [far if kind == "rows" else anywhere] * len(arrays)
    operands += [starts, *kernels, *matrices, *spare]
    specs += [smem] + [local] * (len(kernels) + len(matrices)) + [anywhere] * len(spare)
    scratch = [
        pltpu.VMEM((frames, width), jnp.bfloat16),
        pltpu.VMEM((chunks, width, 2 * part), jnp.bfloat16),
        pltpu.VMEM((2, frames + 2 * PAD, part), jnp.bfloat16),
        pltpu.SemaphoreType.DMA((chunks,)),
    ]
    if select:
        scratch += [pltpu.VMEM((frames, width), jnp.bfloat16), pltpu.SemaphoreType.DMA]
    kinds = [(turn, kind, len(arrays)) for turn, kind, arrays in weights]
    return pl.pallas_call(
        functools.partial(
            layer_body, entry, kinds, fresh_slot, len(recvs), len(spare), base
        ),
        in_specs=specs,
        out_specs=[local, local],
        out_shape=[
            jax.ShapeDtypeStruct((frames, width), jnp.bfloat16),
            jax.ShapeDtypeStruct((8, LANES), jnp.float32),
        ],
        scratch_shapes=scratch,
        compiler_params=pltpu.CompilerParams(vmem_limit_bytes=limit),
        cost_estimate=pl.CostEstimate(
            flops=4 * frames * width * width, bytes_accessed=4 * width * width, transcendentals=0
        ),
        name="layer",
    )(*operands)


def transform_body(m_ref, k_ref, out_ref):
    total = jnp.dot(m_ref[0], k_ref[...], preferred_element_type=jnp.float32)
    for part in range(1, m_ref.shape[0]):
        total = total + jnp.dot(m_ref[part], k_ref[...], preferred_element_type=jnp.float32)
    out_ref[...] = total


def transformed(matrix, kernel):
    return pl.pallas_call(
        transform_body,
        out_shape=jax.ShapeDtypeStruct((matrix.shape[1], kernel.shape[1]), jnp.float32),
        compiler_params=pltpu.CompilerParams(vmem_limit_bytes=VMEM_LIMIT),
        name="transformed",
    )(matrix, kernel)


def unit_rows(values):
    return (values * lax.rsqrt(jnp.sum(values * values, axis=-1, keepdims=True) + 1e-06)).astype(
        jnp.bfloat16
    )


def target_body(wanted, flags, feats, w_tgt, *refs):
    out, feats_ref, w_ref, out_ref, sems = refs[-5:]

    @pl.when(flags[0, 4] == wanted)
    def _():
        load_w = pltpu.make_async_copy(w_tgt, w_ref, sems.at[0])
        load_x = pltpu.make_async_copy(feats, feats_ref, sems.at[1])
        load_w.start()
        load_x.start()
        load_w.wait()
        load_x.wait()

        @pl.loop(0, feats_ref.shape[0])
        def _(slot):
            out_ref[slot] = unit_rows(
                jnp.dot(feats_ref[slot], w_ref[...], preferred_element_type=jnp.float32)
            )

        back = pltpu.make_async_copy(out_ref, out, sems.at[2])
        back.start()
        back.wait()


def targets(flags, feats, w_tgt, wanted, spare, earlier=None):
    operands = [flags, feats, w_tgt, spare] + ([] if earlier is None else [earlier])
    anywhere = pl.BlockSpec(memory_space=pl.ANY)
    shape = feats.shape[:2] + w_tgt.shape[1:]
    return pl.pallas_call(
        functools.partial(target_body, wanted),
        in_specs=[pl.BlockSpec(memory_space=pltpu.SMEM)] + [anywhere] * (len(operands) - 1),
        out_specs=anywhere,
        out_shape=jax.ShapeDtypeStruct(shape, jnp.bfloat16),
        scratch_shapes=[
            pltpu.VMEM(feats.shape, jnp.bfloat16),
            pltpu.VMEM(w_tgt.shape, jnp.bfloat16),
            pltpu.VMEM(shape, jnp.bfloat16),
            pltpu.SemaphoreType.DMA((3,)),
        ],
        input_output_aliases={} if earlier is None else {4: 0},
        compiler_params=pltpu.CompilerParams(vmem_limit_bytes=VMEM_LIMIT),
        cost_estimate=pl.CostEstimate(
            flops=2 * feats.size * w_tgt.shape[1],
            bytes_accessed=2 * (feats.size + w_tgt.size),
            transcendentals=0,
        ),
        name="targets",
    )(*operands)


def loss_body(slot, count, flags, x_ref, w_ref, tgt_ref, pick_ref, out_ref):
    frames = x_ref.shape[0]

    @pl.when(flags[0, 3] == 1)
    def _():
        ctx = unit_rows(jnp.dot(x_ref[...], w_ref[...], preferred_element_type=jnp.float32))
        sims = lax.dot_general(
            ctx, tgt_ref[slot], (((1,), (1,)), ((), ())), preferred_element_type=jnp.float32
        )
        row = lax.broadcasted_iota(jnp.int32, sims.shape, 0)
        col = lax.broadcasted_iota(jnp.int32, sims.shape, 1)
        positive = jnp.sum(jnp.where(row == col, sims, 0.0), axis=1, keepdims=True) * 10.0
        picks = pick_ref[slot]
        lane = picks % LANES
        block = picks // LANES
        negative = jnp.zeros(picks.shape, jnp.float32)
        for part in range(frames // LANES):
            found = jnp.take_along_axis(sims[:, part * LANES : (part + 1) * LANES], lane, axis=1)
            negative = jnp.where(block == part, found, negative)
        place = lax.broadcasted_iota(jnp.int32, picks.shape, 1)
        terms = jnp.where(place < count, jnp.exp(negative * 10.0), 0.0)
        total = jnp.exp(positive) + jnp.sum(terms, axis=1, keepdims=True)
        wide = jnp.broadcast_to(jnp.log(total) - positive, (frames, LANES))
        out_ref[...] = wide.T[0:1, :]


def loss_rows(slot, flags, x, w_ctx, tgt, picks, count):
    frames = x.shape[0]
    whole = pl.BlockSpec(memory_space=pltpu.VMEM)
    return pl.pallas_call(
        functools.partial(loss_body, slot, count),
        in_specs=[pl.BlockSpec(memory_space=pltpu.SMEM)] + [whole] * 4,
        out_specs=whole,
        out_shape=jax.ShapeDtypeStruct((1, frames), jnp.float32),
        compiler_params=pltpu.CompilerParams(vmem_limit_bytes=VMEM_LIMIT),
        name="loss",
    )(flags, x, w_ctx, tgt, picks)


def swap(block, axis, mask):
    return lax.ppermute(block, axis, [(i, i ^ mask) for i in range(lax.axis_size(axis))])


def chip_pieces(block, axis):
    size = lax.axis_size(axis)
    other = swap(block, axis, 1)
    odd = lax.axis_index(axis) % 2 == 1
    both = jnp.concatenate([jnp.where(odd, other, block), jnp.where(odd, block, other)], axis=0)
    return [swap(both, axis, mask) if mask else both for mask in range(0, size, 2)]


def in_order(pieces, axis):
    chip = lax.axis_index(axis) // 2
    mask = 1
    while mask < len(pieces):
        upper = chip // mask % 2 == 1
        pieces = [jnp.where(upper, pieces[i ^ mask], pieces[i]) for i in range(len(pieces))]
        mask *= 2
    return jnp.concatenate(pieces, axis=0)


def crossed(block, axis, small, prepare):
    size = lax.axis_size(axis)
    me = lax.axis_index(axis)
    odd = me % 2
    ahead = [(i, i ^ (2 if i % 2 else 4)) for i in range(size)]
    other = [(i, i ^ (4 if i % 2 else 2)) for i in range(size)]
    near = lax.ppermute(block, axis, ahead)
    block, near, small = lax.optimization_barrier((block, near, small))
    far = lax.ppermute(near, axis, other)
    side = lax.ppermute(block, axis, other)
    small = prepare(small)
    first, second = 4 - 2 * odd, 2 + 2 * odd
    pieces = [block, near, side, far]
    masks = [0, first, second, 6]
    pieces += [swap(piece, axis, 1) for piece in pieces]
    masks += [1, second ^ 1, first ^ 1, 7]
    starts = jnp.stack([(me ^ mask) * block.shape[0] for mask in masks]).astype(jnp.int32)
    return pieces, starts, small


def on_device(feats, w_in, dw_kernel, mask_embed, w_ctx, w_tgt, mask_starts, distractors):
    sections = lax.axis_size("section")
    section = lax.axis_index("section")
    size = lax.axis_size("fsdp")
    micro = feats.shape[0]
    frames = feats.shape[2]
    repeats = w_in.shape[0]
    last = sections - 1
    feats_local = feats[:, 0]


    def work(step, s):
        offset = step - s
        if offset < 0:
            return None
        turn, slot = offset // sections, offset % sections
        return (turn, slot) if slot < micro and turn < repeats else None

    steps = repeats * sections + micro - 1
    plans = [[work(step, s) for s in range(sections)] for step in range(steps)]
    table = [
        [
            [
                int(plan[s] is not None),
                0 if plan[s] is None else plan[s][0],
                int(not (s == 0 and plan[s] is not None and plan[s][0] == 0)),
                int(s == last),
                0,
            ]
            for plan in plans + plans[:1]
        ]
        for s in range(sections)
    ]
    odd = lax.axis_index("fsdp") % 2
    flags = lax.dynamic_index_in_dim(jnp.array(table, jnp.int32), section, 0, keepdims=False)
    lanes = lax.broadcasted_iota(jnp.int32, flags.shape, 1)
    entries = lax.broadcasted_iota(jnp.int32, flags.shape, 0)
    off = (lanes == 0) & (((entries == 0) & (odd == 1)) | ((entries == steps) & (odd == 0)))
    flags = jnp.where(lanes == 4, odd, jnp.where(off, 0, flags))
    middle = micro + 1
    split = (entries == 1) | (entries == middle + 1)
    flags = jnp.where(split & (lanes == 2) & (flags == 1), 1 + odd, flags)

    spots = jnp.arange(frames, dtype=jnp.int32)
    begins = mask_starts[:, 0][:, :, None]
    covered = jnp.any(
        (spots[None, None, :] >= begins) & (spots[None, None, :] < begins + MASK_LEN), axis=1
    )
    masked_in = [
        jnp.where(covered[slot][:, None], mask_embed[None, :], feats_local[slot])
        for slot in range(micro)
    ]

    taps = dw_kernel.shape[2]
    own = jnp.pad(dw_kernel[:, 0], ((0, 0), (0, -taps % 8), (0, 0)))
    own = jnp.transpose(own, (2, 0, 1))
    ring = chip_pieces(own.reshape(own.shape[0], -1), "fsdp")
    forward, inverse, rest = transforms(taps)
    rest = np.pad(rest, ((0, 0), (0, -taps % 8)))
    of_taps = []
    for _ in range(3):
        of_taps.append(rest.astype(ml_dtypes.bfloat16))
        rest = rest - of_taps[-1].astype(np.float64)
    of_taps = jnp.asarray(np.stack(of_taps))
    mats = (jnp.asarray(forward, jnp.bfloat16), jnp.asarray(inverse, jnp.bfloat16))

    def prepare(small):
        ring, w_late = small
        full_k = in_order(ring, "fsdp").reshape(feats.shape[3], repeats, -1)
        full_k = jnp.transpose(full_k, (1, 2, 0))
        kernels = [transformed(of_taps, full_k[0])] + [full_k[turn] for turn in range(1, repeats)]
        later = [w_late[turn, 0] for turn in range(1, repeats)]
        return kernels, masked_in, flags, mats, later

    small = (ring, w_in)
    if size == 8:
        pieces, starts, small = crossed(w_in[0, 0], "fsdp", small, prepare)
        kind = "pieces"
    else:
        pieces = [lax.all_gather(w_in[0, 0], "fsdp", axis=0, tiled=True)]
        starts = jnp.zeros((1,), jnp.int32)
        kind = "rows"
        small = prepare(small)
    pieces, (starts, small) = lax.optimization_barrier((pieces, (starts, small)))
    kernels, masked_in, flags, mats, later = small

    def hop_of(block, route, parity):
        route = [(a * size + f, b * size + f) for a, b in route for f in range(parity, size, 2)]
        return lax.ppermute(block, ("section", "fsdp"), route)

    weights = [(0, kind, pieces)]
    for turn in range(1, repeats):
        rows = lax.all_gather(later[turn - 1], "fsdp", axis=0, tiled=True)
        weights.append((turn, "rows", [rows]))

    early, mark = layer(
        0, flags, masked_in[0], 0, [], weights[:1], starts, kernels[:1], mats
    )
    token = lax.ppermute(mark, "fsdp", [(i, i + 1) for i in range(0, size, 2)])
    early = hop_of(early, [(0, 1)], 0)
    tgt = targets(flags, feats_local, w_tgt, 1, token)
    result, mark = layer(
        steps, flags, masked_in[0], 0, [], weights[:1], starts, kernels[:1], mats, (tgt,)
    )
    state = [early, hop_of(result, [(0, 1)], 1)]
    count = distractors.shape[3]
    parts = []

    losses = []
    for step, plan in enumerate(plans):
        if step == 0:
            continue
        turns = sorted({item[0] for item in plan if item is not None})
        slot = plan[0][1] if plan[0] is not None and plan[0][0] == 0 else None
        used = [weights[turn] for turn in turns]
        k_used = [kernels[turn] for turn in turns]
        spare = ()
        if 1 < step <= last + 1:
            picks, mark = lax.optimization_barrier((distractors[:, 0], mark))
            parts.append(lax.ppermute(picks, "section", [(step - 2, last)]))
            spare = (mark, parts[-1])
        if step == 2:
            tgt = targets(flags, feats_local, w_tgt, 0, mark, tgt)
            spare += (tgt,)
        if step == micro:
            rows = [arrays for _, _, arrays in weights[1:]]
            kernels[1:], rows = lax.optimization_barrier((kernels[1:], rows))
            kernels[1:] = [transformed(of_taps, kernel) for kernel in kernels[1:]]
            weights[1:] = [(turn + 1, "rows", arrays) for turn, arrays in enumerate(rows)]
            used = [weights[turn] for turn in turns]
            k_used = [kernels[turn] for turn in turns]
        base = int(step == micro)
        if step == middle + 1:
            spare, base = (token,), 1
        result, mark = layer(
            step, flags, None if slot is None else masked_in[slot], slot, state, used, starts, k_used, mats, spare, base, step == micro,
            VMEM_LIMIT if step < micro else LATE_VMEM_LIMIT,
        )
        if step == last + 1:
            picks = jnp.concatenate(parts + [distractors[:, 0]], axis=1)
            picks = jnp.pad(picks, ((0, 0), (0, 0), (0, -count % LANES)))
        ends = plan[last]
        if ends is not None and ends[0] == repeats - 1:
            losses.append(loss_rows(ends[1], flags, result, w_ctx, tgt, picks, count))
        state = []
        route = []
        for s, item in enumerate(plan):
            if item is not None and not (s == last and item[0] == repeats - 1):
                route.append((s, (s + 1) % sections))
        if route and step == middle:
            state = [hop_of(result, route, 0)]
            token = lax.ppermute(
                state[0][:16, :LANES], "fsdp", [(i, i + 1) for i in range(0, size, 2)]
            )
            result, token = lax.optimization_barrier((result, token))
            state.append(hop_of(result, route, 1))
        elif route:
            state = [lax.ppermute(result, "section", route)]

    loss = jnp.concatenate(losses, axis=0)
    share = frames // sections
    mine = jnp.zeros((micro, share), jnp.float32)
    for s in range(sections):
        cut = loss[:, s * share : (s + 1) * share]
        if s == last:
            mine = mine + jnp.where(section == last, cut, 0.0)
        else:
            mine = mine + lax.ppermute(cut, "section", [(last, s)])
    return mine[:, None, :]


def solution(mesh):
    placed = (
        P(None, "fsdp", None, None),
        P(None, "section", "fsdp", None),
        P(None, "section", None, "fsdp"),
        P(),
        P(),
        P(),
        P(None, "fsdp", None),
        P(None, "fsdp", "section", None),
    )
    return jax.shard_map(
        on_device, mesh=mesh, in_specs=placed, out_specs=P(None, "fsdp", "section"), check_vma=False
    )
```

```python
import functools

import jax
import jax.numpy as jnp
import ml_dtypes
import numpy as np
from jax import lax
from jax.experimental import pallas as pl
from jax.experimental.pallas import tpu as pltpu
from jax.sharding import PartitionSpec as P

MASK_LEN = 10
LANES = 128
PAD = 16
VMEM_LIMIT = 20 * 1024 * 1024
LATE_VMEM_LIMIT = 48 * 1024 * 1024


BLOCK = 128
WINDOW = BLOCK + 2 * PAD
HALF = WINDOW // 2


def transforms(taps):
    freq = np.arange(HALF)[:, None] * (2 * np.pi / WINDOW)
    spot = np.arange(WINDOW)[None, :]
    forward = np.concatenate([np.cos(freq * spot), -np.sin(freq * spot)])
    forward[HALF] = (-1.0) ** np.arange(WINDOW)
    inverse = forward[:, :BLOCK].T
    at = np.arange(taps)[None, :] + PAD - taps // 2
    scale = np.full((HALF, 1), 2.0 / WINDOW)
    scale[0] = 1.0 / WINDOW
    real, imag = np.cos(freq * at) * scale, np.sin(freq * at) * scale
    last = real.copy()
    last[0] = (-1.0) ** at[0] / WINDOW
    return forward, inverse, np.concatenate([real, imag, last])


def sigmoid(v):
    return 0.5 + 0.5 * jnp.tanh(0.5 * v)


def layer_body(entry, kinds, fresh_slot, recvs, spare, base, flags, *refs):
    refs = list(refs)
    fresh = refs.pop(0) if fresh_slot is not None else None
    recv = [refs.pop(0) for _ in range(recvs)]
    sources = [[refs.pop(0) for _ in range(count)] for _, _, count in kinds]
    starts = refs.pop(0)
    k_ref = refs.pop(0)
    forward, inverse = refs.pop(0), refs.pop(0)
    del refs[:spare]
    out_ref, mark_ref, normed, wbuf, glu, w_sem = (refs.pop(0) for _ in range(6))
    x_ref, x_sem = refs if refs else (recv[0], None)
    chunks, width, part = wbuf.shape
    part = part // 2
    frames = x_ref.shape[0]
    valid = flags[entry, 0]
    turn = flags[entry, 1]

    def weight_copies(kind, source, j, side):
        target, sem = wbuf.at[j, :, pl.ds(side * part, part)], w_sem.at[j]
        cols = pl.ds(pl.multiple_of(side * width + j * part, part), part)
        if kind == "rows":
            return [pltpu.make_async_copy(source[0].at[:, cols], target, sem)]
        copies = []
        for i, piece in enumerate(source):
            size = piece.shape[0]
            place = pl.ds(pl.multiple_of(starts[i], size), size)
            into = wbuf.at[j, place, pl.ds(side * part, part)]
            copies.append(pltpu.make_async_copy(piece.at[:, cols], into, sem))
        return copies

    def start_weights(j):
        def issue(kind, source):
            for side in range(2):
                for copy in weight_copies(kind, source, j, side):
                    copy.start()

        for (which, kind, _), source in zip(kinds, sources):
            if len(kinds) == 1:
                issue(kind, source)
            else:
                pl.when(turn == which)(functools.partial(issue, kind, source))

    def wait_weights(j):
        pltpu.make_async_copy(wbuf.at[j], wbuf.at[j], w_sem.at[j]).wait()

    def project(j, slot):
        both = jnp.dot(normed[...], wbuf[j], preferred_element_type=jnp.float32)
        gated = both[:, :part] * sigmoid(both[:, part:])
        glu[slot, PAD : PAD + frames, :] = gated.astype(jnp.bfloat16)

    def taps(i, cols):
        rows = slice(HALF * i, HALF * (i + 1))
        return k_ref[turn, rows, cols] if len(kinds) > 1 else k_ref[rows, cols]

    def mix(j, slot):
        cols = pl.ds(pl.multiple_of(j * part, part), part)
        real, imag, last = (taps(i, cols) for i in range(3))
        for row in range(0, frames, BLOCK):
            window = glu[slot, row : row + WINDOW, :]
            freq = jnp.dot(forward[...], window, preferred_element_type=jnp.float32)
            up, low = freq[:HALF], freq[HALF:]
            freq = jnp.concatenate([up * real - low * imag, up * imag + low * last], axis=0)
            conv = jnp.dot(
                inverse[...], freq.astype(jnp.bfloat16), preferred_element_type=jnp.float32
            )
            base = x_ref[row : row + BLOCK, cols].astype(jnp.float32)
            out_ref[row : row + BLOCK, cols] = (base + conv * sigmoid(conv)).astype(jnp.bfloat16)

    @pl.when(valid == 1)
    def _():
        ahead = min(3, chunks)
        if x_sem is not None:
            options = ([] if fresh is None else [fresh]) + recv
            first = base
            for i, option in enumerate(options):

                @pl.when(flags[entry, 2] == first + i)
                def _(option=option):
                    pltpu.make_async_copy(option, x_ref, x_sem).start()

        for j in range(ahead):
            start_weights(j)
        zeros = jnp.zeros((2, PAD, part), jnp.bfloat16)
        glu[:, 0:PAD, :] = zeros
        glu[:, PAD + frames :, :] = zeros
        if x_sem is not None:
            pltpu.make_async_copy(x_ref, x_ref, x_sem).wait()
        for row in range(0, frames, 64):
            values = x_ref[row : row + 64, :].astype(jnp.float32)
            center = jnp.mean(values, axis=1, keepdims=True)
            moved = values - center
            spread = jnp.mean(moved * moved, axis=1, keepdims=True)
            normed[row : row + 64, :] = (moved * lax.rsqrt(spread + 1e-05)).astype(jnp.bfloat16)
        wait_weights(0)
        project(0, 0)

        @pl.loop(0, chunks - 1)
        def _(j):
            wait_weights(j + 1)

            @pl.when(j + ahead < chunks)
            def _():
                start_weights(j + ahead)

            mix(j, j % 2)
            project(j + 1, (j + 1) % 2)

        mix(chunks - 1, (chunks - 1) % 2)

    mark_ref[...] = jnp.zeros(mark_ref.shape, mark_ref.dtype)


def layer(
    entry, flags, fresh, fresh_slot, recvs, weights, starts, kernels, matrices, spare=(), base=0,
    outside=False, limit=VMEM_LIMIT,
):
    frames, width = recvs[0].shape if recvs else fresh.shape
    part = 256
    chunks = width // part
    anywhere = pl.BlockSpec(memory_space=pl.ANY)
    local = pl.BlockSpec(memory_space=pltpu.VMEM)
    smem = pl.BlockSpec(memory_space=pltpu.SMEM)
    far = pl.BlockSpec(memory_space=pltpu.HBM)
    select = fresh_slot is not None or len(recvs) > 1 or outside
    operands, specs = [flags], [smem]
    if fresh_slot is not None:
        operands.append(fresh)
        specs.append(far)
    operands += recvs
    specs += [far if outside else anywhere if select else local] * len(recvs)
    for _, kind, arrays in weights:
        operands += arrays
        specs += [far if kind == "rows" else anywhere] * len(arrays)
    operands += [starts, kernels, *matrices, *spare]
    specs += [smem] + [local] * (1 + len(matrices)) + [anywhere] * len(spare)
    scratch = [
        pltpu.VMEM((frames, width), jnp.bfloat16),
        pltpu.VMEM((chunks, width, 2 * part), jnp.bfloat16),
        pltpu.VMEM((2, frames + 2 * PAD, part), jnp.bfloat16),
        pltpu.SemaphoreType.DMA((chunks,)),
    ]
    if select:
        scratch += [pltpu.VMEM((frames, width), jnp.bfloat16), pltpu.SemaphoreType.DMA]
    kinds = [(turn, kind, len(arrays)) for turn, kind, arrays in weights]
    return pl.pallas_call(
        functools.partial(
            layer_body, entry, kinds, fresh_slot, len(recvs), len(spare), base
        ),
        in_specs=specs,
        out_specs=[local, local],
        out_shape=[
            jax.ShapeDtypeStruct((frames, width), jnp.bfloat16),
            jax.ShapeDtypeStruct((8, LANES), jnp.float32),
        ],
        scratch_shapes=scratch,
        compiler_params=pltpu.CompilerParams(vmem_limit_bytes=limit),
        cost_estimate=pl.CostEstimate(
            flops=4 * frames * width * width, bytes_accessed=4 * width * width, transcendentals=0
        ),
        name="layer",
    )(*operands)


def transform_body(m_ref, k_ref, out_ref):
    total = jnp.dot(m_ref[0], k_ref[...], preferred_element_type=jnp.float32)
    for part in range(1, m_ref.shape[0]):
        total = total + jnp.dot(m_ref[part], k_ref[...], preferred_element_type=jnp.float32)
    out_ref[...] = total


def transformed(matrix, kernel):
    return pl.pallas_call(
        transform_body,
        out_shape=jax.ShapeDtypeStruct((matrix.shape[1], kernel.shape[1]), jnp.float32),
        compiler_params=pltpu.CompilerParams(vmem_limit_bytes=VMEM_LIMIT),
        name="transformed",
    )(matrix, kernel)


def unit_rows(values):
    return (values * lax.rsqrt(jnp.sum(values * values, axis=-1, keepdims=True) + 1e-06)).astype(
        jnp.bfloat16
    )


def target_body(wanted, flags, feats, w_tgt, *refs):
    out, feats_ref, w_ref, out_ref, sems = refs[-5:]

    @pl.when(flags[0, 4] == wanted)
    def _():
        load_w = pltpu.make_async_copy(w_tgt, w_ref, sems.at[0])
        load_x = pltpu.make_async_copy(feats, feats_ref, sems.at[1])
        load_w.start()
        load_x.start()
        load_w.wait()
        load_x.wait()

        @pl.loop(0, feats_ref.shape[0])
        def _(slot):
            out_ref[slot] = unit_rows(
                jnp.dot(feats_ref[slot], w_ref[...], preferred_element_type=jnp.float32)
            )

        back = pltpu.make_async_copy(out_ref, out, sems.at[2])
        back.start()
        back.wait()


def targets(flags, feats, w_tgt, wanted, spare, earlier=None):
    operands = [flags, feats, w_tgt, spare] + ([] if earlier is None else [earlier])
    anywhere = pl.BlockSpec(memory_space=pl.ANY)
    shape = feats.shape[:2] + w_tgt.shape[1:]
    return pl.pallas_call(
        functools.partial(target_body, wanted),
        in_specs=[pl.BlockSpec(memory_space=pltpu.SMEM)] + [anywhere] * (len(operands) - 1),
        out_specs=anywhere,
        out_shape=jax.ShapeDtypeStruct(shape, jnp.bfloat16),
        scratch_shapes=[
            pltpu.VMEM(feats.shape, jnp.bfloat16),
            pltpu.VMEM(w_tgt.shape, jnp.bfloat16),
            pltpu.VMEM(shape, jnp.bfloat16),
            pltpu.SemaphoreType.DMA((3,)),
        ],
        input_output_aliases={} if earlier is None else {4: 0},
        compiler_params=pltpu.CompilerParams(vmem_limit_bytes=VMEM_LIMIT),
        cost_estimate=pl.CostEstimate(
            flops=2 * feats.size * w_tgt.shape[1],
            bytes_accessed=2 * (feats.size + w_tgt.size),
            transcendentals=0,
        ),
        name="targets",
    )(*operands)


def loss_body(slot, count, flags, x_ref, w_ref, tgt_ref, pick_ref, out_ref):
    frames = x_ref.shape[0]

    @pl.when(flags[0, 3] == 1)
    def _():
        ctx = unit_rows(jnp.dot(x_ref[...], w_ref[...], preferred_element_type=jnp.float32))
        sims = lax.dot_general(
            ctx, tgt_ref[slot], (((1,), (1,)), ((), ())), preferred_element_type=jnp.float32
        )
        row = lax.broadcasted_iota(jnp.int32, sims.shape, 0)
        col = lax.broadcasted_iota(jnp.int32, sims.shape, 1)
        positive = jnp.sum(jnp.where(row == col, sims, 0.0), axis=1, keepdims=True) * 10.0
        picks = pick_ref[slot]
        lane = picks % LANES
        block = picks // LANES
        negative = jnp.zeros(picks.shape, jnp.float32)
        for part in range(frames // LANES):
            found = jnp.take_along_axis(sims[:, part * LANES : (part + 1) * LANES], lane, axis=1)
            negative = jnp.where(block == part, found, negative)
        place = lax.broadcasted_iota(jnp.int32, picks.shape, 1)
        terms = jnp.where(place < count, jnp.exp(negative * 10.0), 0.0)
        total = jnp.exp(positive) + jnp.sum(terms, axis=1, keepdims=True)
        wide = jnp.broadcast_to(jnp.log(total) - positive, (frames, LANES))
        out_ref[...] = wide.T[0:1, :]


def loss_rows(slot, flags, x, w_ctx, tgt, picks, count):
    frames = x.shape[0]
    whole = pl.BlockSpec(memory_space=pltpu.VMEM)
    return pl.pallas_call(
        functools.partial(loss_body, slot, count),
        in_specs=[pl.BlockSpec(memory_space=pltpu.SMEM)] + [whole] * 4,
        out_specs=whole,
        out_shape=jax.ShapeDtypeStruct((1, frames), jnp.float32),
        compiler_params=pltpu.CompilerParams(vmem_limit_bytes=VMEM_LIMIT),
        name="loss",
    )(flags, x, w_ctx, tgt, picks)


def swap(block, axis, mask):
    return lax.ppermute(block, axis, [(i, i ^ mask) for i in range(lax.axis_size(axis))])


def chip_pieces(block, axis):
    size = lax.axis_size(axis)
    other = swap(block, axis, 1)
    odd = lax.axis_index(axis) % 2 == 1
    both = jnp.concatenate([jnp.where(odd, other, block), jnp.where(odd, block, other)], axis=0)
    return [swap(both, axis, mask) if mask else both for mask in range(0, size, 2)]


def in_order(pieces, axis):
    chip = lax.axis_index(axis) // 2
    mask = 1
    while mask < len(pieces):
        upper = chip // mask % 2 == 1
        pieces = [jnp.where(upper, pieces[i ^ mask], pieces[i]) for i in range(len(pieces))]
        mask *= 2
    return jnp.concatenate(pieces, axis=0)


def crossed(block, axis, small, prepare):
    size = lax.axis_size(axis)
    me = lax.axis_index(axis)
    odd = me % 2
    ahead = [(i, i ^ (2 if i % 2 else 4)) for i in range(size)]
    other = [(i, i ^ (4 if i % 2 else 2)) for i in range(size)]
    near = lax.ppermute(block, axis, ahead)
    block, near, small = lax.optimization_barrier((block, near, small))
    far = lax.ppermute(near, axis, other)
    side = lax.ppermute(block, axis, other)
    small = prepare(small)
    first, second = 4 - 2 * odd, 2 + 2 * odd
    pieces = [block, near, side, far]
    masks = [0, first, second, 6]
    pieces += [swap(piece, axis, 1) for piece in pieces]
    masks += [1, second ^ 1, first ^ 1, 7]
    starts = jnp.stack([(me ^ mask) * block.shape[0] for mask in masks]).astype(jnp.int32)
    return pieces, starts, small


def on_device(feats, w_in, dw_kernel, mask_embed, w_ctx, w_tgt, mask_starts, distractors):
    sections = lax.axis_size("section")
    section = lax.axis_index("section")
    size = lax.axis_size("fsdp")
    micro = feats.shape[0]
    frames = feats.shape[2]
    repeats = w_in.shape[0]
    last = sections - 1
    feats_local = feats[:, 0]


    def work(step, s):
        offset = step - s
        if offset < 0:
            return None
        turn, slot = offset // sections, offset % sections
        return (turn, slot) if slot < micro and turn < repeats else None

    steps = repeats * sections + micro - 1
    plans = [[work(step, s) for s in range(sections)] for step in range(steps)]
    table = [
        [
            [
                int(plan[s] is not None),
                0 if plan[s] is None else plan[s][0],
                int(not (s == 0 and plan[s] is not None and plan[s][0] == 0)),
                int(s == last),
                0,
            ]
            for plan in plans + plans[:1]
        ]
        for s in range(sections)
    ]
    odd = lax.axis_index("fsdp") % 2
    flags = lax.dynamic_index_in_dim(jnp.array(table, jnp.int32), section, 0, keepdims=False)
    lanes = lax.broadcasted_iota(jnp.int32, flags.shape, 1)
    entries = lax.broadcasted_iota(jnp.int32, flags.shape, 0)
    off = (lanes == 0) & (((entries == 0) & (odd == 1)) | ((entries == steps) & (odd == 0)))
    flags = jnp.where(lanes == 4, odd, jnp.where(off, 0, flags))
    middle = micro + 1
    split = (entries == 1) | (entries == middle + 1)
    flags = jnp.where(split & (lanes == 2) & (flags == 1), 1 + odd, flags)

    spots = jnp.arange(frames, dtype=jnp.int32)
    begins = mask_starts[:, 0][:, :, None]
    covered = jnp.any(
        (spots[None, None, :] >= begins) & (spots[None, None, :] < begins + MASK_LEN), axis=1
    )
    masked_in = [
        jnp.where(covered[slot][:, None], mask_embed[None, :], feats_local[slot])
        for slot in range(micro)
    ]

    taps = dw_kernel.shape[2]
    own = jnp.pad(dw_kernel[:, 0], ((0, 0), (0, -taps % 8), (0, 0)))
    own = jnp.transpose(own, (2, 0, 1))
    ring = chip_pieces(own.reshape(own.shape[0], -1), "fsdp")
    forward, inverse, rest = transforms(taps)
    rest = np.pad(rest, ((0, 0), (0, -taps % 8)))
    of_taps = []
    for _ in range(3):
        of_taps.append(rest.astype(ml_dtypes.bfloat16))
        rest = rest - of_taps[-1].astype(np.float64)
    of_taps = jnp.asarray(np.stack(of_taps))
    mats = (jnp.asarray(forward, jnp.bfloat16), jnp.asarray(inverse, jnp.bfloat16))

    def prepare(small):
        ring, w_late = small
        full_k = in_order(ring, "fsdp").reshape(feats.shape[3], repeats, -1)
        full_k = jnp.transpose(full_k, (1, 2, 0))
        kernels = [transformed(of_taps, full_k[0])] + [full_k[turn] for turn in range(1, repeats)]
        later = [w_late[turn, 0] for turn in range(1, repeats)]
        return kernels, masked_in, flags, mats, later

    small = (ring, w_in)
    if size == 8:
        pieces, starts, small = crossed(w_in[0, 0], "fsdp", small, prepare)
        kind = "pieces"
    else:
        pieces = [lax.all_gather(w_in[0, 0], "fsdp", axis=0, tiled=True)]
        starts = jnp.zeros((1,), jnp.int32)
        kind = "rows"
        small = prepare(small)
    pieces, (starts, small) = lax.optimization_barrier((pieces, (starts, small)))
    kernels, masked_in, flags, mats, later = small

    def hop_of(block, route, parity):
        route = [(a * size + f, b * size + f) for a, b in route for f in range(parity, size, 2)]
        return lax.ppermute(block, ("section", "fsdp"), route)

    weights = [(0, kind, pieces)]
    for turn in range(1, repeats):
        rows = lax.all_gather(later[turn - 1], "fsdp", axis=0, tiled=True)
        weights.append((turn, "rows", [rows]))

    early, mark = layer(
        0, flags, masked_in[0], 0, [], weights[:1], starts, kernels[0], mats
    )
    token = lax.ppermute(mark, "fsdp", [(i, i + 1) for i in range(0, size, 2)])
    early = hop_of(early, [(0, 1)], 0)
    tgt = targets(flags, feats_local, w_tgt, 1, token)
    result, mark = layer(
        steps, flags, masked_in[0], 0, [], weights[:1], starts, kernels[0], mats, (tgt,)
    )
    state = [early, hop_of(result, [(0, 1)], 1)]
    count = distractors.shape[3]
    parts = []

    losses = []
    for step, plan in enumerate(plans):
        if step == 0:
            continue
        turns = sorted({item[0] for item in plan if item is not None})
        slot = plan[0][1] if plan[0] is not None and plan[0][0] == 0 else None
        used = [weights[turn] for turn in turns]
        spare = ()
        if 1 < step <= last + 1:
            picks, mark = lax.optimization_barrier((distractors[:, 0], mark))
            parts.append(lax.ppermute(picks, "section", [(step - 2, last)]))
            spare = (mark, parts[-1])
        if step == 2:
            tgt = targets(flags, feats_local, w_tgt, 0, mark, tgt)
            spare += (tgt,)
        if step == micro:
            rows = [arrays for _, _, arrays in weights[1:]]
            kernels[1:], rows = lax.optimization_barrier((kernels[1:], rows))
            kernels[1:] = [transformed(of_taps, kernel) for kernel in kernels[1:]]
            weights[1:] = [(turn + 1, "rows", arrays) for turn, arrays in enumerate(rows)]
            used = [weights[turn] for turn in turns]
            stacked = jnp.stack(kernels)
        k_used = kernels[turns[0]] if len(turns) == 1 else stacked
        base = int(step == micro)
        if step == middle + 1:
            spare, base = (token,), 1
        fresh = None if slot is None else masked_in[slot]
        limit = VMEM_LIMIT if step < micro else LATE_VMEM_LIMIT
        outside = step == micro
        result, mark = layer(
            step, flags, fresh, slot, state, used, starts, k_used, mats, spare, base, outside, limit
        )
        if step == last + 1:
            picks = jnp.concatenate(parts + [distractors[:, 0]], axis=1)
            picks = jnp.pad(picks, ((0, 0), (0, 0), (0, -count % LANES)))
        ends = plan[last]
        if ends is not None and ends[0] == repeats - 1:
            losses.append(loss_rows(ends[1], flags, result, w_ctx, tgt, picks, count))
        state = []
        route = []
        for s, item in enumerate(plan):
            if item is not None and not (s == last and item[0] == repeats - 1):
                route.append((s, (s + 1) % sections))
        if route and step == middle:
            state = [hop_of(result, route, 0)]
            token = lax.ppermute(
                state[0][:16, :LANES], "fsdp", [(i, i + 1) for i in range(0, size, 2)]
            )
            result, token = lax.optimization_barrier((result, token))
            state.append(hop_of(result, route, 1))
        elif route:
            state = [lax.ppermute(result, "section", route)]

    loss = jnp.concatenate(losses, axis=0)
    share = frames // sections
    mine = jnp.zeros((micro, share), jnp.float32)
    for s in range(sections):
        cut = loss[:, s * share : (s + 1) * share]
        if s == last:
            mine = mine + jnp.where(section == last, cut, 0.0)
        else:
            mine = mine + lax.ppermute(cut, "section", [(last, s)])
    return mine[:, None, :]


def solution(mesh):
    placed = (
        P(None, "fsdp", None, None),
        P(None, "section", "fsdp", None),
        P(None, "section", None, "fsdp"),
        P(),
        P(),
        P(),
        P(None, "fsdp", None),
        P(None, "fsdp", "section", None),
    )
    return jax.shard_map(
        on_device, mesh=mesh, in_specs=placed, out_specs=P(None, "fsdp", "section"), check_vma=False
    )
```

```python
import functools

import jax
import jax.numpy as jnp
import ml_dtypes
import numpy as np
from jax import lax
from jax.experimental import pallas as pl
from jax.experimental.pallas import tpu as pltpu
from jax.sharding import PartitionSpec as P

MASK_LEN = 10
LANES = 128
PAD = 16
VMEM_LIMIT = 20 * 1024 * 1024
LATE_VMEM_LIMIT = 48 * 1024 * 1024


BLOCK = 128
WINDOW = BLOCK + 2 * PAD
HALF = WINDOW // 2


def transforms(taps):
    freq = np.arange(HALF)[:, None] * (2 * np.pi / WINDOW)
    spot = np.arange(WINDOW)[None, :]
    forward = np.concatenate([np.cos(freq * spot), -np.sin(freq * spot)])
    forward[HALF] = (-1.0) ** np.arange(WINDOW)
    inverse = forward[:, :BLOCK].T
    at = np.arange(taps)[None, :] + PAD - taps // 2
    scale = np.full((HALF, 1), 2.0 / WINDOW)
    scale[0] = 1.0 / WINDOW
    real, imag = np.cos(freq * at) * scale, np.sin(freq * at) * scale
    last = real.copy()
    last[0] = (-1.0) ** at[0] / WINDOW
    return forward, inverse, np.concatenate([real, imag, last])


def sigmoid(v):
    return 0.5 + 0.5 * jnp.tanh(0.5 * v)


def layer_body(entry, kinds, fresh_slot, recvs, spare, base, flags, *refs):
    refs = list(refs)
    fresh = refs.pop(0) if fresh_slot is not None else None
    recv = [refs.pop(0) for _ in range(recvs)]
    sources = [[refs.pop(0) for _ in range(count)] for _, _, count in kinds]
    starts = refs.pop(0)
    k_refs = [refs.pop(0) for _ in kinds]
    forward, inverse = refs.pop(0), refs.pop(0)
    del refs[:spare]
    out_ref, mark_ref, normed, wbuf, glu, w_sem = (refs.pop(0) for _ in range(6))
    x_ref, x_sem = refs if refs else (recv[0], None)
    chunks, width, part = wbuf.shape
    part = part // 2
    frames = x_ref.shape[0]
    valid = flags[entry, 0]
    turn = flags[entry, 1]

    def weight_copies(kind, source, j, side):
        target, sem = wbuf.at[j, :, pl.ds(side * part, part)], w_sem.at[j]
        cols = pl.ds(pl.multiple_of(side * width + j * part, part), part)
        if kind == "rows":
            return [pltpu.make_async_copy(source[0].at[:, cols], target, sem)]
        copies = []
        for i, piece in enumerate(source):
            size = piece.shape[0]
            place = pl.ds(pl.multiple_of(starts[i], size), size)
            into = wbuf.at[j, place, pl.ds(side * part, part)]
            copies.append(pltpu.make_async_copy(piece.at[:, cols], into, sem))
        return copies

    def start_weights(j):
        def issue(kind, source):
            for side in range(2):
                for copy in weight_copies(kind, source, j, side):
                    copy.start()

        for (which, kind, _), source in zip(kinds, sources):
            if len(kinds) == 1:
                issue(kind, source)
            else:
                pl.when(turn == which)(functools.partial(issue, kind, source))

    def wait_weights(j):
        pltpu.make_async_copy(wbuf.at[j], wbuf.at[j], w_sem.at[j]).wait()

    def project(j, slot):
        both = jnp.dot(normed[...], wbuf[j], preferred_element_type=jnp.float32)
        gated = both[:, :part] * sigmoid(both[:, part:])
        glu[slot, PAD : PAD + frames, :] = gated.astype(jnp.bfloat16)

    def taps(i, cols):
        rows = slice(HALF * i, HALF * (i + 1))
        chosen = k_refs[0][rows, cols]
        for (which, _, _), k_ref in zip(kinds[1:], k_refs[1:]):
            chosen = jnp.where(turn == which, k_ref[rows, cols], chosen)
        return chosen

    def mix(j, slot):
        cols = pl.ds(pl.multiple_of(j * part, part), part)
        real, imag, last = (taps(i, cols) for i in range(3))
        for row in range(0, frames, BLOCK):
            window = glu[slot, row : row + WINDOW, :]
            freq = jnp.dot(forward[...], window, preferred_element_type=jnp.float32)
            up, low = freq[:HALF], freq[HALF:]
            freq = jnp.concatenate([up * real - low * imag, up * imag + low * last], axis=0)
            conv = jnp.dot(
                inverse[...], freq.astype(jnp.bfloat16), preferred_element_type=jnp.float32
            )
            base = x_ref[row : row + BLOCK, cols].astype(jnp.float32)
            out_ref[row : row + BLOCK, cols] = (base + conv * sigmoid(conv)).astype(jnp.bfloat16)

    @pl.when(valid == 1)
    def _():
        ahead = min(2, chunks)
        if x_sem is not None:
            options = ([] if fresh is None else [fresh]) + recv
            first = base
            for i, option in enumerate(options):

                @pl.when(flags[entry, 2] == first + i)
                def _(option=option):
                    pltpu.make_async_copy(option, x_ref, x_sem).start()

        for j in range(ahead):
            start_weights(j)
        zeros = jnp.zeros((2, PAD, part), jnp.bfloat16)
        glu[:, 0:PAD, :] = zeros
        glu[:, PAD + frames :, :] = zeros
        if x_sem is not None:
            pltpu.make_async_copy(x_ref, x_ref, x_sem).wait()
        for row in range(0, frames, 64):
            values = x_ref[row : row + 64, :].astype(jnp.float32)
            center = jnp.mean(values, axis=1, keepdims=True)
            moved = values - center
            spread = jnp.mean(moved * moved, axis=1, keepdims=True)
            normed[row : row + 64, :] = (moved * lax.rsqrt(spread + 1e-05)).astype(jnp.bfloat16)
        wait_weights(0)
        project(0, 0)

        @pl.loop(0, chunks - 1)
        def _(j):
            wait_weights(j + 1)

            @pl.when(j + ahead < chunks)
            def _():
                start_weights(j + ahead)

            mix(j, j % 2)
            project(j + 1, (j + 1) % 2)

        mix(chunks - 1, (chunks - 1) % 2)

    mark_ref[...] = jnp.zeros(mark_ref.shape, mark_ref.dtype)


def layer(
    entry, flags, fresh, fresh_slot, recvs, weights, starts, kernels, matrices, spare=(), base=0,
    outside=False, limit=VMEM_LIMIT,
):
    frames, width = recvs[0].shape if recvs else fresh.shape
    part = 256
    chunks = width // part
    anywhere = pl.BlockSpec(memory_space=pl.ANY)
    local = pl.BlockSpec(memory_space=pltpu.VMEM)
    smem = pl.BlockSpec(memory_space=pltpu.SMEM)
    far = pl.BlockSpec(memory_space=pltpu.HBM)
    select = fresh_slot is not None or len(recvs) > 1 or outside
    operands, specs = [flags], [smem]
    if fresh_slot is not None:
        operands.append(fresh)
        specs.append(far)
    operands += recvs
    specs += [far if outside else anywhere if select else local] * len(recvs)
    for _, kind, arrays in weights:
        operands += arrays
        specs += [far if kind == "rows" else anywhere] * len(arrays)
    operands += [starts, *kernels, *matrices, *spare]
    specs += [smem] + [local] * (len(kernels) + len(matrices)) + [anywhere] * len(spare)
    scratch = [
        pltpu.VMEM((frames, width), jnp.bfloat16),
        pltpu.VMEM((chunks, width, 2 * part), jnp.bfloat16),
        pltpu.VMEM((2, frames + 2 * PAD, part), jnp.bfloat16),
        pltpu.SemaphoreType.DMA((chunks,)),
    ]
    if select:
        scratch += [pltpu.VMEM((frames, width), jnp.bfloat16), pltpu.SemaphoreType.DMA]
    kinds = [(turn, kind, len(arrays)) for turn, kind, arrays in weights]
    return pl.pallas_call(
        functools.partial(
            layer_body, entry, kinds, fresh_slot, len(recvs), len(spare), base
        ),
        in_specs=specs,
        out_specs=[local, local],
        out_shape=[
            jax.ShapeDtypeStruct((frames, width), jnp.bfloat16),
            jax.ShapeDtypeStruct((8, LANES), jnp.float32),
        ],
        scratch_shapes=scratch,
        compiler_params=pltpu.CompilerParams(vmem_limit_bytes=limit),
        cost_estimate=pl.CostEstimate(
            flops=4 * frames * width * width, bytes_accessed=4 * width * width, transcendentals=0
        ),
        name="layer",
    )(*operands)


def transform_body(m_ref, k_ref, out_ref):
    total = jnp.dot(m_ref[0], k_ref[...], preferred_element_type=jnp.float32)
    for part in range(1, m_ref.shape[0]):
        total = total + jnp.dot(m_ref[part], k_ref[...], preferred_element_type=jnp.float32)
    out_ref[...] = total


def transformed(matrix, kernel):
    return pl.pallas_call(
        transform_body,
        out_shape=jax.ShapeDtypeStruct((matrix.shape[1], kernel.shape[1]), jnp.float32),
        compiler_params=pltpu.CompilerParams(vmem_limit_bytes=VMEM_LIMIT),
        name="transformed",
    )(matrix, kernel)


def unit_rows(values):
    return (values * lax.rsqrt(jnp.sum(values * values, axis=-1, keepdims=True) + 1e-06)).astype(
        jnp.bfloat16
    )


def target_body(wanted, flags, feats, w_tgt, *refs):
    out, feats_ref, w_ref, out_ref, sems = refs[-5:]

    @pl.when(flags[0, 4] == wanted)
    def _():
        load_w = pltpu.make_async_copy(w_tgt, w_ref, sems.at[0])
        load_x = pltpu.make_async_copy(feats, feats_ref, sems.at[1])
        load_w.start()
        load_x.start()
        load_w.wait()
        load_x.wait()

        @pl.loop(0, feats_ref.shape[0])
        def _(slot):
            out_ref[slot] = unit_rows(
                jnp.dot(feats_ref[slot], w_ref[...], preferred_element_type=jnp.float32)
            )

        back = pltpu.make_async_copy(out_ref, out, sems.at[2])
        back.start()
        back.wait()


def targets(flags, feats, w_tgt, wanted, spare, earlier=None):
    operands = [flags, feats, w_tgt, spare] + ([] if earlier is None else [earlier])
    anywhere = pl.BlockSpec(memory_space=pl.ANY)
    shape = feats.shape[:2] + w_tgt.shape[1:]
    return pl.pallas_call(
        functools.partial(target_body, wanted),
        in_specs=[pl.BlockSpec(memory_space=pltpu.SMEM)] + [anywhere] * (len(operands) - 1),
        out_specs=anywhere,
        out_shape=jax.ShapeDtypeStruct(shape, jnp.bfloat16),
        scratch_shapes=[
            pltpu.VMEM(feats.shape, jnp.bfloat16),
            pltpu.VMEM(w_tgt.shape, jnp.bfloat16),
            pltpu.VMEM(shape, jnp.bfloat16),
            pltpu.SemaphoreType.DMA((3,)),
        ],
        input_output_aliases={} if earlier is None else {4: 0},
        compiler_params=pltpu.CompilerParams(vmem_limit_bytes=VMEM_LIMIT),
        cost_estimate=pl.CostEstimate(
            flops=2 * feats.size * w_tgt.shape[1],
            bytes_accessed=2 * (feats.size + w_tgt.size),
            transcendentals=0,
        ),
        name="targets",
    )(*operands)


def loss_body(slot, count, flags, x_ref, w_ref, tgt_ref, pick_ref, out_ref):
    frames = x_ref.shape[0]

    @pl.when(flags[0, 3] == 1)
    def _():
        ctx = unit_rows(jnp.dot(x_ref[...], w_ref[...], preferred_element_type=jnp.float32))
        sims = lax.dot_general(
            ctx, tgt_ref[slot], (((1,), (1,)), ((), ())), preferred_element_type=jnp.float32
        )
        row = lax.broadcasted_iota(jnp.int32, sims.shape, 0)
        col = lax.broadcasted_iota(jnp.int32, sims.shape, 1)
        positive = jnp.sum(jnp.where(row == col, sims, 0.0), axis=1, keepdims=True) * 10.0
        picks = pick_ref[slot]
        lane = picks % LANES
        block = picks // LANES
        negative = jnp.zeros(picks.shape, jnp.float32)
        for part in range(frames // LANES):
            found = jnp.take_along_axis(sims[:, part * LANES : (part + 1) * LANES], lane, axis=1)
            negative = jnp.where(block == part, found, negative)
        place = lax.broadcasted_iota(jnp.int32, picks.shape, 1)
        terms = jnp.where(place < count, jnp.exp(negative * 10.0), 0.0)
        total = jnp.exp(positive) + jnp.sum(terms, axis=1, keepdims=True)
        wide = jnp.broadcast_to(jnp.log(total) - positive, (frames, LANES))
        out_ref[...] = wide.T[0:1, :]


def loss_rows(slot, flags, x, w_ctx, tgt, picks, count):
    frames = x.shape[0]
    whole = pl.BlockSpec(memory_space=pltpu.VMEM)
    return pl.pallas_call(
        functools.partial(loss_body, slot, count),
        in_specs=[pl.BlockSpec(memory_space=pltpu.SMEM)] + [whole] * 4,
        out_specs=whole,
        out_shape=jax.ShapeDtypeStruct((1, frames), jnp.float32),
        compiler_params=pltpu.CompilerParams(vmem_limit_bytes=VMEM_LIMIT),
        name="loss",
    )(flags, x, w_ctx, tgt, picks)


def swap(block, axis, mask):
    return lax.ppermute(block, axis, [(i, i ^ mask) for i in range(lax.axis_size(axis))])


def chip_pieces(block, axis):
    size = lax.axis_size(axis)
    other = swap(block, axis, 1)
    odd = lax.axis_index(axis) % 2 == 1
    both = jnp.concatenate([jnp.where(odd, other, block), jnp.where(odd, block, other)], axis=0)
    return [swap(both, axis, mask) if mask else both for mask in range(0, size, 2)]


def in_order(pieces, axis):
    chip = lax.axis_index(axis) // 2
    mask = 1
    while mask < len(pieces):
        upper = chip // mask % 2 == 1
        pieces = [jnp.where(upper, pieces[i ^ mask], pieces[i]) for i in range(len(pieces))]
        mask *= 2
    return jnp.concatenate(pieces, axis=0)


def crossed(block, axis, small, prepare):
    size = lax.axis_size(axis)
    me = lax.axis_index(axis)
    odd = me % 2
    ahead = [(i, i ^ (2 if i % 2 else 4)) for i in range(size)]
    other = [(i, i ^ (4 if i % 2 else 2)) for i in range(size)]
    near = lax.ppermute(block, axis, ahead)
    block, near, small = lax.optimization_barrier((block, near, small))
    far = lax.ppermute(near, axis, other)
    side = lax.ppermute(block, axis, other)
    small = prepare(small)
    first, second = 4 - 2 * odd, 2 + 2 * odd
    pieces = [block, near, side, far]
    masks = [0, first, second, 6]
    pieces += [swap(piece, axis, 1) for piece in pieces]
    masks += [1, second ^ 1, first ^ 1, 7]
    starts = jnp.stack([(me ^ mask) * block.shape[0] for mask in masks]).astype(jnp.int32)
    return pieces, starts, small


def on_device(feats, w_in, dw_kernel, mask_embed, w_ctx, w_tgt, mask_starts, distractors):
    sections = lax.axis_size("section")
    section = lax.axis_index("section")
    size = lax.axis_size("fsdp")
    micro = feats.shape[0]
    frames = feats.shape[2]
    repeats = w_in.shape[0]
    last = sections - 1
    feats_local = feats[:, 0]


    def work(step, s):
        offset = step - s
        if offset < 0:
            return None
        turn, slot = offset // sections, offset % sections
        return (turn, slot) if slot < micro and turn < repeats else None

    steps = repeats * sections + micro - 1
    plans = [[work(step, s) for s in range(sections)] for step in range(steps)]
    table = [
        [
            [
                int(plan[s] is not None),
                0 if plan[s] is None else plan[s][0],
                int(not (s == 0 and plan[s] is not None and plan[s][0] == 0)),
                int(s == last),
                0,
            ]
            for plan in plans + plans[:1]
        ]
        for s in range(sections)
    ]
    odd = lax.axis_index("fsdp") % 2
    flags = lax.dynamic_index_in_dim(jnp.array(table, jnp.int32), section, 0, keepdims=False)
    lanes = lax.broadcasted_iota(jnp.int32, flags.shape, 1)
    entries = lax.broadcasted_iota(jnp.int32, flags.shape, 0)
    off = (lanes == 0) & (((entries == 0) & (odd == 1)) | ((entries == steps) & (odd == 0)))
    flags = jnp.where(lanes == 4, odd, jnp.where(off, 0, flags))
    middle = micro + 1
    split = (entries == 1) | (entries == middle + 1)
    flags = jnp.where(split & (lanes == 2) & (flags == 1), 1 + odd, flags)

    spots = jnp.arange(frames, dtype=jnp.int32)
    begins = mask_starts[:, 0][:, :, None]
    covered = jnp.any(
        (spots[None, None, :] >= begins) & (spots[None, None, :] < begins + MASK_LEN), axis=1
    )
    masked_in = [
        jnp.where(covered[slot][:, None], mask_embed[None, :], feats_local[slot])
        for slot in range(micro)
    ]

    taps = dw_kernel.shape[2]
    own = jnp.pad(dw_kernel[:, 0], ((0, 0), (0, -taps % 8), (0, 0)))
    own = jnp.transpose(own, (2, 0, 1))
    ring = chip_pieces(own.reshape(own.shape[0], -1), "fsdp")
    forward, inverse, rest = transforms(taps)
    rest = np.pad(rest, ((0, 0), (0, -taps % 8)))
    of_taps = []
    for _ in range(3):
        of_taps.append(rest.astype(ml_dtypes.bfloat16))
        rest = rest - of_taps[-1].astype(np.float64)
    of_taps = jnp.asarray(np.stack(of_taps))
    mats = (jnp.asarray(forward, jnp.bfloat16), jnp.asarray(inverse, jnp.bfloat16))

    def prepare(small):
        ring, w_late = small
        full_k = in_order(ring, "fsdp").reshape(feats.shape[3], repeats, -1)
        full_k = jnp.transpose(full_k, (1, 2, 0))
        kernels = [transformed(of_taps, full_k[0])] + [full_k[turn] for turn in range(1, repeats)]
        later = [w_late[turn, 0] for turn in range(1, repeats)]
        return kernels, masked_in, flags, mats, later

    small = (ring, w_in)
    if size == 8:
        pieces, starts, small = crossed(w_in[0, 0], "fsdp", small, prepare)
        kind = "pieces"
    else:
        pieces = [lax.all_gather(w_in[0, 0], "fsdp", axis=0, tiled=True)]
        starts = jnp.zeros((1,), jnp.int32)
        kind = "rows"
        small = prepare(small)
    pieces, (starts, small) = lax.optimization_barrier((pieces, (starts, small)))
    kernels, masked_in, flags, mats, later = small

    def hop_of(block, route, parity):
        route = [(a * size + f, b * size + f) for a, b in route for f in range(parity, size, 2)]
        return lax.ppermute(block, ("section", "fsdp"), route)

    weights = [(0, kind, pieces)]
    for turn in range(1, repeats):
        rows = lax.all_gather(later[turn - 1], "fsdp", axis=0, tiled=True)
        weights.append((turn, "rows", [rows]))

    early, mark = layer(
        0, flags, masked_in[0], 0, [], weights[:1], starts, kernels[:1], mats
    )
    token = lax.ppermute(mark, "fsdp", [(i, i + 1) for i in range(0, size, 2)])
    early = hop_of(early, [(0, 1)], 0)
    tgt = targets(flags, feats_local, w_tgt, 1, token)
    result, mark = layer(
        steps, flags, masked_in[0], 0, [], weights[:1], starts, kernels[:1], mats, (tgt,)
    )
    state = [early, hop_of(result, [(0, 1)], 1)]
    count = distractors.shape[3]
    parts = []

    losses = []
    for step, plan in enumerate(plans):
        if step == 0:
            continue
        turns = sorted({item[0] for item in plan if item is not None})
        slot = plan[0][1] if plan[0] is not None and plan[0][0] == 0 else None
        used = [weights[turn] for turn in turns]
        k_used = [kernels[turn] for turn in turns]
        spare = ()
        if 1 < step <= last + 1:
            picks, mark = lax.optimization_barrier((distractors[:, 0], mark))
            parts.append(lax.ppermute(picks, "section", [(step - 2, last)]))
            spare = (mark, parts[-1])
        if step == 2:
            tgt = targets(flags, feats_local, w_tgt, 0, mark, tgt)
            spare += (tgt,)
        if step == micro:
            rows = [arrays for _, _, arrays in weights[1:]]
            kernels[1:], rows = lax.optimization_barrier((kernels[1:], rows))
            kernels[1:] = [transformed(of_taps, kernel) for kernel in kernels[1:]]
            weights[1:] = [(turn + 1, "rows", arrays) for turn, arrays in enumerate(rows)]
            used = [weights[turn] for turn in turns]
            k_used = [kernels[turn] for turn in turns]
        base = int(step == micro)
        if step == middle + 1:
            spare, base = (token,), 1
        result, mark = layer(
            step, flags, None if slot is None else masked_in[slot], slot, state, used, starts, k_used, mats, spare, base, step == micro,
            VMEM_LIMIT if step < micro else LATE_VMEM_LIMIT,
        )
        if step == last + 1:
            picks = jnp.concatenate(parts + [distractors[:, 0]], axis=1)
            picks = jnp.pad(picks, ((0, 0), (0, 0), (0, -count % LANES)))
        ends = plan[last]
        if ends is not None and ends[0] == repeats - 1:
            losses.append(loss_rows(ends[1], flags, result, w_ctx, tgt, picks, count))
        state = []
        route = []
        for s, item in enumerate(plan):
            if item is not None and not (s == last and item[0] == repeats - 1):
                route.append((s, (s + 1) % sections))
        if route and step == middle:
            state = [hop_of(result, route, 0)]
            token = lax.ppermute(
                state[0][:16, :LANES], "fsdp", [(i, i + 1) for i in range(0, size, 2)]
            )
            result, token = lax.optimization_barrier((result, token))
            state.append(hop_of(result, route, 1))
        elif route:
            state = [lax.ppermute(result, "section", route)]

    loss = jnp.concatenate(losses, axis=0)
    share = frames // sections
    mine = jnp.zeros((micro, share), jnp.float32)
    for s in range(sections):
        cut = loss[:, s * share : (s + 1) * share]
        if s == last:
            mine = mine + jnp.where(section == last, cut, 0.0)
        else:
            mine = mine + lax.ppermute(cut, "section", [(last, s)])
    return mine[:, None, :]


def solution(mesh):
    placed = (
        P(None, "fsdp", None, None),
        P(None, "section", "fsdp", None),
        P(None, "section", None, "fsdp"),
        P(),
        P(),
        P(),
        P(None, "fsdp", None),
        P(None, "fsdp", "section", None),
    )
    return jax.shard_map(
        on_device, mesh=mesh, in_specs=placed, out_specs=P(None, "fsdp", "section"), check_vma=False
    )
```
